32 devices in a mesh: section: 2 (over core), dp: 4 (over z), tensor: 4 (over y, x).
Axes of the slice: x: 2, y: 2, z: 4, core: 2. Of those that a mesh axis runs over, the one named last changes fastest.
Arguments:
- text_in: bfloat16 [2, 4096, 768], P(None, ('dp', 'tensor')), may hold values from -6 to 6
- layout_in: bfloat16 [2, 4096, 192], P(None, ('dp', 'tensor')), may hold values from -6 to 6
- text_cot: bfloat16 [2, 4096, 768], P(None, ('dp', 'tensor')), may hold values from -6 to 6
- layout_cot: bfloat16 [2, 4096, 192], P(None, ('dp', 'tensor')), may hold values from -6 to 6
- lengths: int32 [2, 8], P(None, 'dp'), may hold values from 96 to 512, as said below
- text_attend: bfloat16 [2, 768, 3, 768], P('section', None, None, 'tensor'), may hold values from -0.21875 to 0.21875
- text_biases: bfloat16 [2, 2, 768], P('section', None, 'tensor'), may hold values from -1.796875 to 1.796875
- text_output: bfloat16 [2, 768, 768], P('section', None, 'tensor'), may hold values from -0.875 to 0.875
- text_expand: bfloat16 [2, 768, 3072], P('section', None, 'tensor'), may hold values from -0.21875 to 0.21875
- text_offset: bfloat16 [2, 3072], P('section', 'tensor'), may hold values from -1.796875 to 1.796875
- text_shrink: bfloat16 [2, 768, 3072], P('section', None, 'tensor'), may hold values from -0.109375 to 0.109375
- text_vectors: bfloat16 [2, 6, 768], P('section'), may hold values from -1.5 to 1.5, as said below
- layout_attend: bfloat16 [2, 192, 3, 192], P('section', None, None, 'tensor'), may hold values from -0.4375 to 0.4375
- layout_biases: bfloat16 [2, 2, 192], P('section', None, 'tensor'), may hold values from -1.796875 to 1.796875
- layout_output: bfloat16 [2, 192, 192], P('section', None, 'tensor'), may hold values from -1.75 to 1.75
- layout_expand: bfloat16 [2, 192, 768], P('section', None, 'tensor'), may hold values from -0.4375 to 0.4375
- layout_offset: bfloat16 [2, 768], P('section', 'tensor'), may hold values from -1.796875 to 1.796875
- layout_shrink: bfloat16 [2, 192, 768], P('section', None, 'tensor'), may hold values from -0.21875 to 0.21875
- layout_vectors: bfloat16 [2, 6, 192], P('section'), may hold values from -1.5 to 1.5, as said below
Outputs:
- text_out: bfloat16 [2, 2, 4096, 768], P('section', None, ('dp', 'tensor'))
- layout_out: bfloat16 [2, 2, 4096, 192], P('section', None, ('dp', 'tensor'))
- text_back: bfloat16 [2, 2, 4096, 768], P('section', None, ('dp', 'tensor'))
- layout_back: bfloat16 [2, 2, 4096, 192], P('section', None, ('dp', 'tensor'))
- text_attend_grad: float32 [2, 768, 3, 768], P('section', 'dp', None, 'tensor')
- text_biases_grad: float32 [2, 2, 768], P('section', None, 'tensor')
- text_output_grad: float32 [2, 768, 768], P('section', 'dp', 'tensor')
- text_expand_grad: float32 [2, 768, 3072], P('section', 'dp', 'tensor')
- text_offset_grad: float32 [2, 3072], P('section', 'tensor')
- text_shrink_grad: float32 [2, 768, 3072], P('section', 'dp', 'tensor')
- text_vectors_grad: float32 [2, 6, 768], P('section')
- layout_attend_grad: float32 [2, 192, 3, 192], P('section', 'dp', None, 'tensor')
- layout_biases_grad: float32 [2, 2, 192], P('section', None, 'tensor')
- layout_output_grad: float32 [2, 192, 192], P('section', 'dp', 'tensor')
- layout_expand_grad: float32 [2, 192, 768], P('section', 'dp', 'tensor')
- layout_offset_grad: float32 [2, 768], P('section', 'tensor')
- layout_shrink_grad: float32 [2, 192, 768], P('section', 'dp', 'tensor')
- layout_vectors_grad: float32 [2, 6, 192], P('section')
The draws below stay inside these ranges and needn't reach their ends.
Inputs may be any that keep to these rules, and one draw needn't show every extreme that they name: `lengths`: keys at or past a page's length are padding; some page has exactly 512 tokens. `text_vectors`: rows 1 and 4 are norm gains, the others biases. `layout_vectors`: rows 1 and 4 are norm gains, the others biases.
All inputs are finite; a program needn't handle non-finite values.
Results may differ from the reference program's by a relative error of at most 0.04.
Values may be sent and summed in bfloat16 or wider, within the bound.
A program may use at most 256 MiB of HBM per device.

```python
import jax
import jax.numpy as jnp
from jax import lax

HEADS = 12
HEAD = 64
LHEAD = 16
FF = 3072
LFF = 768
PAGE = 512
MICRO = 2
D = 768
LD = 192
PAGES_MB = 8
TOKENS_MB = 4096


def vector_rows(key, columns):
    subkeys = jax.random.split(key, 2)
    noise = jnp.clip(jax.random.normal(subkeys[0], (2, 6, columns), jnp.float32) * 0.3, -1.5, 1.5)
    gains = 1.0 + jax.random.uniform(subkeys[1], (2, 6, columns), jnp.float32, -0.4, 0.4)
    is_gain = (jnp.arange(6) % 3 == 1)[None, :, None]
    return jnp.where(is_gain, gains, noise).astype(jnp.bfloat16)


def draw_lengths(key, part):
    key = jax.random.fold_in(key, 11)
    subkeys = jax.random.split(key, 3)
    grid_shape = (MICRO, PAGES_MB)
    halving = jax.random.randint(subkeys[0], grid_shape, 0, 3)
    ceiling = PAGE // jnp.left_shift(jnp.ones(grid_shape, jnp.int32), halving)
    trimmed = jax.random.randint(subkeys[1], grid_shape, 0, ceiling // 4 + 1)
    chosen = jax.random.randint(subkeys[2], (), 0, MICRO * PAGES_MB)
    flat = jnp.where(jnp.arange(MICRO * PAGES_MB) == chosen, PAGE, (ceiling - trimmed).reshape(-1))
    return flat.reshape(grid_shape).astype(jnp.int32)


def draw_text_vectors(key, part):
    key = jax.random.fold_in(key, 21)
    return vector_rows(key, HEADS * HEAD)


def draw_layout_vectors(key, part):
    key = jax.random.fold_in(key, 22)
    return vector_rows(key, HEADS * LHEAD)


def spiked(result, own_key, source, target, parts, factor):
    owner, partner = [(jnp.arange(result.shape[position]) // (result.shape[position] // parts)).reshape([-1 if axis == position else 1 for axis in range(result.ndim)]) for position in (source, target)]
    chosen = jax.random.permutation(own_key, parts)[partner]
    strong = (owner == chosen) | (owner == (partner + parts // 2) % parts)
    return jnp.where(strong, factor * result, result)


def levels(key, extent, cuts, least, top_value):
    def one(axis_at, shards_of):
        heights = jax.random.uniform(jax.random.fold_in(jax.random.fold_in(key, 6), axis_at), (shards_of,), jnp.float32, least / len(cuts), top_value / len(cuts))
        return jnp.repeat(jnp.exp(heights), extent[axis_at] // shards_of).reshape((-1,) + (1,) * (len(extent) - axis_at - 1))

    level = one(*cuts[0])
    for cut in cuts[1:]:
        level = level * one(*cut)
    return level


def scatter_about(own_key, extent, scale, bound, pieces=(), dtype=jnp.bfloat16):
    result = scale * jax.random.normal(own_key, extent, jnp.float32)
    if pieces:
        result = result * levels(own_key, extent, pieces, -0.22, 0.18)
    return jnp.clip(result, -bound, bound).astype(dtype)


def bell_draw_with(rng, dims, scale, most, cuts, heavy, dtype=jnp.bfloat16):
    result = scale * jax.random.normal(rng, dims, jnp.float32)
    if cuts:
        result = result * levels(rng, dims, cuts, -0.22, 0.18)
    return jnp.clip(spiked(result, jax.random.fold_in(rng, 3), *heavy), -most, most).astype(dtype)


def setup_inputs(seed: int = 0) -> dict:
    arg_keys = jax.random.split(jax.random.key(seed), 20)
    return {
        "text_in": bell_draw_with(arg_keys[0], (MICRO, TOKENS_MB, D), 1.0, 6.0, ((1, 16),), (1, 2, 16, 2.0)),
        "layout_in": bell_draw_with(arg_keys[1], (MICRO, TOKENS_MB, LD), 1.0, 6.0, ((1, 16),), (1, 2, 16, 2.0)),
        "text_cot": scatter_about(arg_keys[2], (MICRO, TOKENS_MB, D), 1.0, 6.0, ((1, 16),)),
        "layout_cot": scatter_about(arg_keys[3], (MICRO, TOKENS_MB, LD), 1.0, 6.0, ((1, 16),)),
        "lengths": draw_lengths(jax.random.fold_in(arg_keys[19], 71), 0),
        "text_attend": scatter_about(arg_keys[5], (2, D, 3, D), D ** -0.5, 0.21875, ((0, 2), (3, 4))),
        "text_biases": scatter_about(arg_keys[6], (2, 2, D), 0.3, 1.796875, ((0, 2), (2, 4))),
        "text_output": scatter_about(arg_keys[7], (2, D, D), (D // 16) ** -0.5, 0.875, ((0, 2), (2, 4))),
        "text_expand": scatter_about(arg_keys[8], (2, D, FF), D ** -0.5, 0.21875, ((0, 2), (2, 4))),
        "text_offset": scatter_about(arg_keys[9], (2, FF), 0.3, 1.796875, ((0, 2), (1, 4))),
        "text_shrink": scatter_about(arg_keys[10], (2, D, FF), FF ** -0.5, 0.109375, ((0, 2), (2, 4))),
        "text_vectors": draw_text_vectors(jax.random.fold_in(arg_keys[19], 71), 0),
        "layout_attend": scatter_about(arg_keys[12], (2, LD, 3, LD), LD ** -0.5, 0.4375, ((0, 2), (3, 4))),
        "layout_biases": scatter_about(arg_keys[13], (2, 2, LD), 0.3, 1.796875, ((0, 2), (2, 4))),
        "layout_output": scatter_about(arg_keys[14], (2, LD, LD), (LD // 16) ** -0.5, 1.75, ((0, 2), (2, 4))),
        "layout_expand": scatter_about(arg_keys[15], (2, LD, LFF), LD ** -0.5, 0.4375, ((0, 2), (2, 4))),
        "layout_offset": scatter_about(arg_keys[16], (2, LFF), 0.3, 1.796875, ((0, 2), (1, 4))),
        "layout_shrink": scatter_about(arg_keys[17], (2, LD, LFF), LFF ** -0.5, 0.21875, ((0, 2), (2, 4))),
        "layout_vectors": draw_layout_vectors(jax.random.fold_in(arg_keys[19], 71), 0),
    }


@jax.custom_vjp
def low(v):
    return lax.optimization_barrier(v.astype(jnp.bfloat16)).astype(jnp.float32)

@jax.custom_vjp
def low_back(v):
    return v

def low_keep(v):
    return (low(v), None)

def low_pass(kept, grad):
    return (grad,)

def back_keep(v):
    return (v, None)

def back_low(kept, grad):
    return (low(grad),)
low.defvjp(low_keep, low_pass)
low_back.defvjp(back_keep, back_low)
masked_score = -1e+30
norm_epsilon = 1e-05
exact = lax.Precision.HIGHEST

def both_low(tensor):
    return low(low_back(tensor))

def product(left, right):
    return jnp.dot(left, right, precision=exact, preferred_element_type=jnp.float32)

def norm_apply(hidden, scale_gain, bias_shift):
    center = hidden - lax.optimization_barrier(jnp.mean(hidden, axis=-1, keepdims=True))
    spread = lax.optimization_barrier(jnp.mean(center * center, axis=-1, keepdims=True))
    return center * lax.rsqrt(spread + norm_epsilon) * scale_gain + bias_shift

def page_attention(operands):
    query_text, key_text, value_text, query_lay, key_lay, value_lay, page_len = operands
    key_live = jnp.arange(query_text.shape[0]) < page_len
    scores = jnp.einsum('qhd,khd->hqk', query_text, key_text, precision=exact) * HEAD ** (-0.5)
    scores = scores + jnp.einsum('qhd,khd->hqk', query_lay, key_lay, precision=exact) * LHEAD ** (-0.5)
    scores = jnp.where(key_live[None, None, :], scores, masked_score)
    scores = low_back(scores)
    row_top = lax.optimization_barrier(jnp.max(scores, axis=-1, keepdims=True))
    exponent = jnp.exp(scores - row_top)
    prob_low = low(exponent / lax.optimization_barrier(jnp.sum(exponent, axis=-1, keepdims=True)))
    ctx_text = jnp.einsum('hqk,khd->qhd', prob_low, value_text, precision=exact)
    ctx_lay = jnp.einsum('hqk,khd->qhd', prob_low, value_lay, precision=exact)
    return (ctx_text, ctx_lay)

def stream_front(rows_in, attend, biases):
    columns = rows_in.shape[1]
    mixture = product(rows_in, attend.reshape(columns, -1)).reshape(rows_in.shape[0], 3, -1)
    queries = both_low(mixture[:, 0] + biases[0])
    key_rows = both_low(mixture[:, 1])
    value_rows = both_low(mixture[:, 2] + biases[1])
    return (queries, key_rows, value_rows)

def layer(level, text_rows, lay_rows, text_par, lay_par, page_lens):
    streams = (text_par, lay_par)
    row_pairs = (low_back(text_rows), low_back(lay_rows))
    sizes_head = (HEAD, LHEAD)
    page_count = page_lens.shape[0]
    fronts = [stream_front(row_pairs[stream], streams[stream][0][level], streams[stream][1][level]) for stream in range(2)]
    split = [[member.reshape(page_count, PAGE, HEADS, sizes_head[stream]) for member in fronts[stream]] for stream in range(2)]
    contexts = lax.map(jax.checkpoint(page_attention), (split[0][0], split[0][1], split[0][2], split[1][0], split[1][1], split[1][2], page_lens))
    outputs = []
    for stream in range(2):
        params = streams[stream]
        vectors = params[6][level]
        context = both_low(contexts[stream].reshape(row_pairs[stream].shape[0], -1))
        attn = low_back(product(context, params[2][level].T) + vectors[0])
        first = norm_apply(row_pairs[stream] + attn, vectors[1], vectors[2])
        raised = low_back(product(low(first), params[3][level]) + params[4][level])
        active = low(jax.nn.gelu(raised, approximate=False))
        ffn_out = low_back(product(active, params[5][level].T) + vectors[3])
        outputs.append(low(norm_apply(first + ffn_out, vectors[4], vectors[5])))
    return (outputs[0], outputs[1])

def reference(text_in, layout_in, text_cot, layout_cot, lengths, text_attend, text_biases, text_output, text_expand, text_offset, text_shrink, text_vectors, layout_attend, layout_biases, layout_output, layout_expand, layout_offset, layout_shrink, layout_vectors):
    text_rows = text_in.astype(jnp.float32).reshape(-1, text_in.shape[-1])
    lay_rows = layout_in.astype(jnp.float32).reshape(-1, layout_in.shape[-1])
    page_lens = lengths.reshape(-1).astype(jnp.int32)
    text_par = tuple((weight.astype(jnp.float32) for weight in (text_attend, text_biases, text_output, text_expand, text_offset, text_shrink, text_vectors)))
    lay_par = tuple((weight.astype(jnp.float32) for weight in (layout_attend, layout_biases, layout_output, layout_expand, layout_offset, layout_shrink, layout_vectors)))

    def forward(t_rows, l_rows, t_zero, l_zero, t_par, l_par):
        first = layer(0, t_rows, l_rows, t_par, l_par, page_lens)
        second = layer(1, first[0] + t_zero, first[1] + l_zero, t_par, l_par, page_lens)
        return (second, first)
    second, pull, first = jax.vjp(forward, text_rows, lay_rows, jnp.zeros_like(text_rows), jnp.zeros_like(lay_rows), text_par, lay_par, has_aux=True)
    cot_pair = (text_cot.astype(jnp.float32).reshape(text_rows.shape), layout_cot.astype(jnp.float32).reshape(lay_rows.shape))
    grads = pull(cot_pair)
    text_shape = (2,) + text_in.shape
    lay_shape = (2,) + layout_in.shape
    text_out = jnp.stack([first[0], second[0]]).reshape(text_shape).astype(jnp.bfloat16)
    layout_out = jnp.stack([first[1], second[1]]).reshape(lay_shape).astype(jnp.bfloat16)
    text_back = jnp.stack([grads[0], grads[2]]).reshape(text_shape).astype(jnp.bfloat16)
    layout_back = jnp.stack([grads[1], grads[3]]).reshape(lay_shape).astype(jnp.bfloat16)
    text_grads = grads[4]
    lay_grads = grads[5]
    return (text_out, layout_out, text_back, layout_back, text_grads[0], text_grads[1], text_grads[2], text_grads[3], text_grads[4], text_grads[5], text_grads[6], lay_grads[0], lay_grads[1], lay_grads[2], lay_grads[3], lay_grads[4], lay_grads[5], lay_grads[6])
```

```python
import functools
import math

import jax
import jax.numpy as jnp
from jax import lax
from jax.experimental import pallas as pl
from jax.experimental.pallas import tpu as pltpu
from jax.sharding import PartitionSpec as P

HEAD = 64
LHEAD = 16
TENSOR = 4
MESH = pl.DeviceIdType.MESH
bf16 = jnp.bfloat16
f32 = jnp.float32
norm_epsilon = 1e-05
masked_score = -1e30
LANES = 128
SMALL = 1024


def mm(left, right, left_axis, right_axis):
    return lax.dot_general(
        left, right, (((left_axis,), (right_axis,)), ((), ())), preferred_element_type=f32
    )


def flip(index, bit):
    return index + bit - 2 * bit * lax.rem(lax.div(index, bit), 2)


def loop(count, body):
    lax.fori_loop(0, count, lambda i, carry: (body(i), carry)[1], 0)


def at(start, size):
    return pl.ds(pl.multiple_of(start, 16), size)


def kernel(
    dp,
    z_inside,
    text_in, lay_in, text_cot, lay_cot, own_att, own_exp, own_shr, own_lay, own_small, own_vec, key_bias,
    text_out, lay_out, text_back, lay_back, gt, gl, sm_out,
    gb_t, gb_l, r1_t, r1_l, r2_t, r2_l, ro_t, ro_l, zs_t, zs_l, zr_t, zr_l, p_keep,
    w_t, w_l, small, vecs, rows_t, rows_l, cot_t, cot_l, x_fm, qkv_t, qkv_l, probs, ctx_t, ctx_l,
    xh1, n1b, xh2, act, gp, stats, acc, exs, exr, tmpb, g_fm, dup, dqkv, dctx, cols, stg_t, stg_l,
    sv_t, sv_l, sf_t, sf_l, sm, smr,
    ag_recv, ag_own, ag_fwd, vec_sem, row_sem, ex_send, ex_recv, out_sem, stg_sem, p_sem,
    s1_send, s1_recv, s2_send, s2_recv, so_send, so_recv, z_send, z_recv, sv_sem, sf_sem, sm_send, sm_recv, go_sem,
):
    c = lax.axis_index("section")
    d = lax.axis_index("dp")
    t = lax.axis_index("tensor")
    t1, t2 = flip(t, 1), flip(t, 2)
    xb = lax.rem(t, 2)
    zp = lax.rem(d, 2)
    tf = t1 + zp * (t2 - t1)
    td = t2 + zp * (t1 - t2)
    dz = flip(d, 1)
    tw, lw = x_fm.shape[1] - rows_l.shape[1], rows_l.shape[1]
    width = tw + lw
    tokens = x_fm.shape[2]
    half_rows = tokens // 2
    hid_t, hid_l = own_exp.shape[1], own_lay.shape[2]
    hs, ls = ctx_t.shape[2], ctx_l.shape[2]
    heads = hs // HEAD
    blocks = tokens // LANES
    th, lh = tw // 2, lw // 2
    streams = ((0, tw), (tw, lw))

    dp_bits = [1 << k for k in range(dp.bit_length() - 1)]
    z_peers = [lax.rem(d + r, dp) for r in range(1, dp)] if z_inside else [flip(d, b) for b in dp_bits]

    def remote(src, dst, send, recv, device):
        return pltpu.make_async_remote_copy(
            src_ref=src, dst_ref=dst, send_sem=send, recv_sem=recv, device_id=device, device_id_type=MESH
        )

    def landed(ref, sem):
        pltpu.make_async_copy(ref, ref, sem).wait()

    barrier = pltpu.get_barrier_semaphore()
    peers = [(1 - c, d, t), (0, d, t1), (1, d, t1), (0, d, t2), (1, d, t2)] + [(c, z, t) for z in z_peers]
    for peer in peers:
        pl.semaphore_signal(barrier, inc=1, device_id=peer, device_id_type=MESH)
    pl.semaphore_wait(barrier, len(peers))
    other = (1 - c, d, t)

    def row_copies(src_pair, dst_pair, base):
        copies = []
        for k in range(2):
            copies.append(
                remote(
                    src_pair[k].at[1 - xb], dst_pair[k].at[at(xb * half_rows, half_rows)],
                    row_sem.at[base + k, 0], row_sem.at[base + k, 1], (c, d, t1),
                )
            )
        return copies

    def row_own(src_pair, dst_pair, base):
        return [
            pltpu.make_async_copy(
                src_pair[k].at[xb], dst_pair[k].at[at(xb * half_rows, half_rows)], row_sem.at[base + k, 2]
            )
            for k in range(2)
        ]

    def rows_arrive(src_pair, dst_pair, base):
        for copy in row_copies(src_pair, dst_pair, base):
            copy.wait()
        for copy in row_own(src_pair, dst_pair, base):
            copy.wait()

    in_pairs = ((text_in, lay_in), (rows_t, rows_l))
    cot_pairs = ((text_cot, lay_cot), (cot_t, cot_l))
    for copy in row_copies(*in_pairs, 0) + row_own(*in_pairs, 0):
        copy.start()

    own_text = (own_att, own_exp, own_shr)

    def source(p):
        if p < 6:
            return own_text[p // 2].at[pl.ds((p % 2) * th, th)]
        return own_lay.at[p - 6] if p < 9 else own_small

    def place(layer, slot, p):
        if p < 6:
            return w_t.at[layer, slot, p // 2, pl.ds((p % 2) * th, th)]
        return w_l.at[layer, slot, p - 6] if p < 9 else small.at[layer, slot]

    def pieces(j):
        return [j] + ([6 + j // 2] if j % 2 == 0 else []) + ([9] if j == 0 else [])

    def own_first(p):
        return remote(
            source(p), place(c, 1 - zp, p), ag_own.at[p, 0], ag_recv.at[c, 1 - zp, p], (zp, d, tf)
        )

    def own_core(p):
        return remote(source(p), place(1, 0, p), ag_own.at[p, 1], ag_recv.at[1, 0, p], (0, d, t))

    def own_local(p):
        return pltpu.make_async_copy(source(p), place(0, 0, p), ag_recv.at[0, 0, p])

    def forwards(layer, p):
        return (
            remote(
                place(layer, 1 - zp, p), place(layer, 1, p),
                ag_fwd.at[layer, p, 0], ag_recv.at[layer, 1, p], (1, d, td),
            ),
            remote(
                place(layer, 1 - zp, p), place(layer, 1 - zp, p),
                ag_fwd.at[layer, p, 1], ag_recv.at[layer, 1 - zp, p], (zp, dz, t),
            ),
        )

    all_pieces = [p for j in range(6) for p in pieces(j)]

    def forward_step(layer, j):
        @pl.when(c == zp)
        def _():
            for p in pieces(j):
                landed(place(layer, 1 - zp, p), ag_recv.at[layer, 1 - zp, p])
                for copy in forwards(layer, p):
                    copy.start()

    def need_step(layer, j):
        for p in pieces(j):
            landed(place(layer, zp, p), ag_recv.at[layer, zp, p])

        @pl.when(c != zp)
        def _():
            for p in pieces(j):
                landed(place(layer, 1 - zp, p), ag_recv.at[layer, 1 - zp, p])

    vec_local = pltpu.make_async_copy(own_vec, vecs.at[c], vec_sem.at[0])
    vec_remote = remote(own_vec, vecs.at[c], vec_sem.at[1], vec_sem.at[2], other)
    vec_local.start()
    vec_remote.start()

    @pl.when(c == 0)
    def _():
        for p in all_pieces:
            own_first(p).start()
            own_local(p).start()

    @pl.when(c == 1)
    def _():
        for p in all_pieces:
            own_core(p).start()

    def start_second_layer():
        @pl.when(c == 1)
        def _():
            for p in all_pieces:
                own_first(p).start()

    for k in range(2):
        for i in range(5):
            sm[k, i] = jnp.zeros(sm.shape[2:], f32)
    ones = jnp.ones((8, tokens), bf16)
    base_shard = t + c * (t2 - t)
    shards = (base_shard, flip(base_shard, 1))
    once = jnp.where(c == 0, 1.0, 0.0).astype(f32)

    vec_local.wait()
    vec_remote.wait()

    def load_columns(layer):
        for k in range(2):
            cols[k] = small[layer, k].astype(f32).T
        cols[2] = vecs[layer].astype(f32).T

    def column(k, start, size, lane):
        return cols[k, pl.ds(start, size), lane : lane + 1]

    def exchange_copy(n):
        return remote(exs, exr.at[n % 2], ex_send.at[n], ex_recv.at[n], other)

    def exchange(n):
        copy = exchange_copy(n)
        copy.start()
        copy.wait()

    def exchanged(n, start, size, lanes):
        return exs[pl.ds(start, size), lanes].astype(f32) + exr[n % 2, pl.ds(start, size), lanes].astype(f32)

    def project(layer):
        def slot(s):
            mixed = mm(w_t[layer, s, 0, 0 : 3 * hs], x_fm[layer, 0:tw], 1, 0)
            qkv_t[layer, s] = (mixed + cols[s, 0 : 3 * hs, 1:2]).astype(bf16)
            mixed = mm(w_l[layer, s, 0, 0 : 3 * ls], x_fm[layer, tw:width], 1, 0)
            qkv_l[layer, s] = (mixed + cols[s, 3 * hs : 3 * hs + 3 * ls, 1:2]).astype(bf16)

        loop(2, slot)

    def head_rows(layer, s, part, h):
        return (
            qkv_t[layer, s, at(part * hs + h * HEAD, HEAD)],
            qkv_l[layer, s, at(part * ls + h * LHEAD, LHEAD)],
        )

    def query(layer, s, h):
        text, lay = head_rows(layer, s, 0, h)
        return jnp.concatenate([text * HEAD**-0.5, lay * LHEAD**-0.5], axis=0).astype(bf16)

    def attend_forward(layer):
        def head(i):
            s, h = lax.div(i, heads), lax.rem(i, heads)
            keys = jnp.concatenate(head_rows(layer, s, 1, h), axis=0)
            values = jnp.concatenate(head_rows(layer, s, 2, h), axis=0)
            scores = mm(keys, query(layer, s, h), 0, 0) + key_bias[:, 0:1]
            exponent = jnp.exp(scores - jnp.max(scores, axis=0, keepdims=True))
            low = (exponent * (1.0 / jnp.sum(exponent, axis=0, keepdims=True))).astype(bf16)
            probs[i] = low
            context = mm(values, low, 1, 0).astype(bf16)
            ctx_t[layer, s, at(h * HEAD, HEAD)] = context[0:HEAD]
            ctx_l[layer, s, at(h * LHEAD, LHEAD)] = context[HEAD:]

        return head

    def attention_partial(layer):
        exs[0:tw] = (
            mm(w_t[layer, 0, 0, 3 * hs : 4 * hs], ctx_t[layer, 0], 0, 0)
            + mm(w_t[layer, 1, 0, 3 * hs : 4 * hs], ctx_t[layer, 1], 0, 0)
        ).astype(bf16)
        exs[tw:width] = (
            mm(w_l[layer, 0, 0, 3 * ls : 4 * ls], ctx_l[layer, 0], 0, 0)
            + mm(w_l[layer, 1, 0, 3 * ls : 4 * ls], ctx_l[layer, 1], 0, 0)
        ).astype(bf16)

    def normalize(hidden):
        center = hidden - jnp.mean(hidden, axis=0, keepdims=True)
        scale = lax.rsqrt(jnp.mean(center * center, axis=0, keepdims=True) + norm_epsilon)
        return center * scale, scale

    def norm_forward(layer, n, which, base, hat_ref, finish):
        def block(b):
            lanes = pl.ds(pl.multiple_of(b * LANES, LANES), LANES)
            for k, (start, size) in enumerate(streams):
                hidden = base(start, size, lanes) + exchanged(n, start, size, lanes)
                hat, scale = normalize(hidden + column(2, start, size, 3 * which))
                hat_ref[layer, pl.ds(start, size), lanes] = hat.astype(bf16)
                row = 2 * which + k
                stats[layer, row : row + 1, lanes] = scale
                result = hat * column(2, start, size, 3 * which + 1) + column(2, start, size, 3 * which + 2)
                finish(start, size, lanes, result)

        loop(blocks, block)

    def first_norm(layer, n):
        def finish(start, size, lanes, result):
            acc[pl.ds(start, size), lanes] = result
            n1b[layer, pl.ds(start, size), lanes] = result.astype(bf16)

        norm_forward(
            layer, n, 0, lambda s, z, lanes: x_fm[layer, pl.ds(s, z), lanes].astype(f32), xh1, finish
        )

    def second_norm(layer, n, dest):
        def finish(start, size, lanes, result):
            dest[pl.ds(start, size), lanes] = result.astype(bf16)

        norm_forward(layer, n, 1, lambda s, z, lanes: acc[pl.ds(s, z), lanes], xh2, finish)

    def gelu_pair(raised):
        cdf = 0.5 * (1.0 + lax.erf(raised * math.sqrt(0.5)))
        slope = cdf + raised * (jnp.exp(-0.5 * raised * raised) * (1.0 / math.sqrt(2.0 * math.pi)))
        return (raised * cdf).astype(bf16), slope.astype(bf16)

    hb = 256

    def expand_forward(layer):
        def text_block(i):
            s, b = lax.div(i, hid_t // hb), lax.rem(i, hid_t // hb)
            rows = pl.ds(pl.multiple_of(b * hb, hb), hb)
            raised = mm(w_t[layer, s, 1, :, rows], n1b[layer, 0:tw], 0, 0) + cols[s, rows, 0:1]
            act[layer, s, rows], gp[layer, s, rows] = gelu_pair(raised)

        loop(2 * (hid_t // hb), text_block)

        def lay_block(s):
            raised = mm(w_l[layer, s, 1], n1b[layer, tw:width], 0, 0) + cols[s, hid_t : hid_t + hid_l, 0:1]
            act[layer, s, hid_t:], gp[layer, s, hid_t:] = gelu_pair(raised)

        loop(2, lay_block)

    def shrink_partial(layer):
        exs[0:tw] = (
            mm(w_t[layer, 0, 2], act[layer, 0, 0:hid_t], 1, 0) + mm(w_t[layer, 1, 2], act[layer, 1, 0:hid_t], 1, 0)
        ).astype(bf16)
        exs[tw:width] = (
            mm(w_l[layer, 0, 2], act[layer, 0, hid_t:], 1, 0) + mm(w_l[layer, 1, 2], act[layer, 1, hid_t:], 1, 0)
        ).astype(bf16)

    def rows_out(base, dest_pair):
        own, away = [], []
        for k, staged in enumerate((rows_t, rows_l)):
            own.append(
                pltpu.make_async_copy(
                    staged.at[at(xb * half_rows, half_rows)], dest_pair[k].at[xb], out_sem.at[base + k, 0]
                )
            )
            away.append(
                remote(
                    staged.at[at((1 - xb) * half_rows, half_rows)], dest_pair[k].at[xb],
                    out_sem.at[base + k, 1], out_sem.at[base + k, 2], (c, d, t1),
                )
            )
        return own, away

    def send_rows(layer, base, dest_pair, value):
        @pl.when(c == layer)
        def _():
            rows_t[...] = value[0:tw].T
            rows_l[...] = value[tw:width].T
            own, away = rows_out(base, dest_pair)
            for copy in own + away:
                copy.start()

    def finish_rows(layer, base, dest_pair):
        @pl.when(c == layer)
        def _():
            own, away = rows_out(base, dest_pair)
            for copy in own + away:
                copy.wait()

    out_pair, back_pair = (text_out, lay_out), (text_back, lay_back)
    rows_arrive(*in_pairs, 0)
    x_fm[0, 0:tw] = rows_t[...].T
    x_fm[0, tw:width] = rows_l[...].T

    p_store = pltpu.make_async_copy(probs, p_keep, p_sem.at[0])
    p_load = pltpu.make_async_copy(p_keep, probs, p_sem.at[1])

    for layer in range(2):
        forward_step(layer, 0)
        forward_step(layer, 1)
        need_step(layer, 0)
        need_step(layer, 1)
        load_columns(layer)
        project(layer)
        if layer == 1:
            p_store.wait()
            for copy in row_copies(*cot_pairs, 2) + row_own(*cot_pairs, 2):
                copy.start()
        head = attend_forward(layer)
        lax.fori_loop(0, heads, lambda i, carry: (head(i), carry)[1], 0)
        forward_step(layer, 2)
        lax.fori_loop(heads, 2 * heads, lambda i, carry: (head(i), carry)[1], 0)
        if layer == 0:
            p_store.start()
        forward_step(layer, 3)
        attention_partial(layer)
        exchange(2 * layer)
        first_norm(layer, 2 * layer)
        need_step(layer, 2)
        need_step(layer, 3)
        expand_forward(layer)
        forward_step(layer, 4)
        need_step(layer, 4)
        if layer == 0:
            start_second_layer()
        forward_step(layer, 5)
        need_step(layer, 5)
        shrink_partial(layer)
        exchange(2 * layer + 1)
        if layer == 0:
            second_norm(0, 1, x_fm.at[1])
            send_rows(0, 0, out_pair, x_fm.at[1])
        else:
            second_norm(1, 3, tmpb)
            send_rows(1, 0, out_pair, tmpb)

    def grad_store(layer, chunk, s):
        return (
            pltpu.make_async_copy(stg_t.at[s], gb_t.at[layer, chunk, s], stg_sem.at[s, 0]),
            pltpu.make_async_copy(stg_l.at[s], gb_l.at[layer, chunk, s], stg_sem.at[s, 1]),
        )

    def store_grad(layer, chunk, s, text_value, lay_value):
        stg_t[s] = text_value
        stg_l[s] = lay_value
        for copy in grad_store(layer, chunk, s):
            copy.start()

    def first_sends(layer, chunk):
        halves = ((gb_t, r1_t, r2_t, th), (gb_l, r1_l, r2_l, lh))
        zero, one = [], []
        for k, (grad, transit, final, size) in enumerate(halves):
            h1, h2 = pl.ds(0, size), pl.ds(size, size)
            zero.append(
                remote(
                    grad.at[layer, chunk, 1, h1], final.at[chunk, 0, h1],
                    s1_send.at[layer, chunk, k, 0], s2_recv.at[chunk, 0, 0, k], (layer, d, t1),
                )
            )
            one.append(
                remote(
                    grad.at[layer, chunk, 1, h1], transit.at[layer, chunk],
                    s1_send.at[layer, chunk, k, 0], s1_recv.at[layer, chunk, k], (1, d, t1),
                )
            )
            one.append(
                remote(
                    grad.at[layer, chunk, 1, h2], transit.at[layer, chunk],
                    s1_send.at[layer, chunk, k, 1], s1_recv.at[layer, chunk, k], (0, d, t2),
                )
            )
            one.append(
                remote(
                    grad.at[layer, chunk, 0, h2], final.at[chunk, 1, h2],
                    s1_send.at[layer, chunk, k, 2], s2_recv.at[chunk, 1, 1, k], (layer, d, t2),
                )
            )
        if layer == 1:
            for k, (grad, arrive) in enumerate(((gb_t, ro_t), (gb_l, ro_l))):
                zero.append(
                    remote(
                        grad.at[1, chunk, 0], arrive.at[chunk], so_send.at[chunk, k], so_recv.at[chunk, k], other
                    )
                )
        return zero, one

    def grads_go(layer, chunk):
        for s in range(2):
            for copy in grad_store(layer, chunk, s):
                copy.wait()
        zero, one = first_sends(layer, chunk)

        @pl.when(c == 0)
        def _():
            for copy in zero:
                copy.start()

        @pl.when(c == 1)
        def _():
            for copy in one:
                copy.start()

    tx = t1 + c * (t2 - t1)

    def second_sends(layer, chunk):
        return [
            remote(
                grad.at[layer, chunk, 1 - c, at((1 - c) * size, size)],
                final.at[chunk, c, at((1 - c) * size, size)],
                s2_send.at[layer, chunk, k], s2_recv.at[chunk, c, 1 - c, k], (layer, d, tx),
            )
            for k, (grad, final, size) in enumerate(((gb_t, r2_t, th), (gb_l, r2_l, lh)))
        ]

    def transit(layer, chunk):
        loads = []
        for k, (grad, come, size, sv) in enumerate(((gb_t, r1_t, th, sv_t), (gb_l, r1_l, lh, sv_l))):
            landed(come.at[layer, chunk], s1_recv.at[layer, chunk, k])
            mine = grad.at[layer, chunk, 1 - c, at((1 - c) * size, size)]
            loads.append(pltpu.make_async_copy(mine, sv.at[0], sv_sem.at[k, 0]))
            loads.append(pltpu.make_async_copy(come.at[layer, chunk], sv.at[1], sv_sem.at[k, 1]))
        for copy in loads:
            copy.start()
        for copy in loads:
            copy.wait()
        stores = []
        for k, (grad, size, sv) in enumerate(((gb_t, th, sv_t), (gb_l, lh, sv_l))):
            sv[2] = (sv[0].astype(f32) + sv[1].astype(f32)).astype(bf16)
            mine = grad.at[layer, chunk, 1 - c, at((1 - c) * size, size)]
            stores.append(pltpu.make_async_copy(sv.at[2], mine, sv_sem.at[k, 2]))
        for copy in stores:
            copy.start()
        for copy in stores:
            copy.wait()
        for copy in second_sends(layer, chunk):
            copy.start()

    def z_sends(chunk):
        copies = []
        if z_inside:
            for k, (total, come) in enumerate(((zs_t, zr_t), (zs_l, zr_l))):
                size = come.shape[2]
                for r in range(1, dp):
                    j = lax.rem(d + r, dp)
                    copies.append(
                        remote(
                            total.at[chunk, at(j * size, size)], come.at[chunk, r - 1],
                            z_send.at[chunk, k, r - 1], z_recv.at[chunk, k, r - 1], (c, j, t),
                        )
                    )
        return copies

    def final(layer, chunk):
        @pl.when(c == layer)
        def _():
            groups = ((gb_t, ro_t, r2_t, zs_t, th, sv_t), (gb_l, ro_l, r2_l, zs_l, lh, sv_l))
            for k, (grad, arrive, come, total, size, sv) in enumerate(groups):
                for way in range(2):
                    for h in range(2):
                        part = come.at[chunk, way, pl.ds(h * size, size)]
                        landed(part, s2_recv.at[chunk, way, h, k])
                if layer == 1:
                    landed(arrive.at[chunk], so_recv.at[chunk, k])
            for h in range(2):
                loads, stores = [], []
                for k, (grad, arrive, come, total, size, sv) in enumerate(groups):
                    rows = pl.ds(h * size, size)
                    own = arrive.at[chunk, rows] if layer == 1 else grad.at[layer, chunk, 0, rows]
                    loads.append(pltpu.make_async_copy(own, sv.at[0], sv_sem.at[k, 0]))
                    loads.append(pltpu.make_async_copy(come.at[chunk, 0, rows], sv.at[1], sv_sem.at[k, 1]))
                    loads.append(pltpu.make_async_copy(come.at[chunk, 1, rows], sv.at[2], sv_sem.at[k, 2]))
                for copy in loads:
                    copy.start()
                for copy in loads:
                    copy.wait()
                for k, (grad, arrive, come, total, size, sv) in enumerate(groups):
                    sv[3] = (sv[0].astype(f32) + sv[1].astype(f32) + sv[2].astype(f32)).astype(bf16)
                    stores.append(
                        pltpu.make_async_copy(sv.at[3], total.at[chunk, pl.ds(h * size, size)], sv_sem.at[k, 3])
                    )
                for copy in stores:
                    copy.start()
                for copy in stores:
                    copy.wait()
            for copy in z_sends(chunk):
                copy.start()

    def z_final(layer, chunk):
        if not z_inside:
            return

        @pl.when(c == layer)
        def _():
            groups = ((zs_t, zr_t, gt, sf_t), (zs_l, zr_l, gl, sf_l))
            for copy in z_sends(chunk):
                copy.wait()
            loads, stores = [], []
            for k, (total, come, result, sf) in enumerate(groups):
                size = come.shape[2]
                sv = (sv_t, sv_l)[k]
                loads.append(
                    pltpu.make_async_copy(total.at[chunk, at(d * size, size)], sv.at[3, pl.ds(0, size)], sv_sem.at[k, 3])
                )
                for r in range(dp - 1):
                    loads.append(
                        pltpu.make_async_copy(come.at[chunk, r], sv.at[r, pl.ds(0, size)], sv_sem.at[k, r])
                    )
            for copy in loads:
                copy.start()
            for copy in loads:
                copy.wait()
            for k, (total, come, result, sf) in enumerate(groups):
                size = come.shape[2]
                sv = (sv_t, sv_l)[k]
                summed = sv[3, 0:size].astype(f32)
                for r in range(dp - 1):
                    summed = summed + sv[r, 0:size].astype(f32)
                sf[...] = summed
                stores.append(pltpu.make_async_copy(sf, result.at[chunk], sf_sem.at[k]))
            for copy in stores:
                copy.start()
            for copy in stores:
                copy.wait()

    def row_sums(ref, index):
        return mm(ones, ref[index] if index is not None else ref[...], 1, 1)[0:1]

    def vector_sum(layer, row, value):
        sm[layer, 4, row : row + 1, 0:width] = value * once

    def norm_backward(layer, which, hat_ref, incoming):
        def block(b):
            lanes = pl.ds(pl.multiple_of(b * LANES, LANES), LANES)
            for k, (start, size) in enumerate(streams):
                grad = incoming(start, size, lanes)
                hat = hat_ref[layer, pl.ds(start, size), lanes].astype(f32)
                row = 2 * which + k
                scale = stats[layer, row : row + 1, lanes]
                gained = grad * column(2, start, size, 3 * which + 1)
                mean_grad = jnp.mean(gained, axis=0, keepdims=True)
                mean_both = jnp.mean(gained * hat, axis=0, keepdims=True)
                result = scale * (gained - mean_grad - hat * mean_both)
                acc[pl.ds(start, size), lanes] = result
                tmpb[pl.ds(start, size), lanes] = result.astype(bf16)
                exs[pl.ds(start, size), lanes] = (grad * hat).astype(bf16)
                g_fm[pl.ds(start, size), lanes] = grad.astype(bf16)

        loop(blocks, block)
        vector_sum(layer, 3 * which + 1, row_sums(exs, None))
        vector_sum(layer, 3 * which + 2, row_sums(g_fm, None))
        vector_sum(layer, 3 * which, row_sums(tmpb, None))

    def ffn_backward(layer):
        def text_block(i):
            s, b = lax.div(i, hid_t // hb), lax.rem(i, hid_t // hb)
            rows = pl.ds(pl.multiple_of(b * hb, hb), hb)
            back = mm(w_t[layer, s, 2, :, rows], tmpb[0:tw], 0, 0)
            dup[s, rows] = (back * gp[layer, s, rows].astype(f32)).astype(bf16)

        loop(2 * (hid_t // hb), text_block)

        def lay_block(s):
            back = mm(w_l[layer, s, 2], tmpb[tw:width], 0, 0)
            dup[s, hid_t:] = (back * gp[layer, s, hid_t:].astype(f32)).astype(bf16)

        loop(2, lay_block)

    def shrink_grads(layer, s):
        store_grad(
            layer, 2, s,
            mm(tmpb[0:tw], act[layer, s, 0:hid_t], 1, 1).astype(bf16),
            mm(tmpb[tw:width], act[layer, s, hid_t:], 1, 1).astype(bf16),
        )

    def expand_grads(layer, s):
        store_grad(
            layer, 1, s,
            mm(n1b[layer, 0:tw], dup[s, 0:hid_t], 1, 1).astype(bf16),
            mm(n1b[layer, tw:width], dup[s, hid_t:], 1, 1).astype(bf16),
        )

    def expand_partial(layer):
        exs[0:tw] = (
            mm(w_t[layer, 0, 1], dup[0, 0:hid_t], 1, 0) + mm(w_t[layer, 1, 1], dup[1, 0:hid_t], 1, 0)
        ).astype(bf16)
        exs[tw:width] = (
            mm(w_l[layer, 0, 1], dup[0, hid_t:], 1, 0) + mm(w_l[layer, 1, 1], dup[1, hid_t:], 1, 0)
        ).astype(bf16)

    def context_grads(layer):
        def slot(s):
            dctx[s, 0:hs] = mm(w_t[layer, s, 0, 3 * hs : 4 * hs], tmpb[0:tw], 1, 0).astype(bf16)
            dctx[s, hs:] = mm(w_l[layer, s, 0, 3 * ls : 4 * ls], tmpb[tw:width], 1, 0).astype(bf16)

        loop(2, slot)

    def attend_backward(layer):
        def head(i):
            s, h = lax.div(i, heads), lax.rem(i, heads)
            queries = query(layer, s, h)
            key_text, key_lay = head_rows(layer, s, 1, h)
            keys = jnp.concatenate([key_text * HEAD**-0.5, key_lay * LHEAD**-0.5], axis=0).astype(bf16)
            values = jnp.concatenate(head_rows(layer, s, 2, h), axis=0)
            grads = jnp.concatenate([dctx[s, at(h * HEAD, HEAD)], dctx[s, at(hs + h * LHEAD, LHEAD)]], axis=0)
            low = probs[i]
            prob = low.astype(f32)
            dprob = mm(values, grads, 0, 0)
            inner = jnp.sum(dprob * prob, axis=0, keepdims=True)
            dscore = (prob * (dprob - inner)).astype(bf16)
            results = (mm(keys, dscore, 1, 0), mm(queries, dscore, 1, 1), mm(grads, low, 1, 1))
            for part, result in enumerate(results):
                result = result.astype(bf16)
                dqkv[s, at(part * hs + h * HEAD, HEAD)] = result[0:HEAD]
                dqkv[s, at(3 * hs + part * ls + h * LHEAD, LHEAD)] = result[HEAD:]

        loop(2 * heads, head)

    def attend_grads(layer, s):
        text = jnp.concatenate(
            [mm(x_fm[layer, 0:tw], dqkv[s, 0 : 3 * hs], 1, 1), mm(tmpb[0:tw], ctx_t[layer, s], 1, 1)], axis=1
        )
        lay = jnp.concatenate(
            [mm(x_fm[layer, tw:width], dqkv[s, 3 * hs :], 1, 1), mm(tmpb[tw:width], ctx_l[layer, s], 1, 1)], axis=1
        )
        store_grad(layer, 0, s, text.astype(bf16), lay.astype(bf16))

    def attend_partial(layer):
        exs[0:tw] = (
            mm(w_t[layer, 0, 0, 0 : 3 * hs], dqkv[0, 0 : 3 * hs], 0, 0)
            + mm(w_t[layer, 1, 0, 0 : 3 * hs], dqkv[1, 0 : 3 * hs], 0, 0)
        ).astype(bf16)
        exs[tw:width] = (
            mm(w_l[layer, 0, 0, 0 : 3 * ls], dqkv[0, 3 * hs :], 0, 0)
            + mm(w_l[layer, 1, 0, 0 : 3 * ls], dqkv[1, 3 * hs :], 0, 0)
        ).astype(bf16)

    def small_sums(layer, s, row, ref, size):
        sm[layer, shards[s], row : row + 1, 0:size] = mm(ones, ref[s], 1, 1)[0:1]

    rows_arrive(*cot_pairs, 2)
    g_fm[0:tw] = cot_t[...].T
    g_fm[tw:width] = cot_l[...].T
    for layer in (1, 0):
        n = 4 + 2 * (1 - layer)
        if layer == 0:
            load_columns(0)
        norm_backward(layer, 1, xh2, lambda s, z, lanes: g_fm[pl.ds(s, z), lanes].astype(f32))
        if layer == 0:
            grads_go(1, 0)
        for s in range(2):
            shrink_grads(layer, s)
        ffn_backward(layer)
        grads_go(layer, 2)
        for s in range(2):
            expand_grads(layer, s)
        expand_partial(layer)
        exchange(n)
        grads_go(layer, 1)
        for s in range(2):
            small_sums(layer, s, 0, dup, hid_t + hid_l)
        norm_backward_input = functools.partial(
            lambda k, s, z, lanes: acc[pl.ds(s, z), lanes] + exr[k % 2, pl.ds(s, z), lanes].astype(f32)
            + exs[pl.ds(s, z), lanes].astype(f32),
            n,
        )
        norm_backward(layer, 0, xh1, norm_backward_input)
        if layer == 0:
            p_load.wait()
        context_grads(layer)
        attend_backward(layer)
        if layer == 1:
            p_load.start()
        for s in range(2):
            attend_grads(layer, s)
        attend_partial(layer)
        exchange(n + 1)
        for s in range(2):
            small_sums(layer, s, 1, dqkv, 3 * hs + 3 * ls)

        def finish(b):
            lanes = pl.ds(pl.multiple_of(b * LANES, LANES), LANES)
            for start, size in streams:
                total = acc[pl.ds(start, size), lanes] + exchanged(n + 1, start, size, lanes)
                g_fm[pl.ds(start, size), lanes] = total.astype(bf16)

        loop(blocks, finish)
        if layer == 1:
            finish_rows(1, 0, out_pair)
            send_rows(1, 2, back_pair, g_fm)
            transit(1, 2)
        else:
            grads_go(0, 0)
            finish_rows(0, 0, out_pair)
            send_rows(0, 2, back_pair, g_fm)

    steps = [(1 - c, d, t), (c, d, t1), (c, d, t2)] + [(c, flip(d, b), t) for b in dp_bits]
    small_pending = []

    def small_step(i):
        copy = remote(sm, smr.at[i], sm_send.at[i], sm_recv.at[i], steps[i])
        copy.start()
        small_pending.append((i, copy))

    def small_done():
        i, copy = small_pending.pop()
        copy.wait()
        for k in range(2):
            for j in range(5):
                sm[k, j] = sm[k, j] + smr[i, k, j]

    tail = [
        lambda: transit(1, 1), lambda: transit(1, 0), lambda: final(1, 2), lambda: transit(0, 2),
        lambda: final(1, 1), lambda: transit(0, 1), lambda: final(1, 0), lambda: z_final(1, 2),
        lambda: transit(0, 0), lambda: z_final(1, 1), lambda: final(0, 2), lambda: final(0, 1),
        lambda: z_final(1, 0), lambda: z_final(0, 2), lambda: final(0, 0), lambda: z_final(0, 1),
    ]
    count = len(steps)
    for i, task in enumerate(tail):
        if i < count:
            small_step(i)
        task()
        if i < count:
            small_done()
    sm_copy = pltpu.make_async_copy(sm, sm_out, sf_sem.at[2])
    sm_copy.start()
    z_final(0, 0)
    sm_copy.wait()

    for layer in range(2):
        finish_rows(layer, 2, back_pair)

        @pl.when(c == layer)
        def _():
            for p in all_pieces:
                own_first(p).wait_send()
            if layer == 1:
                for p in all_pieces:
                    own_core(p).wait_send()
            if not z_inside:
                for chunk in range(3):
                    for copy in z_sends(chunk):
                        copy.wait_send()

        @pl.when(c == zp)
        def _():
            for p in all_pieces:
                for copy in forwards(layer, p):
                    copy.wait_send()

        for chunk in range(3):
            zero, one = first_sends(layer, chunk)

            @pl.when(c == 0)
            def _():
                for copy in zero:
                    copy.wait_send()

            @pl.when(c == 1)
            def _():
                for copy in one:
                    copy.wait_send()

            for copy in second_sends(layer, chunk):
                copy.wait_send()


def local(
    dp,
    text_in,
    layout_in,
    text_cot,
    layout_cot,
    lengths,
    text_attend,
    text_biases,
    text_output,
    text_expand,
    text_offset,
    text_shrink,
    text_vectors,
    layout_attend,
    layout_biases,
    layout_output,
    layout_expand,
    layout_offset,
    layout_shrink,
    layout_vectors,
):
    section = lax.axis_index("section")
    tensor = lax.axis_index("tensor")
    rows, tw = text_in.shape[1:]
    lw = layout_in.shape[2]
    width, tokens = tw + lw, 2 * rows
    hs, ls = text_output.shape[2], layout_output.shape[2]
    ft, fl = text_expand.shape[2], layout_expand.shape[2]
    z_inside = dp <= 4 and (lw // dp) % 16 == 0 and (tw // dp) % 16 == 0
    zt, zl = tw // dp, lw // dp

    page_len = lengths[lax.rem(tensor, 2), lax.div(tensor, 2)]
    bias_column = jnp.where(jnp.arange(tokens) < page_len, 0.0, masked_score).astype(f32)
    key_bias = jnp.broadcast_to(bias_column[:, None], (tokens, LANES))

    def pack_attend(attend, output):
        return jnp.concatenate(
            [attend[0].transpose(1, 2, 0).reshape(-1, attend.shape[1]), output[0].T], axis=0
        )

    own_att = pack_attend(text_attend, text_output)
    own_lay = jnp.stack([pack_attend(layout_attend, layout_output), layout_expand[0], layout_shrink[0]])

    def biases(pair):
        return jnp.stack([pair[0, 0], jnp.zeros_like(pair[0, 0]), pair[0, 1]]).reshape(-1)

    def padded(values):
        return jnp.pad(values, ((0, 16 - values.shape[0]), (0, SMALL - values.shape[1])))

    first_row = jnp.concatenate([text_offset[0], layout_offset[0]])
    second_row = jnp.concatenate([biases(text_biases), biases(layout_biases)])
    second_row = jnp.pad(second_row, (0, first_row.shape[0] - second_row.shape[0]))
    own_small = padded(jnp.stack([first_row, second_row]))
    own_vec = padded(jnp.concatenate([text_vectors[0], layout_vectors[0]], axis=1))

    hbm = pl.BlockSpec(memory_space=pltpu.HBM)
    vmem = pl.BlockSpec(memory_space=pltpu.VMEM)

    def shape(dims, dtype=bf16):
        return jax.ShapeDtypeStruct(dims, dtype)

    heads = hs // HEAD
    out_shape = [
        shape((2, rows, tw)), shape((2, rows, lw)), shape((2, rows, tw)), shape((2, rows, lw)),
        shape((3, zt, tw), f32), shape((3, zl, lw), f32), shape((2, 5, 8, SMALL), f32),
        shape((2, 3, 2, tw, tw)), shape((2, 3, 2, lw, lw)),
        shape((2, 3, tw // 2, tw)), shape((2, 3, lw // 2, lw)),
        shape((3, 2, tw, tw)), shape((3, 2, lw, lw)),
        shape((3, tw, tw)), shape((3, lw, lw)),
        shape((3, tw, tw)), shape((3, lw, lw)),
        shape((3, 3, zt, tw)), shape((3, 3, zl, lw)),
        shape((2 * heads, tokens, tokens)),
    ]
    dma = pltpu.SemaphoreType.DMA
    bits = dp.bit_length() - 1
    scratch = [
        pltpu.VMEM((2, 2, 3, tw, tw), bf16),
        pltpu.VMEM((2, 2, 3, lw, lw), bf16),
        pltpu.VMEM((2, 2, 16, SMALL), bf16),
        pltpu.VMEM((2, 16, SMALL), bf16),
        pltpu.VMEM((tokens, tw), bf16),
        pltpu.VMEM((tokens, lw), bf16),
        pltpu.VMEM((tokens, tw), bf16),
        pltpu.VMEM((tokens, lw), bf16),
        pltpu.VMEM((2, width, tokens), bf16),
        pltpu.VMEM((2, 2, 3 * hs, tokens), bf16),
        pltpu.VMEM((2, 2, 3 * ls, tokens), bf16),
        pltpu.VMEM((2 * heads, tokens, tokens), bf16),
        pltpu.VMEM((2, 2, hs, tokens), bf16),
        pltpu.VMEM((2, 2, ls, tokens), bf16),
        pltpu.VMEM((2, width, tokens), bf16),
        pltpu.VMEM((2, width, tokens), bf16),
        pltpu.VMEM((2, width, tokens), bf16),
        pltpu.VMEM((2, 2, ft + fl, tokens), bf16),
        pltpu.VMEM((2, 2, ft + fl, tokens), bf16),
        pltpu.VMEM((2, 8, tokens), f32),
        pltpu.VMEM((width, tokens), f32),
        pltpu.VMEM((width, tokens), bf16),
        pltpu.VMEM((2, width, tokens), bf16),
        pltpu.VMEM((width, tokens), bf16),
        pltpu.VMEM((width, tokens), bf16),
        pltpu.VMEM((2, ft + fl, tokens), bf16),
        pltpu.VMEM((2, 3 * hs + 3 * ls, tokens), bf16),
        pltpu.VMEM((2, hs + ls, tokens), bf16),
        pltpu.VMEM((3, SMALL, 16), f32),
        pltpu.VMEM((2, tw, tw), bf16),
        pltpu.VMEM((2, lw, lw), bf16),
        pltpu.VMEM((4, tw // 2, tw), bf16),
        pltpu.VMEM((4, lw // 2, lw), bf16),
        pltpu.VMEM((zt, tw), f32),
        pltpu.VMEM((zl, lw), f32),
        pltpu.VMEM((2, 5, 8, SMALL), f32),
        pltpu.VMEM((3 + bits, 2, 5, 8, SMALL), f32),
        dma((2, 2, 10)), dma((10, 2)), dma((2, 10, 2)), dma((3,)), dma((4, 3)), dma((8,)), dma((8,)),
        dma((4, 3)), dma((2, 2)), dma((2,)),
        dma((2, 3, 2, 3)), dma((2, 3, 2)), dma((2, 3, 2)), dma((3, 2, 2, 2)), dma((3, 2)), dma((3, 2)),
        dma((3, 2, 3)), dma((3, 2, 3)), dma((2, 4)), dma((3,)), dma((3 + bits,)), dma((3 + bits,)),
        pltpu.SemaphoreType.REGULAR,
    ]
    results = pl.pallas_call(
        functools.partial(kernel, dp, z_inside),
        out_shape=out_shape,
        in_specs=[hbm] * 10 + [vmem],
        out_specs=[hbm] * len(out_shape),
        scratch_shapes=scratch,
        compiler_params=pltpu.CompilerParams(
            collective_id=0, has_side_effects=True, vmem_limit_bytes=63 * 1024 * 1024
        ),
    )(
        text_in, layout_in, text_cot, layout_cot, own_att, text_expand[0], text_shrink[0], own_lay,
        own_small, own_vec, key_bias,
    )
    text_out, lay_out, text_back, lay_back, gt, gl, sums = results[:7]
    if not z_inside:
        gt = lax.psum_scatter(results[15], "dp", scatter_dimension=1, tiled=True).astype(f32)
        gl = lax.psum_scatter(results[16], "dp", scatter_dimension=1, tiled=True).astype(f32)
    sums = lax.dynamic_index_in_dim(sums, section, 0, keepdims=False)
    shard = lax.dynamic_index_in_dim(sums, tensor, 0, keepdims=False)

    def bias_grad(start, size):
        return jnp.stack([shard[1, start : start + size], shard[1, start + 2 * size : start + 3 * size]])

    return (
        text_out[None],
        lay_out[None],
        text_back[None],
        lay_back[None],
        gt[0, :, : 3 * hs].reshape(1, zt, 3, hs),
        bias_grad(0, hs)[None],
        gt[0, :, 3 * hs :][None],
        gt[1][None],
        shard[0, :ft][None],
        gt[2][None],
        sums[4, :6, :tw][None],
        gl[0, :, : 3 * ls].reshape(1, zl, 3, ls),
        bias_grad(3 * hs, ls)[None],
        gl[0, :, 3 * ls :][None],
        gl[1][None],
        shard[0, ft : ft + fl][None],
        gl[2][None],
        sums[4, :6, tw:width][None],
    )


def solution(mesh):
    return jax.shard_map(
        functools.partial(local, mesh.shape["dp"]),
        mesh=mesh,
        in_specs=(
            P(None, ("dp", "tensor"), None),
            P(None, ("dp", "tensor"), None),
            P(None, ("dp", "tensor"), None),
            P(None, ("dp", "tensor"), None),
            P(None, "dp"),
            P("section", None, None, "tensor"),
            P("section", None, "tensor"),
            P("section", None, "tensor"),
            P("section", None, "tensor"),
            P("section", "tensor"),
            P("section", None, "tensor"),
            P("section", None, None),
            P("section", None, None, "tensor"),
            P("section", None, "tensor"),
            P("section", None, "tensor"),
            P("section", None, "tensor"),
            P("section", "tensor"),
            P("section", None, "tensor"),
            P("section", None, None),
        ),
        out_specs=(
            P("section", None, ("dp", "tensor"), None),
            P("section", None, ("dp", "tensor"), None),
            P("section", None, ("dp", "tensor"), None),
            P("section", None, ("dp", "tensor"), None),
            P("section", "dp", None, "tensor"),
            P("section", None, "tensor"),
            P("section", "dp", "tensor"),
            P("section", "dp", "tensor"),
            P("section", "tensor"),
            P("section", "dp", "tensor"),
            P("section", None, None),
            P("section", "dp", None, "tensor"),
            P("section", None, "tensor"),
            P("section", "dp", "tensor"),
            P("section", "dp", "tensor"),
            P("section", "tensor"),
            P("section", "dp", "tensor"),
            P("section", None, None),
        ),
        check_vma=False,
    )
```

```python
import functools
import math

import jax
import jax.numpy as jnp
from jax import lax
from jax.experimental import pallas as pl
from jax.experimental.pallas import tpu as pltpu
from jax.sharding import PartitionSpec as P

HEAD = 64
LHEAD = 16
MESH = pl.DeviceIdType.MESH
bf16 = jnp.bfloat16
f32 = jnp.float32
norm_epsilon = 1e-05
masked_score = -1e30
LANES = 128
SMALL = 1024
STEPS = 12


def mm(left, right, left_axis, right_axis):
    return lax.dot_general(
        left, right, (((left_axis,), (right_axis,)), ((), ())), preferred_element_type=f32
    )


def flip(index, bit):
    return index + bit - 2 * bit * lax.rem(lax.div(index, bit), 2)


def loop(start, stop, body):
    lax.fori_loop(start, stop, lambda i, carry: (body(i), carry)[1], 0)


def at(start, size):
    return pl.ds(pl.multiple_of(start, 16), size)


def lanes_at(start, size):
    return pl.ds(pl.multiple_of(start, LANES), size)


def kernel(
    dp,
    z_inside,
    text_in, lay_in, text_cot, lay_cot, att_t, out_t, exp_t, shr_t, att_l, out_l, exp_l, shr_l,
    bias_t, bias_l, off_t, off_l, vec_t, vec_l, lengths,
    text_out, lay_out, text_back, lay_back, sm_out,
    zs_t, zs_l, zr_t, zr_l, gb_t, gb_l, r1_t, r1_l, r2_t, r2_l, ro_t, ro_l, p_keep,
    w_t, w_l, small, vecs, own_small, own_vec, key_bias, rows_t, rows_l, x_fm, qkv_t, qkv_l, probs,
    ctx_t, ctx_l, xh1, n1b, xh2, act, gp, stats, acc, exs, exr, tmpb, g_fm, dup, dqkv, cols,
    stg_t, stg_l, tv_t, tv_l, fv_t, fv_l, smsg, srec, ssum, szr,
    ag_recv, ag_own, ag_fwd, vec_sem, row_sem, ex_send, ex_recv, out_sem, stg_sem, p_sem,
    s1_send, s1_recv, s2_send, s2_recv, so_send, so_recv, z_send, z_recv, tv_sem, fv_sem, zo_sem,
    sm_send, sm_recv, sz_send, sz_recv, so_sem,
):
    c = lax.axis_index("section")
    d = lax.axis_index("dp")
    t = lax.axis_index("tensor")
    t1, t2 = flip(t, 1), flip(t, 2)
    t3 = flip(t1, 2)
    xb = lax.rem(t, 2)
    zp = lax.rem(d, 2)
    tf = t1 + zp * (t2 - t1)
    td = t2 + zp * (t1 - t2)
    dz = flip(d, 1)
    tw = text_in.shape[2]
    lw = lay_in.shape[1]
    width = tw + lw
    tokens = x_fm.shape[2]
    half = tokens // 2
    quarter = tokens // 4
    hid_t, hid_l = exp_t.shape[1], exp_l.shape[1]
    hs, ls = out_t.shape[0], out_l.shape[0]
    heads = hs // HEAD
    blocks = tokens // LANES
    th, lh = tw // 2, lw // 2
    streams = ((0, tw), (tw, lw))
    z_peers = [lax.rem(d + r, dp) for r in range(1, dp)] if z_inside else [dz]

    def remote(src, dst, send, recv, device):
        return pltpu.make_async_remote_copy(
            src_ref=src, dst_ref=dst, send_sem=send, recv_sem=recv, device_id=device, device_id_type=MESH
        )

    def local_copy(src, dst, sem):
        return pltpu.make_async_copy(src, dst, sem)

    def landed(ref, sem):
        pltpu.make_async_copy(ref, ref, sem).wait()

    def start(copies):
        for copy in copies:
            copy.start()

    def wait(copies):
        for copy in copies:
            copy.wait()

    own_vec[...] = jnp.zeros(own_vec.shape, f32)
    own_vec[0:1, 0:hid_t] = off_t[...].astype(f32)
    own_vec[0:1, hid_t : hid_t + hid_l] = off_l[...].astype(f32)
    own_vec[1:2, 0:hs] = bias_t[0:1].astype(f32)
    own_vec[1:2, 2 * hs : 3 * hs] = bias_t[1:2].astype(f32)
    own_vec[1:2, 3 * hs : 3 * hs + ls] = bias_l[0:1].astype(f32)
    own_vec[1:2, 3 * hs + 2 * ls : 3 * hs + 3 * ls] = bias_l[1:2].astype(f32)
    own_small[...] = own_vec[...].astype(bf16)
    own_vec[0:6, 0:tw] = vec_t[...].astype(f32)
    own_vec[0:6, tw:width] = vec_l[...].astype(f32)

    barrier = pltpu.get_barrier_semaphore()
    peers = [(1 - c, d, t)] + [(k, d, other) for other in (t1, t2, t3) for k in range(2)] + [(c, z, t) for z in z_peers]
    for peer in peers:
        pl.semaphore_signal(barrier, inc=1, device_id=peer, device_id_type=MESH)
    pl.semaphore_wait(barrier, len(peers))
    other = (1 - c, d, t)

    def row_copies(text, lay, text_to, lay_to, base):
        mine, theirs = xb * half, (1 - xb) * half
        part = c * quarter
        own = [
            local_copy(text.at[xb], text_to.at[at(mine, half)], row_sem.at[base, 0]),
            local_copy(lay.at[xb], lay_to.at[:, lanes_at(mine, half)], row_sem.at[base + 1, 0]),
        ]
        away = [
            remote(
                text.at[1 - xb, at(part, quarter)], text_to.at[at(mine + part, quarter)],
                row_sem.at[base, 1], row_sem.at[base, 2], (c, d, t1),
            ),
            remote(
                lay.at[1 - xb, :, lanes_at(part, quarter)], lay_to.at[:, lanes_at(mine + part, quarter)],
                row_sem.at[base + 1, 1], row_sem.at[base + 1, 2], (c, d, t1),
            ),
        ]
        text_part = text_to.at[at(theirs + part, quarter)]
        lay_part = lay_to.at[:, lanes_at(theirs + part, quarter)]
        across = [
            remote(text_part, text_part, row_sem.at[base, 3], row_sem.at[base, 4], other),
            remote(lay_part, lay_part, row_sem.at[base + 1, 3], row_sem.at[base + 1, 4], other),
        ]
        return own, away, across

    cot_t = fv_t.at[0, pl.ds(0, tokens)]
    in_rows = row_copies(text_in, lay_in, rows_t, x_fm.at[0, pl.ds(tw, lw)], 0)
    cot_rows = row_copies(text_cot, lay_cot, cot_t, g_fm.at[pl.ds(tw, lw)], 2)

    def rows_begin(copies):
        own, away, across = copies
        start(away + own)

    def rows_cross(copies):
        own, away, across = copies
        wait(away)
        start(across)

    def rows_arrive(copies):
        own, away, across = copies
        wait(own + across)

    rows_begin(in_rows)

    text_sources = [att_t.at[pl.ds(j * hs, hs)] for j in range(3)] + [out_t]
    text_sources += [exp_t.at[pl.ds(j * hs, hs)] for j in range(4)] + [shr_t.at[pl.ds(j * hs, hs)] for j in range(4)]
    lay_sources = {12: att_l, 13: out_l, 14: exp_l, 15: shr_l}
    lay_places = {12: (0, 0, 3 * ls), 13: (0, 3 * ls, ls), 14: (1, 0, lw), 15: (2, 0, lw)}
    riders = {0: [12, 16], 3: [13], 4: [14], 8: [15]}

    def source(p):
        if p < STEPS:
            return text_sources[p]
        return lay_sources[p] if p < 16 else own_small

    def place(layer, slot, p):
        if p < STEPS:
            return w_t.at[layer, slot, p // 4, pl.ds((p % 4) * hs, hs)]
        if p < 16:
            which, first, size = lay_places[p]
            return w_l.at[layer, slot, which, pl.ds(first, size)]
        return small.at[layer, slot]

    def pieces(j):
        return [j] + riders.get(j, [])

    all_pieces = [p for j in range(STEPS) for p in pieces(j)]

    def own_first(p):
        return remote(
            source(p), place(c, 1 - zp, p), ag_own.at[p, 0], ag_recv.at[c, 1 - zp, p], (zp, d, tf)
        )

    def own_core(p):
        return remote(source(p), place(1, 0, p), ag_own.at[p, 1], ag_recv.at[1, 0, p], (0, d, t))

    def own_local(p):
        return local_copy(source(p), place(0, 0, p), ag_recv.at[0, 0, p])

    def forwards(layer, p):
        return [
            remote(
                place(layer, 1 - zp, p), place(layer, 1, p),
                ag_fwd.at[layer, p, 0], ag_recv.at[layer, 1, p], (1, d, td),
            ),
            remote(
                place(layer, 1 - zp, p), place(layer, 1 - zp, p),
                ag_fwd.at[layer, p, 1], ag_recv.at[layer, 1 - zp, p], (zp, dz, t),
            ),
        ]

    def fw(layer, *steps):
        @pl.when(c == zp)
        def _():
            for j in steps:
                for p in pieces(j):
                    landed(place(layer, 1 - zp, p), ag_recv.at[layer, 1 - zp, p])
                    start(forwards(layer, p))

    def need(layer, *steps):
        for j in steps:
            for p in pieces(j):
                landed(place(layer, zp, p), ag_recv.at[layer, zp, p])

        @pl.when(c != zp)
        def _():
            for j in steps:
                for p in pieces(j):
                    landed(place(layer, 1 - zp, p), ag_recv.at[layer, 1 - zp, p])

    vec_copies = [
        local_copy(own_vec, vecs.at[c], vec_sem.at[0]),
        remote(own_vec, vecs.at[c], vec_sem.at[1], vec_sem.at[2], other),
    ]
    start(vec_copies)

    @pl.when(c == 0)
    def _():
        for p in all_pieces:
            start([own_first(p), own_local(p)])

    @pl.when(c == 1)
    def _():
        start([own_core(p) for p in all_pieces])

    def start_second_layer():
        @pl.when(c == 1)
        def _():
            start([own_first(p) for p in all_pieces])

    page_len = lengths[xb, lax.div(t, 2)]
    positions = lax.broadcasted_iota(jnp.int32, key_bias.shape, 0)
    key_bias[...] = jnp.where(positions < page_len, 0.0, masked_score).astype(f32)
    smsg[...] = jnp.zeros(smsg.shape, f32)
    ones = jnp.ones((8, tokens), bf16)
    wait(vec_copies)

    def load_columns(layer):
        for k in range(2):
            cols[k] = small[layer, k].astype(f32).T
        cols[2] = vecs[layer].T

    def column(k, first, size, lane):
        return cols[k, pl.ds(first, size), lane : lane + 1]

    def exchange_copy(n):
        return remote(exs, exr.at[n % 2], ex_send.at[n], ex_recv.at[n], other)

    def exchanged(n, first, size, lanes):
        return exs[pl.ds(first, size), lanes].astype(f32) + exr[n % 2, pl.ds(first, size), lanes].astype(f32)

    def project(layer, s):
        mixed = mm(w_t[layer, s, 0, 0 : 3 * hs], x_fm[layer, 0:tw], 1, 0)
        qkv_t[layer, s] = (mixed + cols[s, 0 : 3 * hs, 1:2]).astype(bf16)
        mixed = mm(w_l[layer, s, 0, 0 : 3 * ls], x_fm[layer, tw:width], 1, 0)
        qkv_l[layer, s] = (mixed + cols[s, 3 * hs : 3 * hs + 3 * ls, 1:2]).astype(bf16)

    def head_rows(layer, s, part, h):
        return (
            qkv_t[layer, s, at(part * hs + h * HEAD, HEAD)],
            qkv_l[layer, s, at(part * ls + h * LHEAD, LHEAD)],
        )

    def query(layer, s, h):
        text, lay = head_rows(layer, s, 0, h)
        return jnp.concatenate([text * HEAD**-0.5, lay * LHEAD**-0.5], axis=0).astype(bf16)

    def attend_forward(layer, i):
        s, h = lax.div(i, heads), lax.rem(i, heads)
        keys = jnp.concatenate(head_rows(layer, s, 1, h), axis=0)
        values = jnp.concatenate(head_rows(layer, s, 2, h), axis=0)
        scores = mm(keys, query(layer, s, h), 0, 0) + key_bias[:, 0:1]
        exponent = jnp.exp(scores - jnp.max(scores, axis=0, keepdims=True))
        low = (exponent * (1.0 / jnp.sum(exponent, axis=0, keepdims=True))).astype(bf16)
        probs[i] = low
        context = mm(values, low, 1, 0).astype(bf16)
        ctx_t[layer, s, at(h * HEAD, HEAD)] = context[0:HEAD]
        ctx_l[layer, s, at(h * LHEAD, LHEAD)] = context[HEAD:]

    def attention_partial(layer):
        exs[0:tw] = (
            mm(w_t[layer, 0, 0, 3 * hs : 4 * hs], ctx_t[layer, 0], 0, 0)
            + mm(w_t[layer, 1, 0, 3 * hs : 4 * hs], ctx_t[layer, 1], 0, 0)
        ).astype(bf16)
        exs[tw:width] = (
            mm(w_l[layer, 0, 0, 3 * ls : 4 * ls], ctx_l[layer, 0], 0, 0)
            + mm(w_l[layer, 1, 0, 3 * ls : 4 * ls], ctx_l[layer, 1], 0, 0)
        ).astype(bf16)

    def normalize(hidden):
        center = hidden - jnp.mean(hidden, axis=0, keepdims=True)
        scale = lax.rsqrt(jnp.mean(center * center, axis=0, keepdims=True) + norm_epsilon)
        return center * scale, scale

    def norm_forward(layer, n, which, base, hat_ref, finish):
        def block(b):
            lanes = lanes_at(b * LANES, LANES)
            for k, (first, size) in enumerate(streams):
                hidden = base(first, size, lanes) + exchanged(n, first, size, lanes)
                hat, scale = normalize(hidden + column(2, first, size, 3 * which))
                hat_ref[layer, pl.ds(first, size), lanes] = hat.astype(bf16)
                row = 2 * which + k
                stats[layer, row : row + 1, lanes] = scale
                result = hat * column(2, first, size, 3 * which + 1) + column(2, first, size, 3 * which + 2)
                finish(first, size, lanes, result)

        loop(0, blocks, block)

    def first_norm(layer, n):
        def finish(first, size, lanes, result):
            acc[pl.ds(first, size), lanes] = result
            n1b[layer, pl.ds(first, size), lanes] = result.astype(bf16)

        norm_forward(
            layer, n, 0, lambda s, z, lanes: x_fm[layer, pl.ds(s, z), lanes].astype(f32), xh1, finish
        )

    def second_norm(layer, n, dest):
        def finish(first, size, lanes, result):
            dest[pl.ds(first, size), lanes] = result.astype(bf16)

        norm_forward(layer, n, 1, lambda s, z, lanes: acc[pl.ds(s, z), lanes], xh2, finish)

    def gelu_pair(raised):
        cdf = 0.5 * (1.0 + lax.erf(raised * math.sqrt(0.5)))
        slope = cdf + raised * (jnp.exp(-0.5 * raised * raised) * (1.0 / math.sqrt(2.0 * math.pi)))
        return (raised * cdf).astype(bf16), slope.astype(bf16)

    hb = 256
    per_slot = hid_t // hb

    def expand_block(layer, i):
        s, b = lax.div(i, per_slot), lax.rem(i, per_slot)
        rows = lanes_at(b * hb, hb)
        raised = mm(w_t[layer, s, 1, :, rows], n1b[layer, 0:tw], 0, 0) + cols[s, rows, 0:1]
        act[layer, s, rows], gp[layer, s, rows] = gelu_pair(raised)

    def expand_lay(layer, s):
        raised = mm(w_l[layer, s, 1], n1b[layer, tw:width], 0, 0) + cols[s, hid_t : hid_t + hid_l, 0:1]
        act[layer, s, hid_t:], gp[layer, s, hid_t:] = gelu_pair(raised)

    def shrink_partial(layer):
        exs[0:tw] = (
            mm(w_t[layer, 0, 2], act[layer, 0, 0:hid_t], 1, 0) + mm(w_t[layer, 1, 2], act[layer, 1, 0:hid_t], 1, 0)
        ).astype(bf16)
        exs[tw:width] = (
            mm(w_l[layer, 0, 2], act[layer, 0, hid_t:], 1, 0) + mm(w_l[layer, 1, 2], act[layer, 1, hid_t:], 1, 0)
        ).astype(bf16)

    def rows_out(base, text_to, lay_to):
        mine, theirs = xb * half, (1 - xb) * half
        pairs = (
            (rows_t.at[at(mine, half)], rows_t.at[at(theirs, half)], text_to),
            (rows_l.at[:, lanes_at(mine, half)], rows_l.at[:, lanes_at(theirs, half)], lay_to),
        )
        copies = []
        for k, (own, away, dest) in enumerate(pairs):
            copies.append(local_copy(own, dest.at[xb], out_sem.at[base + k, 0]))
            copies.append(
                remote(away, dest.at[xb], out_sem.at[base + k, 1], out_sem.at[base + k, 2], (c, d, t1))
            )
        return copies

    def send_rows(layer, base, dest_pair, value):
        @pl.when(c == layer)
        def _():
            rows_t[...] = value[0:tw].T
            rows_l[...] = value[tw:width]
            start(rows_out(base, *dest_pair))

    def finish_rows(layer, base, dest_pair):
        @pl.when(c == layer)
        def _():
            wait(rows_out(base, *dest_pair))

    out_pair, back_pair = (text_out, lay_out), (text_back, lay_back)
    rows_cross(in_rows)
    fw(0, 0)
    rows_arrive(in_rows)
    x_fm[0, 0:tw] = rows_t[...].T
    fw(0, 1)
    need(0, 0)
    load_columns(0)

    p_store = local_copy(probs, p_keep, p_sem.at[0])
    p_load = local_copy(p_keep, probs, p_sem.at[1])

    for layer in range(2):
        last = layer == 1
        fw(layer, 2)
        need(layer, 1)
        fw(layer, 3)
        need(layer, 2)
        project(layer, 0)
        fw(layer, 4)
        project(layer, 1)
        if last:
            p_store.wait()
        fw(layer, 5)
        head = functools.partial(attend_forward, layer)
        loop(0, 2, head)
        fw(layer, 6)
        loop(2, 4, head)
        fw(layer, 7)
        loop(4, 6, head)
        if last:
            rows_cross(cot_rows)
        else:
            p_store.start()
            rows_begin(cot_rows)
        need(layer, 3)
        attention_partial(layer)
        swap = exchange_copy(2 * layer)
        swap.start()
        fw(layer, 8)
        swap.wait()
        first_norm(layer, 2 * layer)
        fw(layer, 9)
        need(layer, 4, 5, 6, 7)
        expand = functools.partial(expand_block, layer)
        loop(0, per_slot, expand)
        fw(layer, 10)
        if not last:
            need(layer, 8, 9)
            start_second_layer()
        loop(per_slot, 2 * per_slot, expand)
        fw(layer, 11)
        loop(0, 2, functools.partial(expand_lay, layer))
        if last:
            need(layer, 8, 9, 10, 11)
            rows_arrive(cot_rows)
        else:
            need(layer, 10)
            fw(1, 0)
            need(layer, 11)
        shrink_partial(layer)
        swap = exchange_copy(2 * layer + 1)
        swap.start()
        if not last:
            fw(1, 1)
        else:
            g_fm[0:tw] = cot_t[...].T
        swap.wait()
        if not last:
            second_norm(0, 1, x_fm.at[1])
            send_rows(0, 0, out_pair, x_fm.at[1])
            need(1, 0)
            load_columns(1)
        else:
            second_norm(1, 3, tmpb)
            send_rows(1, 0, out_pair, tmpb)

    def grad_store(layer, chunk, s):
        return [
            local_copy(stg_t.at[s], gb_t.at[layer, chunk, s], stg_sem.at[s, 0]),
            local_copy(stg_l.at[s], gb_l.at[layer, chunk, s], stg_sem.at[s, 1]),
        ]

    def store_grad(layer, chunk, s, text_value, lay_value):
        stg_t[s] = text_value
        stg_l[s] = lay_value
        start(grad_store(layer, chunk, s))

    def first_sends(layer, chunk):
        zero, one = [], []
        for k, (grad, come, total, size) in enumerate(((gb_t, r1_t, r2_t, th), (gb_l, r1_l, r2_l, lh))):
            h1, h2 = pl.ds(0, size), pl.ds(size, size)
            zero.append(
                remote(
                    grad.at[layer, chunk, 1, h1], total.at[chunk, 0, h1],
                    s1_send.at[layer, chunk, k, 0], s2_recv.at[chunk, 0, 0, k], (layer, d, t1),
                )
            )
            one.append(
                remote(
                    grad.at[layer, chunk, 1, h1], come.at[layer, chunk],
                    s1_send.at[layer, chunk, k, 0], s1_recv.at[layer, chunk, k], (1, d, t1),
                )
            )
            one.append(
                remote(
                    grad.at[layer, chunk, 1, h2], come.at[layer, chunk],
                    s1_send.at[layer, chunk, k, 1], s1_recv.at[layer, chunk, k], (0, d, t2),
                )
            )
            one.append(
                remote(
                    grad.at[layer, chunk, 0, h2], total.at[chunk, 1, h2],
                    s1_send.at[layer, chunk, k, 2], s2_recv.at[chunk, 1, 1, k], (layer, d, t2),
                )
            )
        if layer == 1:
            for k, (grad, arrive) in enumerate(((gb_t, ro_t), (gb_l, ro_l))):
                zero.append(
                    remote(
                        grad.at[1, chunk, 0], arrive.at[chunk], so_send.at[chunk, k], so_recv.at[chunk, k], other
                    )
                )
        return zero, one

    def grads_go(layer, chunk):
        for s in range(2):
            wait(grad_store(layer, chunk, s))
        zero, one = first_sends(layer, chunk)

        @pl.when(c == 0)
        def _():
            start(zero)

        @pl.when(c == 1)
        def _():
            start(one)

    tx = t1 + c * (t2 - t1)
    transit_groups = ((gb_t, r1_t, r2_t, th, tv_t), (gb_l, r1_l, r2_l, lh, tv_l))

    def mine(grad, layer, chunk, size):
        return grad.at[layer, chunk, 1 - c, at((1 - c) * size, size)]

    def second_sends(layer, chunk):
        return [
            remote(
                mine(grad, layer, chunk, size), total.at[chunk, c, at((1 - c) * size, size)],
                s2_send.at[layer, chunk, k], s2_recv.at[chunk, c, 1 - c, k], (layer, d, tx),
            )
            for k, (grad, come, total, size, tv) in enumerate(transit_groups)
        ]

    def transit_loads(layer, chunk):
        copies = []
        for k, (grad, come, total, size, tv) in enumerate(transit_groups):
            copies.append(local_copy(mine(grad, layer, chunk, size), tv.at[0], tv_sem.at[k, 0]))
            copies.append(local_copy(come.at[layer, chunk], tv.at[1], tv_sem.at[k, 1]))
        return copies

    def transit_stores(layer, chunk):
        return [
            local_copy(tv.at[0], mine(grad, layer, chunk, size), tv_sem.at[k, 2])
            for k, (grad, come, total, size, tv) in enumerate(transit_groups)
        ]

    def transit_load(layer, chunk):
        for k, (grad, come, total, size, tv) in enumerate(transit_groups):
            landed(come.at[layer, chunk], s1_recv.at[layer, chunk, k])
        start(transit_loads(layer, chunk))

    def transit_add(layer, chunk):
        wait(transit_loads(layer, chunk))
        for tv in (tv_t, tv_l):
            tv[0] = (tv[0].astype(f32) + tv[1].astype(f32)).astype(bf16)
        start(transit_stores(layer, chunk))

    def transit_send(layer, chunk):
        wait(transit_stores(layer, chunk))
        start(second_sends(layer, chunk))

    def transit(layer, chunk):
        transit_load(layer, chunk)
        transit_add(layer, chunk)
        transit_send(layer, chunk)

    parts = dp if z_inside else 2
    final_groups = ((gb_t, ro_t, r2_t, fv_t, zs_t, zr_t), (gb_l, ro_l, r2_l, fv_l, zs_l, zr_l))

    def part_sends(chunk, r):
        copies = []
        for k, (grad, arrive, total, fv, zs, zr) in enumerate(final_groups):
            size = fv.shape[1] // parts
            if not z_inside:
                rows = pl.ds(r * size, size)
                copies.append(local_copy(fv.at[0, rows], zs.at[chunk, rows], zo_sem.at[k, r]))
                continue
            j = lax.rem(d + r, dp)
            piece = fv.at[0, at(j * size, size)]
            if r == 0:
                copies.append(local_copy(piece, zr.at[chunk, 0], zo_sem.at[k, 0]))
            else:
                copies.append(
                    remote(piece, zr.at[chunk, r], z_send.at[chunk, k, r], z_recv.at[chunk, k, r], (c, j, t))
                )
        return copies

    def part_rows(r, size):
        if not z_inside:
            return pl.ds(r * size, size)
        return at(lax.rem(d + r, dp) * size, size)

    def part_loads(layer, chunk, r):
        copies = []
        for k, (grad, arrive, total, fv, zs, zr) in enumerate(final_groups):
            rows = part_rows(r, fv.shape[1] // parts)
            own = arrive.at[chunk, rows] if layer == 1 else grad.at[layer, chunk, 0, rows]
            for i, src in enumerate((own, total.at[chunk, 0, rows], total.at[chunk, 1, rows])):
                copies.append(local_copy(src, fv.at[i, rows], fv_sem.at[k, i, r]))
        return copies

    order = list(range(1, parts)) + [0]

    def sent(copies, inside):
        for copy in copies:
            if inside:
                copy.wait_send()
            else:
                copy.wait()

    def final(layer, chunk, before):
        @pl.when(c == layer)
        def _():
            if before is not None:
                for r in order:
                    sent(part_sends(before, r), z_inside and r > 0)
            for k, (grad, arrive, total, fv, zs, zr) in enumerate(final_groups):
                size = (th, lh)[k]
                for way in range(2):
                    for h in range(2):
                        landed(total.at[chunk, way, pl.ds(h * size, size)], s2_recv.at[chunk, way, h, k])
                if layer == 1:
                    landed(arrive.at[chunk], so_recv.at[chunk, k])
            for r in order:
                start(part_loads(layer, chunk, r))
            for r in order:
                wait(part_loads(layer, chunk, r))
                for grad, arrive, total, fv, zs, zr in final_groups:
                    rows = part_rows(r, fv.shape[1] // parts)
                    summed = fv[0, rows].astype(f32) + fv[1, rows].astype(f32) + fv[2, rows].astype(f32)
                    fv[0, rows] = summed.astype(bf16)
                start(part_sends(chunk, r))

    def small_sends(layer):
        zero = [remote(smsg.at[layer, 1], srec.at[0], sm_send.at[layer, 0], sm_recv.at[0], (layer, d, t1))]
        if layer == 1:
            zero.append(remote(smsg.at[1, 0], srec.at[3], sm_send.at[1, 1], sm_recv.at[3], other))
        one = [
            remote(smsg.at[layer, 0], srec.at[1], sm_send.at[layer, 0], sm_recv.at[1], (layer, d, t2)),
            remote(smsg.at[layer, 1], srec.at[2], sm_send.at[layer, 1], sm_recv.at[2], (layer, d, t3)),
        ]
        return zero, one

    def small_go(layer):
        zero, one = small_sends(layer)

        @pl.when(c == 0)
        def _():
            start(zero)

        @pl.when(c == 1)
        def _():
            start(one)

    def small_z():
        if not z_inside:
            return []
        return [
            remote(ssum, szr.at[r - 1], sz_send.at[r - 1], sz_recv.at[r - 1], (c, lax.rem(d + r, dp), t))
            for r in range(1, dp)
        ]

    def small_total(layer):
        @pl.when(c == layer)
        def _():
            for i in range(3):
                landed(srec.at[i], sm_recv.at[i])
            if layer == 1:
                landed(srec.at[3], sm_recv.at[3])
                own = srec[3]
            else:
                own = smsg[0, 0]
            ssum[...] = own + srec[0] + srec[1] + srec[2]
            start(small_z())

    def row_sums(ref):
        return mm(ones, ref[...], 1, 1)[0:1]

    def vector_sum(layer, row, value):
        for s in range(2):
            smsg[layer, s, 8 + row : 9 + row, 0:width] = value

    def norm_backward(layer, which, hat_ref, incoming):
        def block(b):
            lanes = lanes_at(b * LANES, LANES)
            for k, (first, size) in enumerate(streams):
                grad = incoming(first, size, lanes)
                hat = hat_ref[layer, pl.ds(first, size), lanes].astype(f32)
                row = 2 * which + k
                scale = stats[layer, row : row + 1, lanes]
                gained = grad * column(2, first, size, 3 * which + 1)
                mean_grad = jnp.mean(gained, axis=0, keepdims=True)
                mean_both = jnp.mean(gained * hat, axis=0, keepdims=True)
                result = scale * (gained - mean_grad - hat * mean_both)
                acc[pl.ds(first, size), lanes] = result
                tmpb[pl.ds(first, size), lanes] = result.astype(bf16)
                exs[pl.ds(first, size), lanes] = (grad * hat).astype(bf16)
                g_fm[pl.ds(first, size), lanes] = grad.astype(bf16)

        loop(0, blocks, block)
        vector_sum(layer, 3 * which + 1, row_sums(exs))
        vector_sum(layer, 3 * which + 2, row_sums(g_fm))
        vector_sum(layer, 3 * which, row_sums(tmpb))

    def ffn_backward(layer):
        def text_block(i):
            s, b = lax.div(i, per_slot), lax.rem(i, per_slot)
            rows = lanes_at(b * hb, hb)
            back = mm(w_t[layer, s, 2, :, rows], tmpb[0:tw], 0, 0)
            dup[s, rows] = (back * gp[layer, s, rows].astype(f32)).astype(bf16)

        loop(0, 2 * per_slot, text_block)

        def lay_block(s):
            back = mm(w_l[layer, s, 2], tmpb[tw:width], 0, 0)
            dup[s, hid_t:] = (back * gp[layer, s, hid_t:].astype(f32)).astype(bf16)

        loop(0, 2, lay_block)

    def shrink_grads(layer, s):
        store_grad(
            layer, 2, s,
            mm(tmpb[0:tw], act[layer, s, 0:hid_t], 1, 1).astype(bf16),
            mm(tmpb[tw:width], act[layer, s, hid_t:], 1, 1).astype(bf16),
        )

    def expand_grads(layer, s):
        store_grad(
            layer, 1, s,
            mm(n1b[layer, 0:tw], dup[s, 0:hid_t], 1, 1).astype(bf16),
            mm(n1b[layer, tw:width], dup[s, hid_t:], 1, 1).astype(bf16),
        )

    def expand_partial(layer):
        exs[0:tw] = (
            mm(w_t[layer, 0, 1], dup[0, 0:hid_t], 1, 0) + mm(w_t[layer, 1, 1], dup[1, 0:hid_t], 1, 0)
        ).astype(bf16)
        exs[tw:width] = (
            mm(w_l[layer, 0, 1], dup[0, hid_t:], 1, 0) + mm(w_l[layer, 1, 1], dup[1, hid_t:], 1, 0)
        ).astype(bf16)

    def context_grads(layer, s):
        dup[s, 0:hs] = mm(w_t[layer, s, 0, 3 * hs : 4 * hs], tmpb[0:tw], 1, 0).astype(bf16)
        dup[s, hs : hs + ls] = mm(w_l[layer, s, 0, 3 * ls : 4 * ls], tmpb[tw:width], 1, 0).astype(bf16)

    def attend_backward(layer, i):
        s, h = lax.div(i, heads), lax.rem(i, heads)
        queries = query(layer, s, h)
        key_text, key_lay = head_rows(layer, s, 1, h)
        keys = jnp.concatenate([key_text * HEAD**-0.5, key_lay * LHEAD**-0.5], axis=0).astype(bf16)
        values = jnp.concatenate(head_rows(layer, s, 2, h), axis=0)
        grads = jnp.concatenate([dup[s, at(h * HEAD, HEAD)], dup[s, at(hs + h * LHEAD, LHEAD)]], axis=0)
        low = probs[i]
        prob = low.astype(f32)
        dprob = mm(values, grads, 0, 0)
        inner = jnp.sum(dprob * prob, axis=0, keepdims=True)
        dscore = (prob * (dprob - inner)).astype(bf16)
        results = (mm(keys, dscore, 1, 0), mm(queries, dscore, 1, 1), mm(grads, low, 1, 1))
        for part, result in enumerate(results):
            result = result.astype(bf16)
            dqkv[s, at(part * hs + h * HEAD, HEAD)] = result[0:HEAD]
            dqkv[s, at(3 * hs + part * ls + h * LHEAD, LHEAD)] = result[HEAD:]

    def attend_grads(layer, s):
        text = jnp.concatenate(
            [mm(x_fm[layer, 0:tw], dqkv[s, 0 : 3 * hs], 1, 1), mm(tmpb[0:tw], ctx_t[layer, s], 1, 1)], axis=1
        )
        lay = jnp.concatenate(
            [mm(x_fm[layer, tw:width], dqkv[s, 3 * hs :], 1, 1), mm(tmpb[tw:width], ctx_l[layer, s], 1, 1)], axis=1
        )
        store_grad(layer, 0, s, text.astype(bf16), lay.astype(bf16))

    def attend_partial(layer):
        exs[0:tw] = (
            mm(w_t[layer, 0, 0, 0 : 3 * hs], dqkv[0, 0 : 3 * hs], 0, 0)
            + mm(w_t[layer, 1, 0, 0 : 3 * hs], dqkv[1, 0 : 3 * hs], 0, 0)
        ).astype(bf16)
        exs[tw:width] = (
            mm(w_l[layer, 0, 0, 0 : 3 * ls], dqkv[0, 3 * hs :], 0, 0)
            + mm(w_l[layer, 1, 0, 0 : 3 * ls], dqkv[1, 3 * hs :], 0, 0)
        ).astype(bf16)

    def small_sums(layer, s, row, ref, size):
        smsg[layer, s, row : row + 1, 0:size] = mm(ones, ref[s], 1, 1)[0:1]

    def first_grad(n, first, size, lanes):
        return acc[pl.ds(first, size), lanes] + exchanged(n, first, size, lanes)

    for layer in (1, 0):
        last = layer == 0
        n = 4 + 2 * (1 - layer)
        if last:
            load_columns(0)
            transit_load(1, 1)
        norm_backward(layer, 1, xh2, lambda s, z, lanes: g_fm[pl.ds(s, z), lanes].astype(f32))
        if last:
            transit_add(1, 1)
        for s in range(2):
            shrink_grads(layer, s)
        if last:
            transit_send(1, 1)
        ffn_backward(layer)
        grads_go(layer, 2)
        for s in range(2):
            expand_grads(layer, s)
        expand_partial(layer)
        swap = exchange_copy(n)
        swap.start()
        for s in range(2):
            small_sums(layer, s, 0, dup, hid_t + hid_l)
        grads_go(layer, 1)
        if last:
            transit_load(1, 0)
        swap.wait()
        norm_backward(layer, 0, xh1, functools.partial(first_grad, n))
        if last:
            transit_add(1, 0)
            p_load.wait()
        for s in range(2):
            context_grads(layer, s)
        if last:
            transit_send(1, 0)
        head = functools.partial(attend_backward, layer)
        loop(0, 3, head)
        transit_load(layer, 2)
        loop(3, 5, head)
        transit_add(layer, 2)
        loop(5, 6, head)
        if not last:
            p_load.start()
        for s in range(2):
            attend_grads(layer, s)
        transit_send(layer, 2)
        attend_partial(layer)
        swap = exchange_copy(n + 1)
        swap.start()
        for s in range(2):
            small_sums(layer, s, 1, dqkv, 3 * hs + 3 * ls)
        small_go(layer)
        grads_go(layer, 0)
        swap.wait()

        def finish(b):
            lanes = lanes_at(b * LANES, LANES)
            for first, size in streams:
                g_fm[pl.ds(first, size), lanes] = first_grad(n + 1, first, size, lanes).astype(bf16)

        loop(0, blocks, finish)
        finish_rows(layer, 0, out_pair)
        send_rows(layer, 2, back_pair, g_fm)

    transit(0, 1)
    small_total(1)
    final(1, 2, None)
    final(0, 2, None)
    transit(0, 0)
    small_total(0)
    final(1, 1, 2)
    final(0, 1, 2)
    final(1, 0, 1)
    final(0, 0, 1)

    for copy in small_z():
        copy.wait()
    if z_inside:
        for r in range(1, dp):
            ssum[...] = ssum[...] + szr[r - 1]
    sm_copy = local_copy(ssum, sm_out, so_sem.at[0])
    sm_copy.start()
    for layer in range(2):
        finish_rows(layer, 2, back_pair)

        @pl.when(c == layer)
        def _():
            for p in all_pieces:
                own_first(p).wait_send()
            if layer == 1:
                for p in all_pieces:
                    own_core(p).wait_send()

        @pl.when(c == zp)
        def _():
            for p in all_pieces:
                for copy in forwards(layer, p):
                    copy.wait_send()

        smalls = small_sends(layer)
        firsts = [first_sends(layer, chunk) for chunk in range(3)]
        for core in range(2):

            @pl.when(c == core)
            def _():
                for copy in smalls[core]:
                    copy.wait_send()
                for pair in firsts:
                    for copy in pair[core]:
                        copy.wait_send()

        for chunk in range(3):
            for copy in second_sends(layer, chunk):
                copy.wait_send()
    for r in order:
        sent(part_sends(0, r), z_inside and r > 0)
    if z_inside:
        for chunk in range(3):
            for r in range(1, dp):
                for copy in part_sends(chunk, r):
                    copy.wait_recv()
    sm_copy.wait()


def finishing(
    zr_t, zr_l, sums, rows_in_0, rows_in_1, rows_in_2, rows_in_3,
    rows_0, rows_1, rows_2, rows_3, att_t, out_t, exp_t, shr_t, att_l, out_l, exp_l, shr_l,
    bias_t, off_t, vec_t, bias_l, off_l, vec_l, sems,
):
    pairs = ((rows_in_0, rows_0), (rows_in_1, rows_1), (rows_in_2, rows_2), (rows_in_3, rows_3))
    copies = [pltpu.make_async_copy(src, dst, sems.at[i]) for i, (src, dst) in enumerate(pairs)]
    for copy in copies:
        copy.start()
    for zr, att, out, exp, shr in ((zr_t, att_t, out_t, exp_t, shr_t), (zr_l, att_l, out_l, exp_l, shr_l)):
        totals = []
        for chunk in range(3):
            total = zr[chunk, 0].astype(f32)
            for r in range(1, zr.shape[1]):
                total = total + zr[chunk, r].astype(f32)
            totals.append(total)
        size = out.shape[1]
        for j in range(3):
            att[j] = totals[0][:, j * size : (j + 1) * size]
        out[...] = totals[0][:, 3 * size : 4 * size]
        exp[...] = totals[1]
        shr[...] = totals[2]
    hs, ls = bias_t.shape[1], bias_l.shape[1]
    ft, fl = off_t.shape[1], off_l.shape[1]
    tw, lw = vec_t.shape[2], vec_l.shape[2]
    off_t[...] = sums[0:1, 0:ft]
    off_l[...] = sums[0:1, ft : ft + fl]
    bias_t[0:1] = sums[1:2, 0:hs]
    bias_t[1:2] = sums[1:2, 2 * hs : 3 * hs]
    bias_l[0:1] = sums[1:2, 3 * hs : 3 * hs + ls]
    bias_l[1:2] = sums[1:2, 3 * hs + 2 * ls : 3 * hs + 3 * ls]
    for row in range(6):
        vec_t[row] = sums[8 + row : 9 + row, 0:tw]
        vec_l[row] = sums[8 + row : 9 + row, tw : tw + lw]
    for copy in copies:
        copy.wait()


def local(
    dp,
    text_in,
    layout_in,
    text_cot,
    layout_cot,
    lengths,
    text_attend,
    text_biases,
    text_output,
    text_expand,
    text_offset,
    text_shrink,
    text_vectors,
    layout_attend,
    layout_biases,
    layout_output,
    layout_expand,
    layout_offset,
    layout_shrink,
    layout_vectors,
):
    rows, tw = text_in.shape[1:]
    lw = layout_in.shape[2]
    width, tokens = tw + lw, 2 * rows
    hs, ls = text_output.shape[2], layout_output.shape[2]
    ft, fl = text_expand.shape[2], layout_expand.shape[2]
    zt, zl = tw // dp, lw // dp
    z_inside = dp <= 4 and zt % 16 == 0 and zl % 16 == 0

    def shape(dims, dtype=bf16):
        return jax.ShapeDtypeStruct(dims, dtype)

    def attend_rows(attend):
        return attend[0].transpose(1, 2, 0).reshape(-1, attend.shape[1])

    hbm = pl.BlockSpec(memory_space=pltpu.HBM)
    vmem = pl.BlockSpec(memory_space=pltpu.VMEM)
    heads = hs // HEAD
    row_shapes = [shape((2, rows, tw)), shape((2, lw, rows)), shape((2, rows, tw)), shape((2, lw, rows))]
    out_shape = row_shapes + [
        shape((16, SMALL), f32),
        shape((3, tw, tw)), shape((3, lw, lw)),
        shape((3, dp, zt, tw)), shape((3, dp, zl, lw)),
        shape((2, 3, 2, tw, tw)), shape((2, 3, 2, lw, lw)),
        shape((2, 3, tw // 2, tw)), shape((2, 3, lw // 2, lw)),
        shape((3, 2, tw, tw)), shape((3, 2, lw, lw)),
        shape((3, tw, tw)), shape((3, lw, lw)),
        shape((2 * heads, tokens, tokens)),
    ]
    dma = pltpu.SemaphoreType.DMA
    scratch = [
        pltpu.VMEM((2, 2, 3, tw, tw), bf16),
        pltpu.VMEM((2, 2, 3, lw, lw), bf16),
        pltpu.VMEM((2, 2, 16, SMALL), bf16),
        pltpu.VMEM((2, 16, SMALL), f32),
        pltpu.VMEM((16, SMALL), bf16),
        pltpu.VMEM((16, SMALL), f32),
        pltpu.VMEM((tokens, LANES), f32),
        pltpu.VMEM((tokens, tw), bf16),
        pltpu.VMEM((lw, tokens), bf16),
        pltpu.VMEM((2, width, tokens), bf16),
        pltpu.VMEM((2, 2, 3 * hs, tokens), bf16),
        pltpu.VMEM((2, 2, 3 * ls, tokens), bf16),
        pltpu.VMEM((2 * heads, tokens, tokens), bf16),
        pltpu.VMEM((2, 2, hs, tokens), bf16),
        pltpu.VMEM((2, 2, ls, tokens), bf16),
        pltpu.VMEM((2, width, tokens), bf16),
        pltpu.VMEM((2, width, tokens), bf16),
        pltpu.VMEM((2, width, tokens), bf16),
        pltpu.VMEM((2, 2, ft + fl, tokens), bf16),
        pltpu.VMEM((2, 2, ft + fl, tokens), bf16),
        pltpu.VMEM((2, 8, tokens), f32),
        pltpu.VMEM((width, tokens), f32),
        pltpu.VMEM((width, tokens), bf16),
        pltpu.VMEM((2, width, tokens), bf16),
        pltpu.VMEM((width, tokens), bf16),
        pltpu.VMEM((width, tokens), bf16),
        pltpu.VMEM((2, ft + fl, tokens), bf16),
        pltpu.VMEM((2, 3 * hs + 3 * ls, tokens), bf16),
        pltpu.VMEM((3, SMALL, 16), f32),
        pltpu.VMEM((2, tw, tw), bf16),
        pltpu.VMEM((2, lw, lw), bf16),
        pltpu.VMEM((2, tw // 2, tw), bf16),
        pltpu.VMEM((2, lw // 2, lw), bf16),
        pltpu.VMEM((3, tw, tw), bf16),
        pltpu.VMEM((3, lw, lw), bf16),
        pltpu.VMEM((2, 2, 16, SMALL), f32),
        pltpu.VMEM((4, 16, SMALL), f32),
        pltpu.VMEM((16, SMALL), f32),
        pltpu.VMEM((3, 16, SMALL), f32),
        dma((2, 2, 17)), dma((17, 2)), dma((2, 17, 2)), dma((3,)), dma((4, 5)), dma((8,)), dma((8,)),
        dma((4, 3)), dma((2, 2)), dma((2,)),
        dma((2, 3, 2, 3)), dma((2, 3, 2)), dma((2, 3, 2)), dma((3, 2, 2, 2)), dma((3, 2)), dma((3, 2)),
        dma((3, 2, 4)), dma((3, 2, 4)), dma((2, 3)), dma((2, 3, 4)), dma((2, 4)),
        dma((2, 2)), dma((4,)), dma((3,)), dma((3,)), dma((1,)),
    ]
    results = pl.pallas_call(
        functools.partial(kernel, dp, z_inside),
        out_shape=out_shape,
        in_specs=[hbm] * 12 + [vmem] * 6 + [pl.BlockSpec(memory_space=pltpu.SMEM)],
        out_specs=[hbm] * len(out_shape),
        scratch_shapes=scratch,
        compiler_params=pltpu.CompilerParams(
            collective_id=0, has_side_effects=True, vmem_limit_bytes=63 * 1024 * 1024
        ),
    )(
        text_in, layout_in.transpose(0, 2, 1), text_cot, layout_cot.transpose(0, 2, 1),
        attend_rows(text_attend), text_output[0].T, text_expand[0], text_shrink[0],
        attend_rows(layout_attend), layout_output[0].T, layout_expand[0], layout_shrink[0],
        text_biases[0], layout_biases[0], text_offset, layout_offset, text_vectors[0], layout_vectors[0], lengths,
    )
    row_results, sums = results[:4], results[4]
    if z_inside:
        parts_t, parts_l = results[7], results[8]
    else:
        parts_t = lax.psum_scatter(results[5], "dp", scatter_dimension=1, tiled=True)[:, None]
        parts_l = lax.psum_scatter(results[6], "dp", scatter_dimension=1, tiled=True)[:, None]
        sums = lax.psum(sums, "dp")
    final_shapes = row_shapes + [
        shape((3, zt, hs), f32), shape((zt, hs), f32), shape((zt, ft), f32), shape((zt, ft), f32),
        shape((3, zl, ls), f32), shape((zl, ls), f32), shape((zl, fl), f32), shape((zl, fl), f32),
        shape((2, hs), f32), shape((1, ft), f32), shape((6, 1, tw), f32),
        shape((2, ls), f32), shape((1, fl), f32), shape((6, 1, lw), f32),
    ]
    (
        text_out, lay_out, text_back, lay_back, att_t, out_t, exp_t, shr_t, att_l, out_l, exp_l, shr_l,
        bias_t, off_t, vec_t, bias_l, off_l, vec_l,
    ) = pl.pallas_call(
        finishing,
        out_shape=final_shapes,
        in_specs=[vmem] * 3 + [hbm] * 4,
        out_specs=[hbm] * 4 + [vmem] * 14,
        scratch_shapes=[dma((4,))],
        compiler_params=pltpu.CompilerParams(vmem_limit_bytes=32 * 1024 * 1024),
    )(parts_t, parts_l, sums, *row_results)
    return (
        text_out[None],
        lay_out.transpose(0, 2, 1)[None],
        text_back[None],
        lay_back.transpose(0, 2, 1)[None],
        att_t.transpose(1, 0, 2)[None],
        bias_t[None],
        out_t[None],
        exp_t[None],
        off_t,
        shr_t[None],
        vec_t.transpose(1, 0, 2),
        att_l.transpose(1, 0, 2)[None],
        bias_l[None],
        out_l[None],
        exp_l[None],
        off_l,
        shr_l[None],
        vec_l.transpose(1, 0, 2),
    )


def solution(mesh):
    return jax.shard_map(
        functools.partial(local, mesh.shape["dp"]),
        mesh=mesh,
        in_specs=(
            P(None, ("dp", "tensor"), None),
            P(None, ("dp", "tensor"), None),
            P(None, ("dp", "tensor"), None),
            P(None, ("dp", "tensor"), None),
            P(None, "dp"),
            P("section", None, None, "tensor"),
            P("section", None, "tensor"),
            P("section", None, "tensor"),
            P("section", None, "tensor"),
            P("section", "tensor"),
            P("section", None, "tensor"),
            P("section", None, None),
            P("section", None, None, "tensor"),
            P("section", None, "tensor"),
            P("section", None, "tensor"),
            P("section", None, "tensor"),
            P("section", "tensor"),
            P("section", None, "tensor"),
            P("section", None, None),
        ),
        out_specs=(
            P("section", None, ("dp", "tensor"), None),
            P("section", None, ("dp", "tensor"), None),
            P("section", None, ("dp", "tensor"), None),
            P("section", None, ("dp", "tensor"), None),
            P("section", "dp", None, "tensor"),
            P("section", None, "tensor"),
            P("section", "dp", "tensor"),
            P("section", "dp", "tensor"),
            P("section", "tensor"),
            P("section", "dp", "tensor"),
            P("section", None, None),
            P("section", "dp", None, "tensor"),
            P("section", None, "tensor"),
            P("section", "dp", "tensor"),
            P("section", "dp", "tensor"),
            P("section", "tensor"),
            P("section", "dp", "tensor"),
            P("section", None, None),
        ),
        check_vma=False,
    )
```

```python
import functools
import math

import jax
import jax.numpy as jnp
from jax import lax
from jax.experimental import pallas as pl
from jax.experimental.pallas import tpu as pltpu
from jax.sharding import PartitionSpec as P

HEAD = 64
LHEAD = 16
MESH = pl.DeviceIdType.MESH
bf16 = jnp.bfloat16
f32 = jnp.float32
norm_epsilon = 1e-05
masked_score = -1e30
LANES = 128
SMALL = 1024
STEPS = 12


def mm(left, right, left_axis, right_axis):
    return lax.dot_general(
        left, right, (((left_axis,), (right_axis,)), ((), ())), preferred_element_type=f32
    )


def flip(index, bit):
    return index + bit - 2 * bit * lax.rem(lax.div(index, bit), 2)


def loop(start, stop, body):
    lax.fori_loop(start, stop, lambda i, carry: (body(i), carry)[1], 0)


def at(start, size):
    return pl.ds(pl.multiple_of(start, 16), size)


def lanes_at(start, size):
    return pl.ds(pl.multiple_of(start, LANES), size)


def kernel(
    dp,
    z_inside,
    text_in, lay_in, text_cot, lay_cot, att_t, out_t, exp_t, shr_t, att_l, out_l, exp_l, shr_l,
    bias_t, bias_l, off_t, off_l, vec_t, vec_l, lengths,
    text_out, lay_out, text_back, lay_back, sm_out,
    zs_t, zs_l, zr_t, zr_l, gb_t, gb_l, rz_t, rz_l, r1_t, r1_l, r2_t, r2_l, ro_t, ro_l, p_keep,
    w_t, w_l, small, vecs, own_small, own_vec, key_bias, rows_t, rows_l, x_fm, qkv_t, qkv_l, probs,
    ctx_t, ctx_l, xh1, n1b, xh2, act, gp, stats, acc, exs, exr, tmpb, g_fm, dup, dqkv, cols,
    stg_t, stg_l, zv_t, zv_l, tv_t, tv_l, fv_t, fv_l, smsg, srec, ssum, szr,
    ag_recv, ag_own, ag_fwd, vec_sem, row_sem, ex_send, ex_recv, out_sem, stg_sem, p_sem,
    rz_send, rz_recv, s1_send, d_send, r1_recv, s2_send, s2_recv, so_send, so_recv, z_send, z_recv,
    zv_sem, tv_sem, fv_sem,
    sm_send, sm_recv, sz_send, sz_recv, so_sem,
):
    c = lax.axis_index("section")
    d = lax.axis_index("dp")
    t = lax.axis_index("tensor")
    t1, t2 = flip(t, 1), flip(t, 2)
    t3 = flip(t1, 2)
    xb = lax.rem(t, 2)
    zp = lax.rem(d, 2)
    tf = t1 + zp * (t2 - t1)
    td = t2 + zp * (t1 - t2)
    dz = flip(d, 1)
    tw = text_in.shape[2]
    lw = lay_in.shape[1]
    width = tw + lw
    tokens = x_fm.shape[2]
    half = tokens // 2
    quarter = tokens // 4
    hid_t, hid_l = exp_t.shape[1], exp_l.shape[1]
    hs, ls = out_t.shape[0], out_l.shape[0]
    heads = hs // HEAD
    blocks = tokens // LANES
    tq, lq = tw // 4, lw // 4
    streams = ((0, tw), (tw, lw))
    z_peers = [lax.rem(d + r, dp) for r in range(1, dp)] if z_inside else [dz]

    def remote(src, dst, send, recv, device):
        return pltpu.make_async_remote_copy(
            src_ref=src, dst_ref=dst, send_sem=send, recv_sem=recv, device_id=device, device_id_type=MESH
        )

    def local_copy(src, dst, sem):
        return pltpu.make_async_copy(src, dst, sem)

    def landed(ref, sem):
        pltpu.make_async_copy(ref, ref, sem).wait()

    def start(copies):
        for copy in copies:
            copy.start()

    def wait(copies):
        for copy in copies:
            copy.wait()

    own_vec[...] = jnp.zeros(own_vec.shape, f32)
    own_vec[0:1, 0:hid_t] = off_t[...].astype(f32)
    own_vec[0:1, hid_t : hid_t + hid_l] = off_l[...].astype(f32)
    own_vec[1:2, 0:hs] = bias_t[0:1].astype(f32)
    own_vec[1:2, 2 * hs : 3 * hs] = bias_t[1:2].astype(f32)
    own_vec[1:2, 3 * hs : 3 * hs + ls] = bias_l[0:1].astype(f32)
    own_vec[1:2, 3 * hs + 2 * ls : 3 * hs + 3 * ls] = bias_l[1:2].astype(f32)
    own_small[...] = own_vec[...].astype(bf16)
    own_vec[0:6, 0:tw] = vec_t[...].astype(f32)
    own_vec[0:6, tw:width] = vec_l[...].astype(f32)

    barrier = pltpu.get_barrier_semaphore()
    peers = [(1 - c, d, t)] + [(k, d, other) for other in (t1, t2, t3) for k in range(2)] + [(c, z, t) for z in z_peers]
    for peer in peers:
        pl.semaphore_signal(barrier, inc=1, device_id=peer, device_id_type=MESH)
    pl.semaphore_wait(barrier, len(peers))
    other = (1 - c, d, t)

    def row_copies(text, lay, text_to, lay_to, base):
        mine, theirs = xb * half, (1 - xb) * half
        part = c * quarter
        own = [
            local_copy(text.at[xb], text_to.at[at(mine, half)], row_sem.at[base, 0]),
            local_copy(lay.at[xb], lay_to.at[:, lanes_at(mine, half)], row_sem.at[base + 1, 0]),
        ]
        away = [
            remote(
                text.at[1 - xb, at(part, quarter)], text_to.at[at(mine + part, quarter)],
                row_sem.at[base, 1], row_sem.at[base, 2], (c, d, t1),
            ),
            remote(
                lay.at[1 - xb, :, lanes_at(part, quarter)], lay_to.at[:, lanes_at(mine + part, quarter)],
                row_sem.at[base + 1, 1], row_sem.at[base + 1, 2], (c, d, t1),
            ),
        ]
        text_part = text_to.at[at(theirs + part, quarter)]
        lay_part = lay_to.at[:, lanes_at(theirs + part, quarter)]
        across = [
            remote(text_part, text_part, row_sem.at[base, 3], row_sem.at[base, 4], other),
            remote(lay_part, lay_part, row_sem.at[base + 1, 3], row_sem.at[base + 1, 4], other),
        ]
        return own, away, across

    cot_t = fv_t.at[0, pl.ds(0, tokens)]
    in_rows = row_copies(text_in, lay_in, rows_t, x_fm.at[0, pl.ds(tw, lw)], 0)
    cot_rows = row_copies(text_cot, lay_cot, cot_t, g_fm.at[pl.ds(tw, lw)], 2)

    def rows_begin(copies):
        own, away, across = copies
        start(away + own)

    def rows_cross(copies):
        own, away, across = copies
        wait(away)
        start(across)

    def rows_arrive(copies):
        own, away, across = copies
        wait(own + across)

    rows_begin(in_rows)

    text_sources = [att_t.at[pl.ds(j * hs, hs)] for j in range(3)] + [out_t]
    text_sources += [exp_t.at[pl.ds(j * hs, hs)] for j in range(4)] + [shr_t.at[pl.ds(j * hs, hs)] for j in range(4)]
    lay_sources = {12: att_l, 13: out_l, 14: exp_l, 15: shr_l}
    lay_places = {12: (0, 0, 3 * ls), 13: (0, 3 * ls, ls), 14: (1, 0, lw), 15: (2, 0, lw)}
    riders = {0: [12, 16], 3: [13], 4: [14], 8: [15]}

    def source(p):
        if p < STEPS:
            return text_sources[p]
        return lay_sources[p] if p < 16 else own_small

    def place(layer, slot, p):
        if p < STEPS:
            return w_t.at[layer, slot, p // 4, pl.ds((p % 4) * hs, hs)]
        if p < 16:
            which, first, size = lay_places[p]
            return w_l.at[layer, slot, which, pl.ds(first, size)]
        return small.at[layer, slot]

    def pieces(j):
        return [j] + riders.get(j, [])

    all_pieces = [p for j in range(STEPS) for p in pieces(j)]

    def own_first(p):
        return remote(
            source(p), place(c, 1 - zp, p), ag_own.at[p, 0], ag_recv.at[c, 1 - zp, p], (zp, d, tf)
        )

    def own_core(p):
        return remote(source(p), place(1, 0, p), ag_own.at[p, 1], ag_recv.at[1, 0, p], (0, d, t))

    def own_local(p):
        return local_copy(source(p), place(0, 0, p), ag_recv.at[0, 0, p])

    def forwards(layer, p):
        return [
            remote(
                place(layer, 1 - zp, p), place(layer, 1, p),
                ag_fwd.at[layer, p, 0], ag_recv.at[layer, 1, p], (1, d, td),
            ),
            remote(
                place(layer, 1 - zp, p), place(layer, 1 - zp, p),
                ag_fwd.at[layer, p, 1], ag_recv.at[layer, 1 - zp, p], (zp, dz, t),
            ),
        ]

    def fw(layer, *steps):
        @pl.when(c == zp)
        def _():
            for j in steps:
                for p in pieces(j):
                    landed(place(layer, 1 - zp, p), ag_recv.at[layer, 1 - zp, p])
                    start(forwards(layer, p))

    def need(layer, *steps):
        for j in steps:
            for p in pieces(j):
                landed(place(layer, zp, p), ag_recv.at[layer, zp, p])

        @pl.when(c != zp)
        def _():
            for j in steps:
                for p in pieces(j):
                    landed(place(layer, 1 - zp, p), ag_recv.at[layer, 1 - zp, p])

    vec_copies = [
        local_copy(own_vec, vecs.at[c], vec_sem.at[0]),
        remote(own_vec, vecs.at[c], vec_sem.at[1], vec_sem.at[2], other),
    ]
    start(vec_copies)

    @pl.when(c == 0)
    def _():
        for p in all_pieces:
            start([own_first(p), own_local(p)])

    @pl.when(c == 1)
    def _():
        start([own_core(p) for p in all_pieces])

    def start_second_layer():
        @pl.when(c == 1)
        def _():
            start([own_first(p) for p in all_pieces])

    page_len = lengths[xb, lax.div(t, 2)]
    positions = lax.broadcasted_iota(jnp.int32, key_bias.shape, 0)
    key_bias[...] = jnp.where(positions < page_len, 0.0, masked_score).astype(f32)
    smsg[...] = jnp.zeros(smsg.shape, f32)
    ones = jnp.ones((8, tokens), bf16)
    wait(vec_copies)

    def load_columns(layer):
        for k in range(2):
            cols[k] = small[layer, k].astype(f32).T
        cols[2] = vecs[layer].T

    def column(k, first, size, lane):
        return cols[k, pl.ds(first, size), lane : lane + 1]

    def exchange_copy(n):
        return remote(exs, exr.at[n % 2], ex_send.at[n], ex_recv.at[n], other)

    def exchanged(n, first, size, lanes):
        return exs[pl.ds(first, size), lanes].astype(f32) + exr[n % 2, pl.ds(first, size), lanes].astype(f32)

    def project(layer, s):
        mixed = mm(w_t[layer, s, 0, 0 : 3 * hs], x_fm[layer, 0:tw], 1, 0)
        qkv_t[layer, s] = (mixed + cols[s, 0 : 3 * hs, 1:2]).astype(bf16)
        mixed = mm(w_l[layer, s, 0, 0 : 3 * ls], x_fm[layer, tw:width], 1, 0)
        qkv_l[layer, s] = (mixed + cols[s, 3 * hs : 3 * hs + 3 * ls, 1:2]).astype(bf16)

    def head_rows(layer, s, part, h):
        return (
            qkv_t[layer, s, at(part * hs + h * HEAD, HEAD)],
            qkv_l[layer, s, at(part * ls + h * LHEAD, LHEAD)],
        )

    def query(layer, s, h):
        text, lay = head_rows(layer, s, 0, h)
        return jnp.concatenate([text * HEAD**-0.5, lay * LHEAD**-0.5], axis=0).astype(bf16)

    def attend_forward(layer, i):
        s, h = lax.div(i, heads), lax.rem(i, heads)
        keys = jnp.concatenate(head_rows(layer, s, 1, h), axis=0)
        values = jnp.concatenate(head_rows(layer, s, 2, h), axis=0)
        scores = mm(keys, query(layer, s, h), 0, 0) + key_bias[:, 0:1]
        exponent = jnp.exp(scores - jnp.max(scores, axis=0, keepdims=True))
        low = (exponent * (1.0 / jnp.sum(exponent, axis=0, keepdims=True))).astype(bf16)
        probs[i] = low
        context = mm(values, low, 1, 0).astype(bf16)
        ctx_t[layer, s, at(h * HEAD, HEAD)] = context[0:HEAD]
        ctx_l[layer, s, at(h * LHEAD, LHEAD)] = context[HEAD:]

    def attention_partial(layer):
        exs[0:tw] = (
            mm(w_t[layer, 0, 0, 3 * hs : 4 * hs], ctx_t[layer, 0], 0, 0)
            + mm(w_t[layer, 1, 0, 3 * hs : 4 * hs], ctx_t[layer, 1], 0, 0)
        ).astype(bf16)
        exs[tw:width] = (
            mm(w_l[layer, 0, 0, 3 * ls : 4 * ls], ctx_l[layer, 0], 0, 0)
            + mm(w_l[layer, 1, 0, 3 * ls : 4 * ls], ctx_l[layer, 1], 0, 0)
        ).astype(bf16)

    def normalize(hidden):
        center = hidden - jnp.mean(hidden, axis=0, keepdims=True)
        scale = lax.rsqrt(jnp.mean(center * center, axis=0, keepdims=True) + norm_epsilon)
        return center * scale, scale

    def norm_forward(layer, n, which, base, hat_ref, finish):
        def block(b):
            lanes = lanes_at(b * LANES, LANES)
            for k, (first, size) in enumerate(streams):
                hidden = base(first, size, lanes) + exchanged(n, first, size, lanes)
                hat, scale = normalize(hidden + column(2, first, size, 3 * which))
                hat_ref[layer, pl.ds(first, size), lanes] = hat.astype(bf16)
                row = 2 * which + k
                stats[layer, row : row + 1, lanes] = scale
                result = hat * column(2, first, size, 3 * which + 1) + column(2, first, size, 3 * which + 2)
                finish(first, size, lanes, result)

        loop(0, blocks, block)

    def first_norm(layer, n):
        def finish(first, size, lanes, result):
            acc[pl.ds(first, size), lanes] = result
            n1b[layer, pl.ds(first, size), lanes] = result.astype(bf16)

        norm_forward(
            layer, n, 0, lambda s, z, lanes: x_fm[layer, pl.ds(s, z), lanes].astype(f32), xh1, finish
        )

    def second_norm(layer, n, dest):
        def finish(first, size, lanes, result):
            dest[pl.ds(first, size), lanes] = result.astype(bf16)

        norm_forward(layer, n, 1, lambda s, z, lanes: acc[pl.ds(s, z), lanes], xh2, finish)

    def gelu_pair(raised):
        cdf = 0.5 * (1.0 + lax.erf(raised * math.sqrt(0.5)))
        slope = cdf + raised * (jnp.exp(-0.5 * raised * raised) * (1.0 / math.sqrt(2.0 * math.pi)))
        return (raised * cdf).astype(bf16), slope.astype(bf16)

    hb = 256
    per_slot = hid_t // hb

    def expand_block(layer, i):
        s, b = lax.div(i, per_slot), lax.rem(i, per_slot)
        rows = lanes_at(b * hb, hb)
        raised = mm(w_t[layer, s, 1, :, rows], n1b[layer, 0:tw], 0, 0) + cols[s, rows, 0:1]
        act[layer, s, rows], gp[layer, s, rows] = gelu_pair(raised)

    def expand_lay(layer, s):
        raised = mm(w_l[layer, s, 1], n1b[layer, tw:width], 0, 0) + cols[s, hid_t : hid_t + hid_l, 0:1]
        act[layer, s, hid_t:], gp[layer, s, hid_t:] = gelu_pair(raised)

    def shrink_partial(layer):
        exs[0:tw] = (
            mm(w_t[layer, 0, 2], act[layer, 0, 0:hid_t], 1, 0) + mm(w_t[layer, 1, 2], act[layer, 1, 0:hid_t], 1, 0)
        ).astype(bf16)
        exs[tw:width] = (
            mm(w_l[layer, 0, 2], act[layer, 0, hid_t:], 1, 0) + mm(w_l[layer, 1, 2], act[layer, 1, hid_t:], 1, 0)
        ).astype(bf16)

    def rows_out(base, text_to, lay_to):
        mine, theirs = xb * half, (1 - xb) * half
        pairs = (
            (rows_t.at[at(mine, half)], rows_t.at[at(theirs, half)], text_to),
            (rows_l.at[:, lanes_at(mine, half)], rows_l.at[:, lanes_at(theirs, half)], lay_to),
        )
        copies = []
        for k, (own, away, dest) in enumerate(pairs):
            copies.append(local_copy(own, dest.at[xb], out_sem.at[base + k, 0]))
            copies.append(
                remote(away, dest.at[xb], out_sem.at[base + k, 1], out_sem.at[base + k, 2], (c, d, t1))
            )
        return copies

    def stage_rows(layer, value):
        @pl.when(c == layer)
        def _():
            rows_t[...] = value[0:tw].T
            rows_l[...] = value[tw:width]

    def send_rows(layer, base, dest_pair, value):
        stage_rows(layer, value)

        @pl.when(c == layer)
        def _():
            start(rows_out(base, *dest_pair))

    def finish_rows(layer, base, dest_pair):
        @pl.when(c == layer)
        def _():
            wait(rows_out(base, *dest_pair))

    out_pair, back_pair = (text_out, lay_out), (text_back, lay_back)
    rows_cross(in_rows)
    fw(0, 0)
    rows_arrive(in_rows)
    x_fm[0, 0:tw] = rows_t[...].T
    fw(0, 1)
    need(0, 0)
    load_columns(0)

    p_store = local_copy(probs, p_keep, p_sem.at[0])
    p_load = local_copy(p_keep, probs, p_sem.at[1])

    for layer in range(2):
        last = layer == 1
        fw(layer, 2)
        need(layer, 1)
        fw(layer, 3)
        need(layer, 2)
        project(layer, 0)
        fw(layer, 4)
        project(layer, 1)
        if last:
            p_store.wait()
        fw(layer, 5)
        head = functools.partial(attend_forward, layer)
        loop(0, 2, head)
        fw(layer, 6)
        loop(2, 4, head)
        fw(layer, 7)
        loop(4, 6, head)
        if last:
            rows_cross(cot_rows)
        else:
            p_store.start()
            rows_begin(cot_rows)
        need(layer, 3)
        attention_partial(layer)
        swap = exchange_copy(2 * layer)
        swap.start()
        fw(layer, 8)
        swap.wait()
        first_norm(layer, 2 * layer)
        fw(layer, 9)
        need(layer, 4, 5, 6, 7)
        expand = functools.partial(expand_block, layer)
        loop(0, per_slot, expand)
        fw(layer, 10)
        if not last:
            need(layer, 8, 9)
            start_second_layer()
        loop(per_slot, 2 * per_slot, expand)
        fw(layer, 11)
        loop(0, 2, functools.partial(expand_lay, layer))
        if last:
            need(layer, 8, 9, 10, 11)
            rows_arrive(cot_rows)
        else:
            need(layer, 10)
            fw(1, 0)
            need(layer, 11)
        shrink_partial(layer)
        swap = exchange_copy(2 * layer + 1)
        swap.start()
        if not last:
            fw(1, 1)
        else:
            g_fm[0:tw] = cot_t[...].T
        swap.wait()
        if not last:
            second_norm(0, 1, x_fm.at[1])
            need(1, 0)
            load_columns(1)
        else:
            send_rows(0, 0, out_pair, x_fm.at[1])
            second_norm(1, 3, tmpb)
            send_rows(1, 0, out_pair, tmpb)

    def grad_store(layer, chunk, s):
        return [
            local_copy(stg_t.at[s], gb_t.at[layer, chunk, s], stg_sem.at[s, 0]),
            local_copy(stg_l.at[s], gb_l.at[layer, chunk, s], stg_sem.at[s, 1]),
        ]

    def store_grad(layer, chunk, s, text_value, lay_value):
        stg_t[s] = text_value
        stg_l[s] = lay_value
        start(grad_store(layer, chunk, s))

    groups = (
        (gb_t, rz_t, r1_t, r2_t, ro_t, zs_t, zr_t, zv_t, tv_t, fv_t, w_t, tq),
        (gb_l, rz_l, r1_l, r2_l, ro_l, zs_l, zr_l, zv_l, tv_l, fv_l, w_l, lq),
    )
    tx = t1 + c * (t2 - t1)
    near, far = 2 * zp, 2 * (1 - zp)

    def quarters(first, count, size):
        return at(first * size, count * size)

    def first_sends(layer, chunk):
        copies = []
        for g, (gb, rz, r1, r2, ro, zs, zr, zv, tv, fv, w, size) in enumerate(groups):
            for i, rows in enumerate((quarters(far, 2, size), quarters(near + c, 1, size))):
                copies.append(
                    remote(
                        gb.at[layer, chunk, 1 - c, rows], r2.at[chunk, c, rows],
                        s1_send.at[layer, chunk, g, i], s2_recv.at[chunk, c, i, g], (layer, d, tx),
                    )
                )
        return copies

    def own_sends(chunk):
        return [
            remote(gb.at[1, chunk, 0], ro.at[chunk], so_send.at[chunk, g], so_recv.at[chunk, g], other)
            for g, (gb, rz, r1, r2, ro, *_) in enumerate(groups)
        ]

    def pair_sends(layer, chunk):
        return [
            remote(
                gb.at[layer, chunk, 1, quarters(far, 2, size)], rz.at[layer, chunk],
                rz_send.at[layer, chunk, g], rz_recv.at[layer, chunk, g], (1, dz, t),
            )
            for g, (gb, rz, *_, size) in enumerate(groups)
        ]

    def grads_go(layer, chunk):
        for s in range(2):
            wait(grad_store(layer, chunk, s))

        @pl.when(c == 1)
        def _():
            start(pair_sends(layer, chunk))

        if layer == 1:

            @pl.when(c == 0)
            def _():
                start(own_sends(chunk))

        start(first_sends(layer, chunk))

    def pair_loads(layer, chunk):
        copies = []
        for g, (gb, rz, r1, r2, ro, zs, zr, zv, tv, fv, w, size) in enumerate(groups):
            copies.append(local_copy(gb.at[layer, chunk, 1, quarters(near, 2, size)], zv.at[0], zv_sem.at[g, 0]))
            copies.append(local_copy(rz.at[layer, chunk], zv.at[1], zv_sem.at[g, 1]))
        return copies

    def pair_stores(layer, chunk):
        return [
            local_copy(zv.at[0], gb.at[layer, chunk, 1, quarters(near, 2, size)], zv_sem.at[g, 2])
            for g, (gb, rz, r1, r2, ro, zs, zr, zv, tv, fv, w, size) in enumerate(groups)
        ]

    def diagonal_sends(layer, chunk):
        copies = []
        for g, (gb, rz, r1, *_, size) in enumerate(groups):
            for i, device in enumerate(((1, d, t1), (0, d, t2))):
                copies.append(
                    remote(
                        gb.at[layer, chunk, 1, quarters(near + i, 1, size)], r1.at[layer, chunk],
                        d_send.at[layer, chunk, g, i], r1_recv.at[layer, chunk, g], device,
                    )
                )
        return copies

    def pair_load(layer, chunk):
        @pl.when(c == 1)
        def _():
            for g, (gb, rz, *_) in enumerate(groups):
                landed(rz.at[layer, chunk], rz_recv.at[layer, chunk, g])
            start(pair_loads(layer, chunk))

    def pair_add(layer, chunk):
        @pl.when(c == 1)
        def _():
            wait(pair_loads(layer, chunk))
            for zv in (zv_t, zv_l):
                zv[0] = (zv[0].astype(f32) + zv[1].astype(f32)).astype(bf16)
            start(pair_stores(layer, chunk))

    def pair_send(layer, chunk):
        @pl.when(c == 1)
        def _():
            wait(pair_stores(layer, chunk))
            start(diagonal_sends(layer, chunk))

    def waiting(gb, layer, chunk, size):
        return gb.at[layer, chunk, 1 - c, quarters(near + 1 - c, 1, size)]

    def transit_loads(layer, chunk):
        copies = []
        for g, (gb, rz, r1, r2, ro, zs, zr, zv, tv, fv, w, size) in enumerate(groups):
            copies.append(local_copy(waiting(gb, layer, chunk, size), tv.at[0], tv_sem.at[g, 0]))
            copies.append(local_copy(r1.at[layer, chunk], tv.at[1], tv_sem.at[g, 1]))
        return copies

    def transit_stores(layer, chunk):
        return [
            local_copy(tv.at[0], waiting(gb, layer, chunk, size), tv_sem.at[g, 2])
            for g, (gb, rz, r1, r2, ro, zs, zr, zv, tv, fv, w, size) in enumerate(groups)
        ]

    def second_sends(layer, chunk):
        return [
            remote(
                waiting(gb, layer, chunk, size), r2.at[chunk, c, quarters(near + 1 - c, 1, size)],
                s2_send.at[layer, chunk, g], s2_recv.at[chunk, c, 2, g], (layer, d, tx),
            )
            for g, (gb, rz, r1, r2, *_, size) in enumerate(groups)
        ]

    def transit_load(layer, chunk):
        for g, (gb, rz, r1, *_) in enumerate(groups):
            landed(r1.at[layer, chunk], r1_recv.at[layer, chunk, g])
        start(transit_loads(layer, chunk))

    def transit_add(layer, chunk):
        wait(transit_loads(layer, chunk))
        for tv in (tv_t, tv_l):
            tv[0] = (tv[0].astype(f32) + tv[1].astype(f32)).astype(bf16)
        start(transit_stores(layer, chunk))

    def transit_send(layer, chunk):
        wait(transit_stores(layer, chunk))
        start(second_sends(layer, chunk))

    def final_loads(layer, chunk, stage):
        first = near if stage else far
        copies = []
        for g, (gb, rz, r1, r2, ro, zs, zr, zv, tv, fv, w, size) in enumerate(groups):
            rows = quarters(first, 2, size)
            own = ro.at[chunk, rows] if layer == 1 else gb.at[0, chunk, 0, rows]
            places = (w.at[1, 0, chunk, rows], w.at[1, 1, chunk, rows], fv.at[chunk, rows])
            for i, src in enumerate((own, r2.at[chunk, 0, rows], r2.at[chunk, 1, rows])):
                copies.append(local_copy(src, places[i], fv_sem.at[chunk, stage, g, i]))
        return copies

    def final_load(layer, chunk, stage):
        @pl.when(c == layer)
        def _():
            for g, (gb, rz, r1, r2, ro, zs, zr, zv, tv, fv, w, size) in enumerate(groups):
                for way in range(2):
                    if stage == 0:
                        landed(r2.at[chunk, way, quarters(far, 2, size)], s2_recv.at[chunk, way, 0, g])
                    else:
                        landed(r2.at[chunk, way, quarters(near + way, 1, size)], s2_recv.at[chunk, way, 1, g])
                        landed(r2.at[chunk, way, quarters(near + 1 - way, 1, size)], s2_recv.at[chunk, way, 2, g])
                if layer == 1 and stage == 0:
                    landed(ro.at[chunk], so_recv.at[chunk, g])
            start(final_loads(layer, chunk, stage))

    def z_send_of(chunk, stage, i, g):
        gb, rz, r1, r2, ro, zs, zr, zv, tv, fv, w, size = groups[g]
        j = (near if stage else far) + i
        return j, w.at[1, 0, chunk, quarters(j, 1, size)], zr.at[chunk, d]

    def z_remote(chunk, stage, i, g):
        j, piece, dest = z_send_of(chunk, stage, i, g)
        return remote(piece, dest, z_send.at[chunk, stage, i, g], z_recv.at[chunk, d, g], (c, j, t))

    def sum_stores(chunk, stage):
        first = near if stage else far
        return [
            local_copy(
                w.at[1, 0, chunk, quarters(first, 2, size)], zs.at[chunk, quarters(first, 2, size)],
                z_send.at[chunk, stage, 0, g],
            )
            for g, (gb, rz, r1, r2, ro, zs, zr, zv, tv, fv, w, size) in enumerate(groups)
        ]

    def final_add(layer, chunk, stage):
        @pl.when(c == layer)
        def _():
            wait(final_loads(layer, chunk, stage))
            for gb, rz, r1, r2, ro, zs, zr, zv, tv, fv, w, size in groups:
                rows = quarters(near if stage else far, 2, size)
                total = w[1, 0, chunk, rows].astype(f32) + w[1, 1, chunk, rows].astype(f32)
                w[1, 0, chunk, rows] = (total + fv[chunk, rows].astype(f32)).astype(bf16)
            if not z_inside:
                start(sum_stores(chunk, stage))
                return
            for i in range(2):
                for g in range(2):
                    j, piece, dest = z_send_of(chunk, stage, i, g)

                    @pl.when(j != d)
                    def _():
                        z_remote(chunk, stage, i, g).start()

                    @pl.when(j == d)
                    def _():
                        local_copy(piece, dest, z_recv.at[chunk, d, g]).start()

    def final(layer, chunk, stage):
        final_load(layer, chunk, stage)
        final_add(layer, chunk, stage)

    def sums_done():
        for chunk in range(3):
            for stage in range(2):
                if not z_inside:
                    wait(sum_stores(chunk, stage))
                    continue
                for i in range(2):
                    for g in range(2):

                        @pl.when(z_send_of(chunk, stage, i, g)[0] != d)
                        def _():
                            z_remote(chunk, stage, i, g).wait_send()

            if z_inside:
                for j in range(dp):
                    for g in range(2):
                        landed(groups[g][6].at[chunk, j], z_recv.at[chunk, j, g])

    def small_sends(layer):
        zero = [remote(smsg.at[layer, 1], srec.at[0], sm_send.at[layer, 0], sm_recv.at[0], (layer, d, t1))]
        if layer == 1:
            zero.append(remote(smsg.at[1, 0], srec.at[3], sm_send.at[1, 1], sm_recv.at[3], other))
        one = [
            remote(smsg.at[layer, 0], srec.at[1], sm_send.at[layer, 0], sm_recv.at[1], (layer, d, t2)),
            remote(smsg.at[layer, 1], srec.at[2], sm_send.at[layer, 1], sm_recv.at[2], (layer, d, t3)),
        ]
        return zero, one

    def small_go(layer):
        zero, one = small_sends(layer)

        @pl.when(c == 0)
        def _():
            start(zero)

        @pl.when(c == 1)
        def _():
            start(one)

    def small_z():
        if not z_inside:
            return []
        return [
            remote(ssum, szr.at[r - 1], sz_send.at[r - 1], sz_recv.at[r - 1], (c, lax.rem(d + r, dp), t))
            for r in range(1, dp)
        ]

    def small_total(layer):
        @pl.when(c == layer)
        def _():
            for i in range(3):
                landed(srec.at[i], sm_recv.at[i])
            if layer == 1:
                landed(srec.at[3], sm_recv.at[3])
                own = srec[3]
            else:
                own = smsg[0, 0]
            ssum[...] = own + srec[0] + srec[1] + srec[2]
            start(small_z())

    def row_sums(ref):
        return mm(ones, ref[...], 1, 1)[0:1]

    def vector_sum(layer, row, value):
        for s in range(2):
            smsg[layer, s, 8 + row : 9 + row, 0:width] = value

    def norm_backward(layer, which, hat_ref, incoming):
        def block(b):
            lanes = lanes_at(b * LANES, LANES)
            for k, (first, size) in enumerate(streams):
                grad = incoming(first, size, lanes)
                hat = hat_ref[layer, pl.ds(first, size), lanes].astype(f32)
                row = 2 * which + k
                scale = stats[layer, row : row + 1, lanes]
                gained = grad * column(2, first, size, 3 * which + 1)
                mean_grad = jnp.mean(gained, axis=0, keepdims=True)
                mean_both = jnp.mean(gained * hat, axis=0, keepdims=True)
                result = scale * (gained - mean_grad - hat * mean_both)
                acc[pl.ds(first, size), lanes] = result
                tmpb[pl.ds(first, size), lanes] = result.astype(bf16)
                exs[pl.ds(first, size), lanes] = (grad * hat).astype(bf16)
                g_fm[pl.ds(first, size), lanes] = grad.astype(bf16)

        loop(0, blocks, block)
        vector_sum(layer, 3 * which + 1, row_sums(exs))
        vector_sum(layer, 3 * which + 2, row_sums(g_fm))
        vector_sum(layer, 3 * which, row_sums(tmpb))

    def ffn_backward(layer):
        def text_block(i):
            s, b = lax.div(i, per_slot), lax.rem(i, per_slot)
            rows = lanes_at(b * hb, hb)
            back = mm(w_t[layer, s, 2, :, rows], tmpb[0:tw], 0, 0)
            dup[s, rows] = (back * gp[layer, s, rows].astype(f32)).astype(bf16)

        loop(0, 2 * per_slot, text_block)

        def lay_block(s):
            back = mm(w_l[layer, s, 2], tmpb[tw:width], 0, 0)
            dup[s, hid_t:] = (back * gp[layer, s, hid_t:].astype(f32)).astype(bf16)

        loop(0, 2, lay_block)

    def shrink_grads(layer, s):
        store_grad(
            layer, 2, s,
            mm(tmpb[0:tw], act[layer, s, 0:hid_t], 1, 1).astype(bf16),
            mm(tmpb[tw:width], act[layer, s, hid_t:], 1, 1).astype(bf16),
        )

    def expand_grads(layer, s):
        store_grad(
            layer, 1, s,
            mm(n1b[layer, 0:tw], dup[s, 0:hid_t], 1, 1).astype(bf16),
            mm(n1b[layer, tw:width], dup[s, hid_t:], 1, 1).astype(bf16),
        )

    def expand_partial(layer):
        exs[0:tw] = (
            mm(w_t[layer, 0, 1], dup[0, 0:hid_t], 1, 0) + mm(w_t[layer, 1, 1], dup[1, 0:hid_t], 1, 0)
        ).astype(bf16)
        exs[tw:width] = (
            mm(w_l[layer, 0, 1], dup[0, hid_t:], 1, 0) + mm(w_l[layer, 1, 1], dup[1, hid_t:], 1, 0)
        ).astype(bf16)

    def context_grads(layer, s):
        dup[s, 0:hs] = mm(w_t[layer, s, 0, 3 * hs : 4 * hs], tmpb[0:tw], 1, 0).astype(bf16)
        dup[s, hs : hs + ls] = mm(w_l[layer, s, 0, 3 * ls : 4 * ls], tmpb[tw:width], 1, 0).astype(bf16)

    def attend_backward(layer, i):
        s, h = lax.div(i, heads), lax.rem(i, heads)
        queries = query(layer, s, h)
        key_text, key_lay = head_rows(layer, s, 1, h)
        keys = jnp.concatenate([key_text * HEAD**-0.5, key_lay * LHEAD**-0.5], axis=0).astype(bf16)
        values = jnp.concatenate(head_rows(layer, s, 2, h), axis=0)
        grads = jnp.concatenate([dup[s, at(h * HEAD, HEAD)], dup[s, at(hs + h * LHEAD, LHEAD)]], axis=0)
        low = probs[i]
        prob = low.astype(f32)
        dprob = mm(values, grads, 0, 0)
        inner = jnp.sum(dprob * prob, axis=0, keepdims=True)
        dscore = (prob * (dprob - inner)).astype(bf16)
        results = (mm(keys, dscore, 1, 0), mm(queries, dscore, 1, 1), mm(grads, low, 1, 1))
        for part, result in enumerate(results):
            result = result.astype(bf16)
            dqkv[s, at(part * hs + h * HEAD, HEAD)] = result[0:HEAD]
            dqkv[s, at(3 * hs + part * ls + h * LHEAD, LHEAD)] = result[HEAD:]

    def attend_grads(layer, s):
        text = jnp.concatenate(
            [mm(x_fm[layer, 0:tw], dqkv[s, 0 : 3 * hs], 1, 1), mm(tmpb[0:tw], ctx_t[layer, s], 1, 1)], axis=1
        )
        lay = jnp.concatenate(
            [mm(x_fm[layer, tw:width], dqkv[s, 3 * hs :], 1, 1), mm(tmpb[tw:width], ctx_l[layer, s], 1, 1)], axis=1
        )
        store_grad(layer, 0, s, text.astype(bf16), lay.astype(bf16))

    def attend_partial(layer):
        exs[0:tw] = (
            mm(w_t[layer, 0, 0, 0 : 3 * hs], dqkv[0, 0 : 3 * hs], 0, 0)
            + mm(w_t[layer, 1, 0, 0 : 3 * hs], dqkv[1, 0 : 3 * hs], 0, 0)
        ).astype(bf16)
        exs[tw:width] = (
            mm(w_l[layer, 0, 0, 0 : 3 * ls], dqkv[0, 3 * hs :], 0, 0)
            + mm(w_l[layer, 1, 0, 0 : 3 * ls], dqkv[1, 3 * hs :], 0, 0)
        ).astype(bf16)

    def small_sums(layer, s, row, ref, size):
        smsg[layer, s, row : row + 1, 0:size] = mm(ones, ref[s], 1, 1)[0:1]

    def first_grad(n, first, size, lanes):
        return acc[pl.ds(first, size), lanes] + exchanged(n, first, size, lanes)

    def gather_sent():
        for layer in range(2):

            @pl.when(c == layer)
            def _():
                for p in all_pieces:
                    own_first(p).wait_send()
                    if layer == 1:
                        own_core(p).wait_send()

            @pl.when(c == zp)
            def _():
                for p in all_pieces:
                    for copy in forwards(layer, p):
                        copy.wait_send()

    def run(*tasks):
        for task in tasks:
            task[0](*task[1:])

    Z, T, F = (pair_load, pair_add, pair_send), (transit_load, transit_add, transit_send), (final_load, final_add)
    service = {
        (1, "context"): [(Z[0], 1, 2)],
        (1, "heads 0"): [(Z[1], 1, 2)],
        (1, "heads 1"): [(Z[2], 1, 2), (Z[0], 1, 1)],
        (1, "heads 2"): [(Z[1], 1, 1)],
        (1, "attend grads"): [(Z[2], 1, 1)],
        (1, "swap"): [(T[0], 1, 2)],
        (1, "swapped"): [(T[1], 1, 2)],
        (1, "finished"): [(T[2], 1, 2)],
        (0, "begin"): [(gather_sent,), (T[0], 1, 1)],
        (0, "second norm"): [(T[1], 1, 1), (Z[0], 1, 0), (F[0], 1, 2, 0)],
        (0, "shrink grads"): [(T[2], 1, 1), (Z[1], 1, 0)],
        (0, "ffn"): [(Z[2], 1, 0), (F[1], 1, 2, 0)],
        (0, "expand grads"): [(T[0], 1, 0), (F[0], 1, 2, 1)],
        (0, "ffn swap"): [(F[1], 1, 2, 1)],
        (0, "first norm"): [(T[1], 1, 0), (F[0], 1, 1, 0), (Z[0], 0, 2)],
        (0, "context"): [(T[2], 1, 0)],
        (0, "heads 0"): [(Z[1], 0, 2), (F[1], 1, 1, 0), (F[0], 1, 1, 1)],
        (0, "heads 1"): [(Z[2], 0, 2), (Z[0], 0, 1), (F[1], 1, 1, 1)],
        (0, "heads 2"): [(Z[1], 0, 1), (T[0], 0, 2), (F[0], 1, 0, 0)],
        (0, "attend grads"): [(Z[2], 0, 1), (T[1], 0, 2), (F[1], 1, 0, 0)],
        (0, "swap"): [(T[2], 0, 2), (F[0], 1, 0, 1)],
        (0, "finished"): [(F[1], 1, 0, 1)],
    }

    for layer in (1, 0):
        last = layer == 0
        n = 4 + 2 * (1 - layer)

        def point(name):
            run(*service.get((layer, name), []))

        if last:
            load_columns(0)
        point("begin")
        norm_backward(layer, 1, xh2, lambda s, z, lanes: g_fm[pl.ds(s, z), lanes].astype(f32))
        point("second norm")
        for s in range(2):
            shrink_grads(layer, s)
        point("shrink grads")
        ffn_backward(layer)
        grads_go(layer, 2)
        point("ffn")
        for s in range(2):
            expand_grads(layer, s)
        point("expand grads")
        expand_partial(layer)
        swap = exchange_copy(n)
        swap.start()
        for s in range(2):
            small_sums(layer, s, 0, dup, hid_t + hid_l)
        grads_go(layer, 1)
        point("ffn swap")
        swap.wait()
        norm_backward(layer, 0, xh1, functools.partial(first_grad, n))
        point("first norm")
        if last:
            p_load.wait()
        for s in range(2):
            context_grads(layer, s)
        point("context")
        head = functools.partial(attend_backward, layer)
        for i in range(3):
            loop(2 * i, 2 * i + 2, head)
            point(f"heads {i}")
        if not last:
            p_load.start()
        for s in range(2):
            attend_grads(layer, s)
        point("attend grads")
        attend_partial(layer)
        swap = exchange_copy(n + 1)
        swap.start()
        for s in range(2):
            small_sums(layer, s, 1, dqkv, 3 * hs + 3 * ls)
        small_go(layer)
        grads_go(layer, 0)
        point("swap")
        swap.wait()
        point("swapped")

        def finish(b):
            lanes = lanes_at(b * LANES, LANES)
            for first, size in streams:
                g_fm[pl.ds(first, size), lanes] = first_grad(n + 1, first, size, lanes).astype(bf16)

        loop(0, blocks, finish)
        point("finished")
        finish_rows(layer, 0, out_pair)
        stage_rows(layer, g_fm)

    run(
        *((step, 0, 1) for step in T), *((step, 0, 0) for step in Z),
        (final, 0, 2, 0), (final, 0, 2, 1), (small_total, 1), (final, 0, 1, 0),
        *((step, 0, 0) for step in T),
    )
    start(rows_out(2, *back_pair))
    run((small_total, 0), (final, 0, 1, 1), (final, 0, 0, 0), (final, 0, 0, 1))

    for copy in small_z():
        copy.wait()
    if z_inside:
        for r in range(1, dp):
            ssum[...] = ssum[...] + szr[r - 1]
    sm_copy = local_copy(ssum, sm_out, so_sem.at[0])
    sm_copy.start()
    wait(rows_out(2, *back_pair))
    for layer in range(2):
        smalls = small_sends(layer)
        for core in range(2):

            @pl.when(c == core)
            def _():
                for copy in smalls[core]:
                    copy.wait_send()
                for chunk in range(3):
                    if core == 1:
                        for copy in pair_sends(layer, chunk) + diagonal_sends(layer, chunk):
                            copy.wait_send()
                    elif layer == 1:
                        for copy in own_sends(chunk):
                            copy.wait_send()

        for chunk in range(3):
            for copy in first_sends(layer, chunk) + second_sends(layer, chunk):
                copy.wait_send()
    sums_done()
    sm_copy.wait()


def finishing(
    parts_t, parts_l, sums_in, rows_in_0, rows_in_1, rows_in_2, rows_in_3,
    rows_0, rows_1, rows_2, rows_3, att_t, out_t, exp_t, shr_t, att_l, out_l, exp_l, shr_l,
    bias_t, off_t, vec_t, bias_l, off_l, vec_l,
    zr_t, zr_l, sums, held_0, held_1, held_2, held_3, sems,
):
    pairs = ((rows_in_0, held_0), (rows_in_1, held_1), (rows_in_2, held_2), (rows_in_3, held_3))
    pairs += ((parts_t, zr_t), (parts_l, zr_l), (sums_in, sums))
    loads = [pltpu.make_async_copy(src, dst, sems.at[i]) for i, (src, dst) in enumerate(pairs)]
    for copy in loads:
        copy.start()
    pairs = ((held_0, rows_0), (held_1, rows_1), (held_2, rows_2), (held_3, rows_3))
    copies = [pltpu.make_async_copy(src, dst, sems.at[7 + i]) for i, (src, dst) in enumerate(pairs)]
    for load, copy in zip(loads[:4], copies):
        load.wait()
        copy.start()
    for load in loads[4:]:
        load.wait()
    for zr, att, out, exp, shr in ((zr_t, att_t, out_t, exp_t, shr_t), (zr_l, att_l, out_l, exp_l, shr_l)):
        totals = []
        for chunk in range(3):
            total = zr[chunk, 0].astype(f32)
            for r in range(1, zr.shape[1]):
                total = total + zr[chunk, r].astype(f32)
            totals.append(total)
        size = out.shape[1]
        for j in range(3):
            att[j] = totals[0][:, j * size : (j + 1) * size]
        out[...] = totals[0][:, 3 * size : 4 * size]
        exp[...] = totals[1]
        shr[...] = totals[2]
    hs, ls = bias_t.shape[1], bias_l.shape[1]
    ft, fl = off_t.shape[1], off_l.shape[1]
    tw, lw = vec_t.shape[2], vec_l.shape[2]
    off_t[...] = sums[0:1, 0:ft]
    off_l[...] = sums[0:1, ft : ft + fl]
    bias_t[0:1] = sums[1:2, 0:hs]
    bias_t[1:2] = sums[1:2, 2 * hs : 3 * hs]
    bias_l[0:1] = sums[1:2, 3 * hs : 3 * hs + ls]
    bias_l[1:2] = sums[1:2, 3 * hs + 2 * ls : 3 * hs + 3 * ls]
    for row in range(6):
        vec_t[row] = sums[8 + row : 9 + row, 0:tw]
        vec_l[row] = sums[8 + row : 9 + row, tw : tw + lw]
    for copy in copies:
        copy.wait()


def local(
    dp,
    text_in,
    layout_in,
    text_cot,
    layout_cot,
    lengths,
    text_attend,
    text_biases,
    text_output,
    text_expand,
    text_offset,
    text_shrink,
    text_vectors,
    layout_attend,
    layout_biases,
    layout_output,
    layout_expand,
    layout_offset,
    layout_shrink,
    layout_vectors,
):
    rows, tw = text_in.shape[1:]
    lw = layout_in.shape[2]
    width, tokens = tw + lw, 2 * rows
    hs, ls = text_output.shape[2], layout_output.shape[2]
    ft, fl = text_expand.shape[2], layout_expand.shape[2]
    zt, zl = tw // dp, lw // dp
    z_inside = dp == 4

    def shape(dims, dtype=bf16):
        return jax.ShapeDtypeStruct(dims, dtype)

    def attend_rows(attend):
        return attend[0].transpose(1, 2, 0).reshape(-1, attend.shape[1])

    hbm = pl.BlockSpec(memory_space=pltpu.HBM)
    vmem = pl.BlockSpec(memory_space=pltpu.VMEM)
    heads = hs // HEAD
    row_shapes = [shape((2, rows, tw)), shape((2, lw, rows)), shape((2, rows, tw)), shape((2, lw, rows))]
    out_shape = row_shapes + [
        shape((16, SMALL), f32),
        shape((3, tw, tw)), shape((3, lw, lw)),
        shape((3, 4, tw // 4, tw)), shape((3, 4, lw // 4, lw)),
        shape((2, 3, 2, tw, tw)), shape((2, 3, 2, lw, lw)),
        shape((2, 3, tw // 2, tw)), shape((2, 3, lw // 2, lw)),
        shape((2, 3, tw // 4, tw)), shape((2, 3, lw // 4, lw)),
        shape((3, 2, tw, tw)), shape((3, 2, lw, lw)),
        shape((3, tw, tw)), shape((3, lw, lw)),
        shape((2 * heads, tokens, tokens)),
    ]
    dma = pltpu.SemaphoreType.DMA
    scratch = [
        pltpu.VMEM((2, 2, 3, tw, tw), bf16),
        pltpu.VMEM((2, 2, 3, lw, lw), bf16),
        pltpu.VMEM((2, 2, 16, SMALL), bf16),
        pltpu.VMEM((2, 16, SMALL), f32),
        pltpu.VMEM((16, SMALL), bf16),
        pltpu.VMEM((16, SMALL), f32),
        pltpu.VMEM((tokens, LANES), f32),
        pltpu.VMEM((tokens, tw), bf16),
        pltpu.VMEM((lw, tokens), bf16),
        pltpu.VMEM((2, width, tokens), bf16),
        pltpu.VMEM((2, 2, 3 * hs, tokens), bf16),
        pltpu.VMEM((2, 2, 3 * ls, tokens), bf16),
        pltpu.VMEM((2 * heads, tokens, tokens), bf16),
        pltpu.VMEM((2, 2, hs, tokens), bf16),
        pltpu.VMEM((2, 2, ls, tokens), bf16),
        pltpu.VMEM((2, width, tokens), bf16),
        pltpu.VMEM((2, width, tokens), bf16),
        pltpu.VMEM((2, width, tokens), bf16),
        pltpu.VMEM((2, 2, ft + fl, tokens), bf16),
        pltpu.VMEM((2, 2, ft + fl, tokens), bf16),
        pltpu.VMEM((2, 8, tokens), f32),
        pltpu.VMEM((width, tokens), f32),
        pltpu.VMEM((width, tokens), bf16),
        pltpu.VMEM((2, width, tokens), bf16),
        pltpu.VMEM((width, tokens), bf16),
        pltpu.VMEM((width, tokens), bf16),
        pltpu.VMEM((2, ft + fl, tokens), bf16),
        pltpu.VMEM((2, 3 * hs + 3 * ls, tokens), bf16),
        pltpu.VMEM((3, SMALL, 16), f32),
        pltpu.VMEM((2, tw, tw), bf16),
        pltpu.VMEM((2, lw, lw), bf16),
        pltpu.VMEM((2, tw // 2, tw), bf16),
        pltpu.VMEM((2, lw // 2, lw), bf16),
        pltpu.VMEM((2, tw // 4, tw), bf16),
        pltpu.VMEM((2, lw // 4, lw), bf16),
        pltpu.VMEM((3, tw, tw), bf16),
        pltpu.VMEM((3, lw, lw), bf16),
        pltpu.VMEM((2, 2, 16, SMALL), f32),
        pltpu.VMEM((4, 16, SMALL), f32),
        pltpu.VMEM((16, SMALL), f32),
        pltpu.VMEM((3, 16, SMALL), f32),
        dma((2, 2, 17)), dma((17, 2)), dma((2, 17, 2)), dma((3,)), dma((4, 5)), dma((8,)), dma((8,)),
        dma((4, 3)), dma((2, 2)), dma((2,)),
        dma((2, 3, 2)), dma((2, 3, 2)), dma((2, 3, 2, 2)), dma((2, 3, 2, 2)), dma((2, 3, 2)), dma((2, 3, 2)),
        dma((3, 2, 3, 2)), dma((3, 2)), dma((3, 2)), dma((3, 2, 2, 2)), dma((3, 4, 2)),
        dma((2, 3)), dma((2, 3)), dma((3, 2, 2, 3)),
        dma((2, 2)), dma((4,)), dma((3,)), dma((3,)), dma((1,)),
    ]
    results = pl.pallas_call(
        functools.partial(kernel, dp, z_inside),
        out_shape=out_shape,
        in_specs=[hbm] * 12 + [vmem] * 6 + [pl.BlockSpec(memory_space=pltpu.SMEM)],
        out_specs=[hbm] * len(out_shape),
        scratch_shapes=scratch,
        compiler_params=pltpu.CompilerParams(
            collective_id=0, has_side_effects=True, vmem_limit_bytes=63 * 1024 * 1024
        ),
    )(
        text_in, layout_in.transpose(0, 2, 1), text_cot, layout_cot.transpose(0, 2, 1),
        attend_rows(text_attend), text_output[0].T, text_expand[0], text_shrink[0],
        attend_rows(layout_attend), layout_output[0].T, layout_expand[0], layout_shrink[0],
        text_biases[0], layout_biases[0], text_offset, layout_offset, text_vectors[0], layout_vectors[0], lengths,
    )
    row_results, sums = results[:4], results[4]
    if z_inside:
        parts_t, parts_l = results[7], results[8]
    else:
        parts_t = lax.psum_scatter(results[5], "dp", scatter_dimension=1, tiled=True)[:, None]
        parts_l = lax.psum_scatter(results[6], "dp", scatter_dimension=1, tiled=True)[:, None]
        sums = lax.psum(sums, "dp")
    final_shapes = row_shapes + [
        shape((3, zt, hs), f32), shape((zt, hs), f32), shape((zt, ft), f32), shape((zt, ft), f32),
        shape((3, zl, ls), f32), shape((zl, ls), f32), shape((zl, fl), f32), shape((zl, fl), f32),
        shape((2, hs), f32), shape((1, ft), f32), shape((6, 1, tw), f32),
        shape((2, ls), f32), shape((1, fl), f32), shape((6, 1, lw), f32),
    ]
    (
        text_out, lay_out, text_back, lay_back, att_t, out_t, exp_t, shr_t, att_l, out_l, exp_l, shr_l,
        bias_t, off_t, vec_t, bias_l, off_l, vec_l,
    ) = pl.pallas_call(
        finishing,
        out_shape=final_shapes,
        in_specs=[hbm] * 7,
        out_specs=[hbm] * 4 + [vmem] * 14,
        scratch_shapes=[
            pltpu.VMEM(parts_t.shape, bf16), pltpu.VMEM(parts_l.shape, bf16), pltpu.VMEM((16, SMALL), f32),
            *(pltpu.VMEM(rows.shape, bf16) for rows in row_shapes), dma((11,)),
        ],
        compiler_params=pltpu.CompilerParams(vmem_limit_bytes=62 * 1024 * 1024),
    )(parts_t, parts_l, sums, *row_results)
    return (
        text_out[None],
        lay_out.transpose(0, 2, 1)[None],
        text_back[None],
        lay_back.transpose(0, 2, 1)[None],
        att_t.transpose(1, 0, 2)[None],
        bias_t[None],
        out_t[None],
        exp_t[None],
        off_t,
        shr_t[None],
        vec_t.transpose(1, 0, 2),
        att_l.transpose(1, 0, 2)[None],
        bias_l[None],
        out_l[None],
        exp_l[None],
        off_l,
        shr_l[None],
        vec_l.transpose(1, 0, 2),
    )


def solution(mesh):
    return jax.shard_map(
        functools.partial(local, mesh.shape["dp"]),
        mesh=mesh,
        in_specs=(
            P(None, ("dp", "tensor"), None),
            P(None, ("dp", "tensor"), None),
            P(None, ("dp", "tensor"), None),
            P(None, ("dp", "tensor"), None),
            P(None, "dp"),
            P("section", None, None, "tensor"),
            P("section", None, "tensor"),
            P("section", None, "tensor"),
            P("section", None, "tensor"),
            P("section", "tensor"),
            P("section", None, "tensor"),
            P("section", None, None),
            P("section", None, None, "tensor"),
            P("section", None, "tensor"),
            P("section", None, "tensor"),
            P("section", None, "tensor"),
            P("section", "tensor"),
            P("section", None, "tensor"),
            P("section", None, None),
        ),
        out_specs=(
            P("section", None, ("dp", "tensor"), None),
            P("section", None, ("dp", "tensor"), None),
            P("section", None, ("dp", "tensor"), None),
            P("section", None, ("dp", "tensor"), None),
            P("section", "dp", None, "tensor"),
            P("section", None, "tensor"),
            P("section", "dp", "tensor"),
            P("section", "dp", "tensor"),
            P("section", "tensor"),
            P("section", "dp", "tensor"),
            P("section", None, None),
            P("section", "dp", None, "tensor"),
            P("section", None, "tensor"),
            P("section", "dp", "tensor"),
            P("section", "dp", "tensor"),
            P("section", "tensor"),
            P("section", "dp", "tensor"),
            P("section", None, None),
        ),
        check_vma=False,
    )
```

```python
import functools
import math

import jax
import jax.numpy as jnp
from jax import lax
from jax.experimental import pallas as pl
from jax.experimental.pallas import tpu as pltpu
from jax.sharding import PartitionSpec as P

HEAD = 64
LHEAD = 16
MESH = pl.DeviceIdType.MESH
bf16 = jnp.bfloat16
f32 = jnp.float32
norm_epsilon = 1e-05
masked_score = -1e30
LANES = 128
SMALL = 1024
STEPS = 12


def mm(left, right, left_axis, right_axis):
    return lax.dot_general(
        left, right, (((left_axis,), (right_axis,)), ((), ())), preferred_element_type=f32
    )


def flip(index, bit):
    return index + bit - 2 * bit * lax.rem(lax.div(index, bit), 2)


def loop(start, stop, body):
    lax.fori_loop(start, stop, lambda i, carry: (body(i), carry)[1], 0)


def at(start, size):
    return pl.ds(pl.multiple_of(start, 16), size)


def lanes_at(start, size):
    return pl.ds(pl.multiple_of(start, LANES), size)


def kernel(
    dp,
    z_inside,
    text_in, lay_in, text_cot, lay_cot, att_t, out_t, exp_t, shr_t, att_l, out_l, exp_l, shr_l,
    bias_t, bias_l, off_t, off_l, vec_t, vec_l, lengths,
    text_out, lay_out, text_back, lay_back, sm_out,
    zs_t, zs_l, zr_t, zr_l, zh_t, zh_l, gb_t, gb_l, rz_t, rz_l, rh_t, rh_l, r1_t, r1_l, r2_t, r2_l, ro_t, ro_l, p_keep,
    w_t, w_l, small, vecs, own_small, own_vec, key_bias, rows_t, rows_l, x_fm, qkv_t, qkv_l, probs,
    ctx_t, ctx_l, xh1, n1b, xh2, act, gp, stats, acc, exs, exr, tmpb, g_fm, dup, dqkv, cols,
    stg_t, stg_l, zv_t, zv_l, tv_t, tv_l, fv_t, fv_l, smsg, srec, ssum, szr,
    ag_recv, ag_own, ag_fwd, vec_sem, row_sem, ex_send, ex_recv, out_sem, stg_sem, p_sem,
    rz_send, rz_recv, s1_send, d_send, r1_recv, s2_send, s2_recv, so_send, so_recv, z_send, z_recv, zh_recv,
    zv_sem, tv_sem, fv_sem,
    sm_send, sm_recv, sz_send, sz_recv, so_sem,
):
    c = lax.axis_index("section")
    d = lax.axis_index("dp")
    t = lax.axis_index("tensor")
    t1, t2 = flip(t, 1), flip(t, 2)
    t3 = flip(t1, 2)
    xb = lax.rem(t, 2)
    zp = lax.rem(d, 2)
    tf = t1 + zp * (t2 - t1)
    td = t2 + zp * (t1 - t2)
    dz = flip(d, 1)
    tw = text_in.shape[2]
    lw = lay_in.shape[1]
    width = tw + lw
    tokens = x_fm.shape[2]
    half = tokens // 2
    quarter = tokens // 4
    hid_t, hid_l = exp_t.shape[1], exp_l.shape[1]
    hs, ls = out_t.shape[0], out_l.shape[0]
    heads = hs // HEAD
    blocks = tokens // LANES
    tq, lq = tw // 4, lw // 4
    streams = ((0, tw), (tw, lw))
    z_peers = [lax.rem(d + r, dp) for r in range(1, dp)] if z_inside else [dz]

    def remote(src, dst, send, recv, device):
        return pltpu.make_async_remote_copy(
            src_ref=src, dst_ref=dst, send_sem=send, recv_sem=recv, device_id=device, device_id_type=MESH
        )

    def local_copy(src, dst, sem):
        return pltpu.make_async_copy(src, dst, sem)

    def landed(ref, sem):
        pltpu.make_async_copy(ref, ref, sem).wait()

    def start(copies):
        for copy in copies:
            copy.start()

    def wait(copies):
        for copy in copies:
            copy.wait()

    barrier = pltpu.get_barrier_semaphore()
    peers = [(1 - c, d, t)] + [(k, d, other) for other in (t1, t2, t3) for k in range(2)] + [(c, z, t) for z in z_peers]
    for peer in peers:
        pl.semaphore_signal(barrier, inc=1, device_id=peer, device_id_type=MESH)

    own_vec[...] = jnp.zeros(own_vec.shape, f32)
    own_vec[0:1, 0:hid_t] = off_t[...].astype(f32)
    own_vec[0:1, hid_t : hid_t + hid_l] = off_l[...].astype(f32)
    own_vec[1:2, 0:hs] = bias_t[0:1].astype(f32)
    own_vec[1:2, 2 * hs : 3 * hs] = bias_t[1:2].astype(f32)
    own_vec[1:2, 3 * hs : 3 * hs + ls] = bias_l[0:1].astype(f32)
    own_vec[1:2, 3 * hs + 2 * ls : 3 * hs + 3 * ls] = bias_l[1:2].astype(f32)
    own_small[...] = own_vec[...].astype(bf16)
    own_vec[0:6, 0:tw] = vec_t[...].astype(f32)
    own_vec[0:6, tw:width] = vec_l[...].astype(f32)
    pl.semaphore_wait(barrier, len(peers))
    other = (1 - c, d, t)

    def row_copies(text, lay, text_to, lay_to, base):
        mine, theirs = xb * half, (1 - xb) * half
        part = c * quarter
        own = [
            local_copy(text.at[xb], text_to.at[at(mine, half)], row_sem.at[base, 0]),
            local_copy(lay.at[xb], lay_to.at[:, lanes_at(mine, half)], row_sem.at[base + 1, 0]),
        ]
        away = [
            remote(
                text.at[1 - xb, at(part, quarter)], text_to.at[at(mine + part, quarter)],
                row_sem.at[base, 1], row_sem.at[base, 2], (c, d, t1),
            ),
            remote(
                lay.at[1 - xb, :, lanes_at(part, quarter)], lay_to.at[:, lanes_at(mine + part, quarter)],
                row_sem.at[base + 1, 1], row_sem.at[base + 1, 2], (c, d, t1),
            ),
        ]
        text_part = text_to.at[at(theirs + part, quarter)]
        lay_part = lay_to.at[:, lanes_at(theirs + part, quarter)]
        across = [
            remote(text_part, text_part, row_sem.at[base, 3], row_sem.at[base, 4], other),
            remote(lay_part, lay_part, row_sem.at[base + 1, 3], row_sem.at[base + 1, 4], other),
        ]
        return own, away, across

    cot_t = fv_t.at[0, pl.ds(0, tokens)]
    in_rows = row_copies(text_in, lay_in, rows_t, x_fm.at[0, pl.ds(tw, lw)], 0)
    cot_rows = row_copies(text_cot, lay_cot, cot_t, g_fm.at[pl.ds(tw, lw)], 2)

    def rows_begin(copies):
        own, away, across = copies
        start(away + own)

    def rows_cross(copies):
        own, away, across = copies
        wait(away)
        start(across)

    def rows_arrive(copies):
        own, away, across = copies
        wait(own + across)

    rows_begin(in_rows)

    text_sources = [att_t.at[pl.ds(j * hs, hs)] for j in range(3)] + [out_t]
    text_sources += [exp_t.at[pl.ds(j * hs, hs)] for j in range(4)] + [shr_t.at[pl.ds(j * hs, hs)] for j in range(4)]
    lay_sources = {12: att_l, 13: out_l, 14: exp_l, 15: shr_l}
    lay_places = {12: (0, 0, 3 * ls), 13: (0, 3 * ls, ls), 14: (1, 0, lw), 15: (2, 0, lw)}
    riders = {0: [12, 16], 3: [13], 4: [14], 8: [15]}

    def source(p):
        if p < STEPS:
            return text_sources[p]
        return lay_sources[p] if p < 16 else own_small

    def place(layer, slot, p):
        if p < STEPS:
            return w_t.at[layer, slot, p // 4, pl.ds((p % 4) * hs, hs)]
        if p < 16:
            which, first, size = lay_places[p]
            return w_l.at[layer, slot, which, pl.ds(first, size)]
        return small.at[layer, slot]

    def pieces(j):
        return [j] + riders.get(j, [])

    all_pieces = [p for j in range(STEPS) for p in pieces(j)]

    def own_first(p):
        return remote(
            source(p), place(c, 1 - zp, p), ag_own.at[p, 0], ag_recv.at[c, 1 - zp, p], (zp, d, tf)
        )

    def own_core(p):
        return remote(source(p), place(1, 0, p), ag_own.at[p, 1], ag_recv.at[1, 0, p], (0, d, t))

    def own_local(p):
        return local_copy(source(p), place(0, 0, p), ag_recv.at[0, 0, p])

    def forwards(layer, p):
        return [
            remote(
                place(layer, 1 - zp, p), place(layer, 1, p),
                ag_fwd.at[layer, p, 0], ag_recv.at[layer, 1, p], (1, d, td),
            ),
            remote(
                place(layer, 1 - zp, p), place(layer, 1 - zp, p),
                ag_fwd.at[layer, p, 1], ag_recv.at[layer, 1 - zp, p], (zp, dz, t),
            ),
        ]

    def fw(layer, *steps):
        @pl.when(c == zp)
        def _():
            for j in steps:
                for p in pieces(j):
                    landed(place(layer, 1 - zp, p), ag_recv.at[layer, 1 - zp, p])
                    start(forwards(layer, p))

    def need(layer, *steps):
        for j in steps:
            for p in pieces(j):
                landed(place(layer, zp, p), ag_recv.at[layer, zp, p])

        @pl.when(c != zp)
        def _():
            for j in steps:
                for p in pieces(j):
                    landed(place(layer, 1 - zp, p), ag_recv.at[layer, 1 - zp, p])

    vec_copies = [
        local_copy(own_vec, vecs.at[c], vec_sem.at[0]),
        remote(own_vec, vecs.at[c], vec_sem.at[1], vec_sem.at[2], other),
    ]

    @pl.when(c == 0)
    def _():
        start([own_first(p) for p in all_pieces])

    start(vec_copies)

    @pl.when(c == 0)
    def _():
        start([own_local(p) for p in all_pieces])

    @pl.when(c == 1)
    def _():
        start([own_core(p) for p in all_pieces])

    def start_second_layer():
        @pl.when(c == 1)
        def _():
            start([own_first(p) for p in all_pieces])

    page_len = lengths[xb, lax.div(t, 2)]
    positions = lax.broadcasted_iota(jnp.int32, key_bias.shape, 0)
    key_bias[...] = jnp.where(positions < page_len, 0.0, masked_score).astype(f32)
    smsg[...] = jnp.zeros(smsg.shape, f32)
    ones = jnp.ones((8, tokens), bf16)
    wait(vec_copies)

    def load_columns(layer):
        for k in range(2):
            cols[k] = small[layer, k].astype(f32).T
        cols[2] = vecs[layer].T

    def column(k, first, size, lane):
        return cols[k, pl.ds(first, size), lane : lane + 1]

    def exchange_copy(n):
        return remote(exs, exr.at[n % 2], ex_send.at[n], ex_recv.at[n], other)

    def exchanged(n, first, size, lanes):
        return exs[pl.ds(first, size), lanes].astype(f32) + exr[n % 2, pl.ds(first, size), lanes].astype(f32)

    def project(layer, s):
        mixed = mm(w_t[layer, s, 0, 0 : 3 * hs], x_fm[layer, 0:tw], 1, 0)
        qkv_t[layer, s] = (mixed + cols[s, 0 : 3 * hs, 1:2]).astype(bf16)
        mixed = mm(w_l[layer, s, 0, 0 : 3 * ls], x_fm[layer, tw:width], 1, 0)
        qkv_l[layer, s] = (mixed + cols[s, 3 * hs : 3 * hs + 3 * ls, 1:2]).astype(bf16)

    def head_rows(layer, s, part, h):
        return (
            qkv_t[layer, s, at(part * hs + h * HEAD, HEAD)],
            qkv_l[layer, s, at(part * ls + h * LHEAD, LHEAD)],
        )

    def query(layer, s, h):
        text, lay = head_rows(layer, s, 0, h)
        return jnp.concatenate([text * HEAD**-0.5, lay * LHEAD**-0.5], axis=0).astype(bf16)

    def attend_forward(layer, i):
        s, h = lax.div(i, heads), lax.rem(i, heads)
        keys = jnp.concatenate(head_rows(layer, s, 1, h), axis=0)
        values = jnp.concatenate(head_rows(layer, s, 2, h), axis=0)
        scores = mm(keys, query(layer, s, h), 0, 0) + key_bias[:, 0:1]
        exponent = jnp.exp(scores - jnp.max(scores, axis=0, keepdims=True))
        low = (exponent * (1.0 / jnp.sum(exponent, axis=0, keepdims=True))).astype(bf16)
        probs[i] = low
        context = mm(values, low, 1, 0).astype(bf16)
        ctx_t[layer, s, at(h * HEAD, HEAD)] = context[0:HEAD]
        ctx_l[layer, s, at(h * LHEAD, LHEAD)] = context[HEAD:]

    def attention_partial(layer):
        exs[0:tw] = (
            mm(w_t[layer, 0, 0, 3 * hs : 4 * hs], ctx_t[layer, 0], 0, 0)
            + mm(w_t[layer, 1, 0, 3 * hs : 4 * hs], ctx_t[layer, 1], 0, 0)
        ).astype(bf16)
        exs[tw:width] = (
            mm(w_l[layer, 0, 0, 3 * ls : 4 * ls], ctx_l[layer, 0], 0, 0)
            + mm(w_l[layer, 1, 0, 3 * ls : 4 * ls], ctx_l[layer, 1], 0, 0)
        ).astype(bf16)

    def normalize(hidden):
        center = hidden - jnp.mean(hidden, axis=0, keepdims=True)
        scale = lax.rsqrt(jnp.mean(center * center, axis=0, keepdims=True) + norm_epsilon)
        return center * scale, scale

    def norm_forward(layer, n, which, base, hat_ref, finish):
        def block(b):
            lanes = lanes_at(b * LANES, LANES)
            for k, (first, size) in enumerate(streams):
                hidden = base(first, size, lanes) + exchanged(n, first, size, lanes)
                hat, scale = normalize(hidden + column(2, first, size, 3 * which))
                hat_ref[layer, pl.ds(first, size), lanes] = hat.astype(bf16)
                row = 2 * which + k
                stats[layer, row : row + 1, lanes] = scale
                result = hat * column(2, first, size, 3 * which + 1) + column(2, first, size, 3 * which + 2)
                finish(first, size, lanes, result)

        loop(0, blocks, block)

    def first_norm(layer, n):
        def finish(first, size, lanes, result):
            acc[pl.ds(first, size), lanes] = result
            n1b[layer, pl.ds(first, size), lanes] = result.astype(bf16)

        norm_forward(
            layer, n, 0, lambda s, z, lanes: x_fm[layer, pl.ds(s, z), lanes].astype(f32), xh1, finish
        )

    def second_norm(layer, n, dest):
        def finish(first, size, lanes, result):
            dest[pl.ds(first, size), lanes] = result.astype(bf16)

        norm_forward(layer, n, 1, lambda s, z, lanes: acc[pl.ds(s, z), lanes], xh2, finish)

    def gelu_pair(raised):
        cdf = 0.5 * (1.0 + lax.erf(raised * math.sqrt(0.5)))
        slope = cdf + raised * (jnp.exp(-0.5 * raised * raised) * (1.0 / math.sqrt(2.0 * math.pi)))
        return (raised * cdf).astype(bf16), slope.astype(bf16)

    hb = 256
    per_slot = hid_t // hb

    def expand_block(layer, i):
        s, b = lax.div(i, per_slot), lax.rem(i, per_slot)
        rows = lanes_at(b * hb, hb)
        raised = mm(w_t[layer, s, 1, :, rows], n1b[layer, 0:tw], 0, 0) + cols[s, rows, 0:1]
        act[layer, s, rows], gp[layer, s, rows] = gelu_pair(raised)

    def expand_lay(layer, s):
        raised = mm(w_l[layer, s, 1], n1b[layer, tw:width], 0, 0) + cols[s, hid_t : hid_t + hid_l, 0:1]
        act[layer, s, hid_t:], gp[layer, s, hid_t:] = gelu_pair(raised)

    def shrink_partial(layer):
        exs[0:tw] = (
            mm(w_t[layer, 0, 2], act[layer, 0, 0:hid_t], 1, 0) + mm(w_t[layer, 1, 2], act[layer, 1, 0:hid_t], 1, 0)
        ).astype(bf16)
        exs[tw:width] = (
            mm(w_l[layer, 0, 2], act[layer, 0, hid_t:], 1, 0) + mm(w_l[layer, 1, 2], act[layer, 1, hid_t:], 1, 0)
        ).astype(bf16)

    def rows_out(base, text_to, lay_to):
        mine, theirs = xb * half, (1 - xb) * half
        pairs = (
            (rows_t.at[at(mine, half)], rows_t.at[at(theirs, half)], text_to),
            (rows_l.at[:, lanes_at(mine, half)], rows_l.at[:, lanes_at(theirs, half)], lay_to),
        )
        copies = []
        for k, (own, away, dest) in enumerate(pairs):
            copies.append(local_copy(own, dest.at[xb], out_sem.at[base + k, 0]))
            copies.append(
                remote(away, dest.at[xb], out_sem.at[base + k, 1], out_sem.at[base + k, 2], (c, d, t1))
            )
        return copies

    def stage_rows(layer, value):
        @pl.when(c == layer)
        def _():
            rows_t[...] = value[0:tw].T
            rows_l[...] = value[tw:width]

    def send_rows(layer, base, dest_pair, value):
        stage_rows(layer, value)

        @pl.when(c == layer)
        def _():
            start(rows_out(base, *dest_pair))

    def finish_rows(layer, base, dest_pair):
        @pl.when(c == layer)
        def _():
            wait(rows_out(base, *dest_pair))

    out_pair, back_pair = (text_out, lay_out), (text_back, lay_back)
    rows_cross(in_rows)
    fw(0, 0)
    rows_arrive(in_rows)
    x_fm[0, 0:tw] = rows_t[...].T
    fw(0, 1)
    need(0, 0)
    load_columns(0)

    p_store = local_copy(probs, p_keep, p_sem.at[0])
    p_load = local_copy(p_keep, probs, p_sem.at[1])

    for layer in range(2):
        last = layer == 1
        fw(layer, 2)
        need(layer, 1)
        fw(layer, 3)
        need(layer, 2)
        project(layer, 0)
        fw(layer, 4)
        project(layer, 1)
        if last:
            p_store.wait()
        fw(layer, 5)
        head = functools.partial(attend_forward, layer)
        loop(0, 2, head)
        fw(layer, 6)
        loop(2, 4, head)
        fw(layer, 7)
        loop(4, 6, head)
        if last:
            rows_cross(cot_rows)
        else:
            p_store.start()
            rows_begin(cot_rows)
        need(layer, 3)
        attention_partial(layer)
        swap = exchange_copy(2 * layer)
        swap.start()
        fw(layer, 8)
        swap.wait()
        first_norm(layer, 2 * layer)
        fw(layer, 9)
        need(layer, 4, 5, 6, 7)
        expand = functools.partial(expand_block, layer)
        loop(0, per_slot, expand)
        fw(layer, 10)
        if not last:
            need(layer, 8, 9)
            start_second_layer()
        loop(per_slot, 2 * per_slot, expand)
        fw(layer, 11)
        loop(0, 2, functools.partial(expand_lay, layer))
        if last:
            need(layer, 8, 9, 10, 11)
            rows_arrive(cot_rows)
        else:
            need(layer, 10)
            fw(1, 0)
            need(layer, 11)
        shrink_partial(layer)
        swap = exchange_copy(2 * layer + 1)
        swap.start()
        if not last:
            fw(1, 1)
        else:
            g_fm[0:tw] = cot_t[...].T
        swap.wait()
        if not last:
            second_norm(0, 1, x_fm.at[1])
            need(1, 0)
            load_columns(1)
        else:
            second_norm(1, 3, dup.at[0])

    def grad_store(layer, chunk, s):
        return [
            local_copy(stg_t.at[s], gb_t.at[layer, chunk, s], stg_sem.at[s, 0]),
            local_copy(stg_l.at[s], gb_l.at[layer, chunk, s], stg_sem.at[s, 1]),
        ]

    def store_grad(layer, chunk, s, text_value, lay_value):
        stg_t[s] = text_value
        stg_l[s] = lay_value
        start(grad_store(layer, chunk, s))

    groups = (
        (gb_t, rz_t, r1_t, r2_t, ro_t, zs_t, zr_t, zv_t, tv_t, fv_t, w_t, tq),
        (gb_l, rz_l, r1_l, r2_l, ro_l, zs_l, zr_l, zv_l, tv_l, fv_l, w_l, lq),
    )
    tx = t1 + c * (t2 - t1)
    near, far = 2 * zp, 2 * (1 - zp)

    def quarters(first, count, size):
        return at(first * size, count * size)

    def first_sends(layer, chunk, core):
        copies = []
        for g, (gb, rz, r1, r2, ro, zs, zr, zv, tv, fv, w, size) in enumerate(groups):
            if layer == 1:
                parts = [pl.ds(0, 4 * size) if core else quarters(far, 2, size)]
            else:
                parts = [quarters(far, 2, size), quarters(near + core, 1, size)]
            for i, rows in enumerate(parts):
                copies.append(
                    remote(
                        gb.at[layer, chunk, 1 - core, rows], r2.at[chunk, core, rows],
                        s1_send.at[layer, chunk, g, i], s2_recv.at[chunk, core, i, g],
                        (layer, d, t2 if core else t1),
                    )
                )
        return copies

    def own_sends(chunk):
        return [
            remote(gb.at[1, chunk, 0], ro.at[chunk], so_send.at[chunk, g], so_recv.at[chunk, g], other)
            for g, (gb, rz, r1, r2, ro, *_) in enumerate(groups)
        ]

    def pair_sends(layer, chunk):
        return [
            remote(
                gb.at[layer, chunk, 1, quarters(far, 2, size)], rz.at[layer, chunk],
                rz_send.at[layer, chunk, g], rz_recv.at[layer, chunk, g], (1, dz, t),
            )
            for g, (gb, rz, *_, size) in enumerate(groups)
        ]

    def diagonal_sends(layer, chunk):
        copies = []
        for g, (gb, rz, r1, *_, size) in enumerate(groups):
            if layer == 1:
                parts = [(quarters(near, 2, size), (rh_t, rh_l)[g].at[chunk], (0, d, t2))]
            else:
                parts = [(quarters(near + i, 1, size), r1.at[chunk], (1 - i, d, (t1, t2)[i])) for i in range(2)]
            for i, (rows, dest, device) in enumerate(parts):
                copies.append(
                    remote(
                        gb.at[layer, chunk, 1, rows], dest,
                        d_send.at[layer, chunk, g, i], r1_recv.at[layer, chunk, g], device,
                    )
                )
        return copies

    def on(core, task, *args):
        @pl.when(c == core)
        def _():
            task(*args)

    def grads_go(layer, chunk):
        for s in range(2):
            wait(grad_store(layer, chunk, s))
        on(1, lambda: start(pair_sends(layer, chunk) + first_sends(layer, chunk, 1)))
        on(0, lambda: start(first_sends(layer, chunk, 0)))
        if layer == 1:
            on(0, lambda: start(own_sends(chunk)))

    def pair_loads(layer, chunk):
        copies = []
        for g, (gb, rz, r1, r2, ro, zs, zr, zv, tv, fv, w, size) in enumerate(groups):
            copies.append(local_copy(gb.at[layer, chunk, 1, quarters(near, 2, size)], zv.at[0], zv_sem.at[g, 0]))
            copies.append(local_copy(rz.at[layer, chunk], zv.at[1], zv_sem.at[g, 1]))
        return copies

    def pair_stores(layer, chunk):
        return [
            local_copy(zv.at[0], gb.at[layer, chunk, 1, quarters(near, 2, size)], zv_sem.at[g, 2])
            for g, (gb, rz, r1, r2, ro, zs, zr, zv, tv, fv, w, size) in enumerate(groups)
        ]

    def pair_load(layer, chunk):
        @pl.when(c == 1)
        def _():
            for g, (gb, rz, *_) in enumerate(groups):
                landed(rz.at[layer, chunk], rz_recv.at[layer, chunk, g])
            start(pair_loads(layer, chunk))

    def pair_add(layer, chunk):
        @pl.when(c == 1)
        def _():
            wait(pair_loads(layer, chunk))
            for zv in (zv_t, zv_l):
                zv[0] = (zv[0].astype(f32) + zv[1].astype(f32)).astype(bf16)
            start(pair_stores(layer, chunk))

    def pair_send(layer, chunk):
        @pl.when(c == 1)
        def _():
            wait(pair_stores(layer, chunk))
            start(diagonal_sends(layer, chunk))

    def transit_parts(layer, chunk):
        parts = []
        for g, (gb, rz, r1, r2, ro, zs, zr, zv, tv, fv, w, size) in enumerate(groups):
            if layer == 1:
                parts.append((gb.at[1, chunk, 1, quarters(near, 2, size)], (rh_t, rh_l)[g].at[chunk], zv, zv_sem))
            else:
                rows = quarters(near + 1 - c, 1, size)
                parts.append((gb.at[0, chunk, 1 - c, rows], r1.at[chunk], tv, tv_sem))
        return parts

    def transit_loads(layer, chunk):
        copies = []
        for g, (mine, come, held, sem) in enumerate(transit_parts(layer, chunk)):
            copies.append(local_copy(mine, held.at[0], sem.at[g, 0]))
            copies.append(local_copy(come, held.at[1], sem.at[g, 1]))
        return copies

    def transit_stores(layer, chunk):
        return [
            local_copy(held.at[0], mine, sem.at[g, 2])
            for g, (mine, come, held, sem) in enumerate(transit_parts(layer, chunk))
        ]

    def second_sends(layer, chunk):
        copies = []
        for g, (mine, come, held, sem) in enumerate(transit_parts(layer, chunk)):
            gb, rz, r1, r2, *_, size = groups[g]
            if layer == 1:
                dest, device = r2.at[chunk, 0, quarters(near, 2, size)], (1, d, t1)
            else:
                dest, device = r2.at[chunk, c, quarters(near + 1 - c, 1, size)], (0, d, tx)
            way, which = (0, 1) if layer == 1 else (c, 2)
            copies.append(
                remote(mine, dest, s2_send.at[layer, chunk, g], s2_recv.at[chunk, way, which, g], device)
            )
        return copies

    def transit_load(layer, chunk):
        for g, (mine, come, held, sem) in enumerate(transit_parts(layer, chunk)):
            landed(come, r1_recv.at[layer, chunk, g])
        start(transit_loads(layer, chunk))

    def transit_add(layer, chunk):
        wait(transit_loads(layer, chunk))
        for mine, come, held, sem in transit_parts(layer, chunk):
            held[0] = (held[0].astype(f32) + held[1].astype(f32)).astype(bf16)
        start(transit_stores(layer, chunk))

    def transit_send(layer, chunk):
        wait(transit_stores(layer, chunk))
        start(second_sends(layer, chunk))

    def final_loads(layer, chunk, stage):
        copies = []
        for g, (gb, rz, r1, r2, ro, zs, zr, zv, tv, fv, w, size) in enumerate(groups):
            rows = quarters(near if stage else far, 2, size)
            own = ro.at[chunk, rows] if layer == 1 else gb.at[0, chunk, 0, rows]
            terms = [
                (own, w.at[1, 0, chunk, rows]),
                (r2.at[chunk, 0, rows], w.at[1, 1, chunk, rows]),
                (r2.at[chunk, 1, rows], fv.at[chunk, rows]),
            ]
            if z_inside and stage == 1:
                terms.append(((zh_t, zh_l)[g].at[chunk], fv.at[chunk, quarters(far, 2, size)]))
            for i, (src, dst) in enumerate(terms):
                copies.append(local_copy(src, dst, fv_sem.at[chunk, stage, g, i]))
        return copies

    def final_load(layer, chunk, stage):
        @pl.when(c == layer)
        def _():
            for g, (gb, rz, r1, r2, ro, zs, zr, zv, tv, fv, w, size) in enumerate(groups):

                def came(way, first, count, which):
                    landed(r2.at[chunk, way, quarters(first, count, size)], s2_recv.at[chunk, way, which, g])

                if layer == 1 and stage == 0:
                    came(0, far, 2, 0)
                    came(1, 0, 4, 0)
                    landed(ro.at[chunk], so_recv.at[chunk, g])
                elif layer == 1:
                    came(0, near, 2, 1)
                else:
                    for way in range(2):
                        if stage == 0:
                            came(way, far, 2, 0)
                        else:
                            came(way, near + way, 1, 1)
                            came(way, near + 1 - way, 1, 2)
                if z_inside and stage == 1:
                    landed((zh_t, zh_l)[g].at[chunk], zh_recv.at[chunk, g])
            start(final_loads(layer, chunk, stage))

    def half_send(chunk, g):
        gb, rz, r1, r2, ro, zs, zr, zv, tv, fv, w, size = groups[g]
        return remote(
            w.at[1, 0, chunk, quarters(far, 2, size)], (zh_t, zh_l)[g].at[chunk],
            z_send.at[chunk, 0, g], zh_recv.at[chunk, g], (c, dz, t),
        )

    def quarter_send(chunk, i, g, away):
        gb, rz, r1, r2, ro, zs, zr, zv, tv, fv, w, size = groups[g]
        piece, dest = w.at[1, 0, chunk, quarters(near + i, 1, size)], zr.at[chunk, lax.div(d, 2)]
        recv = z_recv.at[chunk, lax.div(d, 2), g]
        if away:
            return remote(piece, dest, z_send.at[chunk, 1 + i, g], recv, (c, near + i, t))
        return local_copy(piece, dest, recv)

    def sum_stores(chunk, stage):
        copies = []
        for g, (gb, rz, r1, r2, ro, zs, zr, zv, tv, fv, w, size) in enumerate(groups):
            rows = quarters(near if stage else far, 2, size)
            copies.append(local_copy(w.at[1, 0, chunk, rows], zs.at[chunk, rows], z_send.at[chunk, stage, g]))
        return copies

    def final_add(layer, chunk, stage):
        @pl.when(c == layer)
        def _():
            wait(final_loads(layer, chunk, stage))
            for gb, rz, r1, r2, ro, zs, zr, zv, tv, fv, w, size in groups:
                rows = quarters(near if stage else far, 2, size)
                total = w[1, 0, chunk, rows].astype(f32) + w[1, 1, chunk, rows].astype(f32)
                total = total + fv[chunk, rows].astype(f32)
                if z_inside and stage == 1:
                    total = total + fv[chunk, quarters(far, 2, size)].astype(f32)
                w[1, 0, chunk, rows] = total.astype(bf16)
            if not z_inside:
                start(sum_stores(chunk, stage))
            elif stage == 0:
                start([half_send(chunk, g) for g in range(2)])
            else:
                for i in range(2):

                    @pl.when(near + i != d)
                    def _():
                        start([quarter_send(chunk, i, g, True) for g in range(2)])

                    @pl.when(near + i == d)
                    def _():
                        start([quarter_send(chunk, i, g, False) for g in range(2)])

    def sums_done():
        for chunk in range(3):
            if not z_inside:
                wait(sum_stores(chunk, 0) + sum_stores(chunk, 1))
                continue
            for g in range(2):
                half_send(chunk, g).wait_send()
                for i in range(2):

                    @pl.when(near + i != d)
                    def _():
                        quarter_send(chunk, i, g, True).wait_send()

                for k in range(2):
                    landed(groups[g][6].at[chunk, k], z_recv.at[chunk, k, g])

    def small_sends(layer):
        zero = [remote(smsg.at[layer, 1], srec.at[0], sm_send.at[layer, 0], sm_recv.at[0], (layer, d, t1))]
        if layer == 1:
            zero.append(remote(smsg.at[1, 0], srec.at[3], sm_send.at[1, 1], sm_recv.at[3], other))
        one = [
            remote(smsg.at[layer, 0], srec.at[1], sm_send.at[layer, 0], sm_recv.at[1], (layer, d, t2)),
            remote(smsg.at[layer, 1], srec.at[2], sm_send.at[layer, 1], sm_recv.at[2], (layer, d, t3)),
        ]
        return zero, one

    def small_go(layer):
        zero, one = small_sends(layer)

        @pl.when(c == 0)
        def _():
            start(zero)

        @pl.when(c == 1)
        def _():
            start(one)

    def small_z():
        if not z_inside:
            return []
        return [
            remote(ssum, szr.at[r - 1], sz_send.at[r - 1], sz_recv.at[r - 1], (c, lax.rem(d + r, dp), t))
            for r in range(1, dp)
        ]

    def small_total(layer):
        @pl.when(c == layer)
        def _():
            for i in range(3):
                landed(srec.at[i], sm_recv.at[i])
            if layer == 1:
                landed(srec.at[3], sm_recv.at[3])
                own = srec[3]
            else:
                own = smsg[0, 0]
            ssum[...] = own + srec[0] + srec[1] + srec[2]
            start(small_z())

    def row_sums(ref):
        return mm(ones, ref[...], 1, 1)[0:1]

    def vector_sum(layer, row, value):
        for s in range(2):
            smsg[layer, s, 8 + row : 9 + row, 0:width] = value

    def norm_backward(layer, which, hat_ref, incoming):
        def block(b):
            lanes = lanes_at(b * LANES, LANES)
            for k, (first, size) in enumerate(streams):
                grad = incoming(first, size, lanes)
                hat = hat_ref[layer, pl.ds(first, size), lanes].astype(f32)
                row = 2 * which + k
                scale = stats[layer, row : row + 1, lanes]
                gained = grad * column(2, first, size, 3 * which + 1)
                mean_grad = jnp.mean(gained, axis=0, keepdims=True)
                mean_both = jnp.mean(gained * hat, axis=0, keepdims=True)
                result = scale * (gained - mean_grad - hat * mean_both)
                acc[pl.ds(first, size), lanes] = result
                tmpb[pl.ds(first, size), lanes] = result.astype(bf16)
                exs[pl.ds(first, size), lanes] = (grad * hat).astype(bf16)
                g_fm[pl.ds(first, size), lanes] = grad.astype(bf16)

        loop(0, blocks, block)

    def norm_sums(layer, which):
        vector_sum(layer, 3 * which + 1, row_sums(exs))
        vector_sum(layer, 3 * which + 2, row_sums(g_fm))
        vector_sum(layer, 3 * which, row_sums(tmpb))

    def ffn_backward(layer):
        def text_block(i):
            s, b = lax.div(i, per_slot), lax.rem(i, per_slot)
            rows = lanes_at(b * hb, hb)
            back = mm(w_t[layer, s, 2, :, rows], tmpb[0:tw], 0, 0)
            dup[s, rows] = (back * gp[layer, s, rows].astype(f32)).astype(bf16)

        loop(0, 2 * per_slot, text_block)

        def lay_block(s):
            back = mm(w_l[layer, s, 2], tmpb[tw:width], 0, 0)
            dup[s, hid_t:] = (back * gp[layer, s, hid_t:].astype(f32)).astype(bf16)

        loop(0, 2, lay_block)

    def shrink_grads(layer, s):
        store_grad(
            layer, 2, s,
            mm(tmpb[0:tw], act[layer, s, 0:hid_t], 1, 1).astype(bf16),
            mm(tmpb[tw:width], act[layer, s, hid_t:], 1, 1).astype(bf16),
        )

    def expand_grads(layer, s):
        store_grad(
            layer, 1, s,
            mm(n1b[layer, 0:tw], dup[s, 0:hid_t], 1, 1).astype(bf16),
            mm(n1b[layer, tw:width], dup[s, hid_t:], 1, 1).astype(bf16),
        )

    def expand_partial(layer):
        exs[0:tw] = (
            mm(w_t[layer, 0, 1], dup[0, 0:hid_t], 1, 0) + mm(w_t[layer, 1, 1], dup[1, 0:hid_t], 1, 0)
        ).astype(bf16)
        exs[tw:width] = (
            mm(w_l[layer, 0, 1], dup[0, hid_t:], 1, 0) + mm(w_l[layer, 1, 1], dup[1, hid_t:], 1, 0)
        ).astype(bf16)

    def context_grads(layer, s):
        dup[s, 0:hs] = mm(w_t[layer, s, 0, 3 * hs : 4 * hs], tmpb[0:tw], 1, 0).astype(bf16)
        dup[s, hs : hs + ls] = mm(w_l[layer, s, 0, 3 * ls : 4 * ls], tmpb[tw:width], 1, 0).astype(bf16)

    def attend_backward(layer, i):
        s, h = lax.div(i, heads), lax.rem(i, heads)
        queries = query(layer, s, h)
        key_text, key_lay = head_rows(layer, s, 1, h)
        keys = jnp.concatenate([key_text * HEAD**-0.5, key_lay * LHEAD**-0.5], axis=0).astype(bf16)
        values = jnp.concatenate(head_rows(layer, s, 2, h), axis=0)
        grads = jnp.concatenate([dup[s, at(h * HEAD, HEAD)], dup[s, at(hs + h * LHEAD, LHEAD)]], axis=0)
        low = probs[i]
        prob = low.astype(f32)
        dprob = mm(values, grads, 0, 0)
        inner = jnp.sum(dprob * prob, axis=0, keepdims=True)
        dscore = (prob * (dprob - inner)).astype(bf16)
        results = (mm(keys, dscore, 1, 0), mm(queries, dscore, 1, 1), mm(grads, low, 1, 1))
        for part, result in enumerate(results):
            result = result.astype(bf16)
            dqkv[s, at(part * hs + h * HEAD, HEAD)] = result[0:HEAD]
            dqkv[s, at(3 * hs + part * ls + h * LHEAD, LHEAD)] = result[HEAD:]

    def attend_grads(layer, s):
        text = jnp.concatenate(
            [mm(x_fm[layer, 0:tw], dqkv[s, 0 : 3 * hs], 1, 1), mm(tmpb[0:tw], ctx_t[layer, s], 1, 1)], axis=1
        )
        lay = jnp.concatenate(
            [mm(x_fm[layer, tw:width], dqkv[s, 3 * hs :], 1, 1), mm(tmpb[tw:width], ctx_l[layer, s], 1, 1)], axis=1
        )
        store_grad(layer, 0, s, text.astype(bf16), lay.astype(bf16))

    def attend_partial(layer):
        exs[0:tw] = (
            mm(w_t[layer, 0, 0, 0 : 3 * hs], dqkv[0, 0 : 3 * hs], 0, 0)
            + mm(w_t[layer, 1, 0, 0 : 3 * hs], dqkv[1, 0 : 3 * hs], 0, 0)
        ).astype(bf16)
        exs[tw:width] = (
            mm(w_l[layer, 0, 0, 0 : 3 * ls], dqkv[0, 3 * hs :], 0, 0)
            + mm(w_l[layer, 1, 0, 0 : 3 * ls], dqkv[1, 3 * hs :], 0, 0)
        ).astype(bf16)

    def small_sums(layer, s, row, ref, size):
        smsg[layer, s, row : row + 1, 0:size] = mm(ones, ref[s], 1, 1)[0:1]

    def first_grad(n, first, size, lanes):
        return acc[pl.ds(first, size), lanes] + exchanged(n, first, size, lanes)

    def gather_sent():
        for layer in range(2):

            @pl.when(c == layer)
            def _():
                for p in all_pieces:
                    own_first(p).wait_send()
                    if layer == 1:
                        own_core(p).wait_send()

            @pl.when(c == zp)
            def _():
                for p in all_pieces:
                    for copy in forwards(layer, p):
                        copy.wait_send()

    def run(*tasks):
        for task in tasks:
            task[0](*task[1:])

    Z, T, F = (pair_load, pair_add, pair_send), (transit_load, transit_add, transit_send), (final_load, final_add)
    service = {
        (1, "context"): [(Z[0], 1, 2)],
        (1, "heads 0"): [(Z[1], 1, 2)],
        (1, "heads 1"): [(Z[2], 1, 2), (Z[0], 1, 1)],
        (1, "heads 2"): [(Z[1], 1, 1)],
        (1, "attend grads"): [(Z[2], 1, 1)],
        (0, "begin"): [(gather_sent,), (F[0], 1, 2, 0)],
        (0, "second norm"): [(F[1], 1, 2, 0)],
        (0, "shrink grads"): [(Z[0], 1, 0), (F[0], 1, 1, 0)],
        (0, "ffn"): [(Z[1], 1, 0)],
        (0, "expand grads"): [(Z[2], 1, 0), (on, 0, T[0], 1, 2)],
        (0, "ffn swap"): [(on, 0, T[1], 1, 2), (F[1], 1, 1, 0)],
        (0, "first norm"): [(on, 0, T[2], 1, 2), (on, 0, T[0], 1, 1), (Z[0], 0, 2)],
        (0, "context"): [(on, 0, T[1], 1, 1), (Z[1], 0, 2)],
        (0, "heads 0"): [(on, 0, T[2], 1, 1), (Z[2], 0, 2)],
        (0, "heads 2"): [(Z[0], 0, 1)],
        (0, "attend grads"): [(Z[1], 0, 1)],
        (0, "swap"): [(Z[2], 0, 1), (F[0], 1, 0, 0)],
        (0, "finished"): [(F[1], 1, 0, 0)],
    }

    for layer in (1, 0):
        last = layer == 0
        n = 4 + 2 * (1 - layer)

        def point(name):
            run(*service.get((layer, name), []))

        if last:
            load_columns(0)
        point("begin")
        norm_backward(layer, 1, xh2, lambda s, z, lanes: g_fm[pl.ds(s, z), lanes].astype(f32))
        point("second norm")
        for s in range(2):
            shrink_grads(layer, s)
        norm_sums(layer, 1)
        grads_go(layer, 2)
        if not last:
            send_rows(0, 0, out_pair, x_fm.at[1])
            send_rows(1, 0, out_pair, dup.at[0])
        point("shrink grads")
        ffn_backward(layer)
        point("ffn")
        for s in range(2):
            expand_grads(layer, s)
        point("expand grads")
        expand_partial(layer)
        swap = exchange_copy(n)
        swap.start()
        for s in range(2):
            small_sums(layer, s, 0, dup, hid_t + hid_l)
        grads_go(layer, 1)
        point("ffn swap")
        swap.wait()
        norm_backward(layer, 0, xh1, functools.partial(first_grad, n))
        norm_sums(layer, 0)
        point("first norm")
        if last:
            p_load.wait()
        for s in range(2):
            context_grads(layer, s)
        point("context")
        head = functools.partial(attend_backward, layer)
        for i in range(3):
            loop(2 * i, 2 * i + 2, head)
            point(f"heads {i}")
        if not last:
            p_load.start()
        for s in range(2):
            attend_grads(layer, s)
        point("attend grads")
        attend_partial(layer)
        swap = exchange_copy(n + 1)
        swap.start()
        for s in range(2):
            small_sums(layer, s, 1, dqkv, 3 * hs + 3 * ls)
        small_go(layer)
        grads_go(layer, 0)
        point("swap")
        swap.wait()
        point("swapped")

        def finish(b):
            lanes = lanes_at(b * LANES, LANES)
            for first, size in streams:
                g_fm[pl.ds(first, size), lanes] = first_grad(n + 1, first, size, lanes).astype(bf16)

        loop(0, blocks, finish)
        point("finished")
        finish_rows(layer, 0, out_pair)
        stage_rows(layer, g_fm)

    def transit(layer, chunk):
        run(*((step, layer, chunk) for step in T))

    def final(layer, chunk, stage):
        run(*((step, layer, chunk, stage) for step in F))

    @pl.when(c == 0)
    def _():
        run((final, 0, 2, 0), (transit, 1, 0), (final, 0, 1, 0), (transit, 0, 2), (final, 0, 0, 0))
        run((transit, 0, 1), (transit, 0, 0))
        start(rows_out(2, *back_pair))
        run((final, 0, 2, 1), (final, 0, 1, 1), (small_total, 0), (final, 0, 0, 1))

    @pl.when(c == 1)
    def _():
        run(*((step, 0, 0) for step in Z), (transit, 0, 2), (final, 1, 2, 1), (transit, 0, 1), (final, 1, 1, 1))
        run((small_total, 1), (transit, 0, 0))
        start(rows_out(2, *back_pair))
        run((final, 1, 0, 1))

    for copy in small_z():
        copy.wait()
    if z_inside:
        for r in range(1, dp):
            ssum[...] = ssum[...] + szr[r - 1]
    sm_copy = local_copy(ssum, sm_out, so_sem.at[0])
    sm_copy.start()
    wait(rows_out(2, *back_pair))
    for layer in range(2):
        smalls = small_sends(layer)
        for core in range(2):

            @pl.when(c == core)
            def _():
                for copy in smalls[core]:
                    copy.wait_send()
                for chunk in range(3):
                    copies = first_sends(layer, chunk, core)
                    if core == 1:
                        copies += pair_sends(layer, chunk) + diagonal_sends(layer, chunk)
                    elif layer == 1:
                        copies += own_sends(chunk)
                    if core == 0 or layer == 0:
                        copies += second_sends(layer, chunk)
                    for copy in copies:
                        copy.wait_send()

    sums_done()
    sm_copy.wait()


def finishing(
    parts_t, parts_l, sums_in, rows_in_0, rows_in_1, rows_in_2, rows_in_3,
    rows_0, rows_1, rows_2, rows_3, att_t, out_t, exp_t, shr_t, att_l, out_l, exp_l, shr_l,
    bias_t, off_t, vec_t, bias_l, off_l, vec_l,
    zr_t, zr_l, sums, held_0, held_1, held_2, held_3, sems,
):
    pairs = ((rows_in_0, held_0), (rows_in_1, held_1), (rows_in_2, held_2), (rows_in_3, held_3))
    pairs += ((parts_t, zr_t), (parts_l, zr_l), (sums_in, sums))
    loads = [pltpu.make_async_copy(src, dst, sems.at[i]) for i, (src, dst) in enumerate(pairs)]
    for copy in loads:
        copy.start()
    pairs = ((held_0, rows_0), (held_1, rows_1), (held_2, rows_2), (held_3, rows_3))
    copies = [pltpu.make_async_copy(src, dst, sems.at[7 + i]) for i, (src, dst) in enumerate(pairs)]
    for load, copy in zip(loads[:4], copies):
        load.wait()
        copy.start()
    for load in loads[4:]:
        load.wait()
    for zr, att, out, exp, shr in ((zr_t, att_t, out_t, exp_t, shr_t), (zr_l, att_l, out_l, exp_l, shr_l)):
        totals = []
        for chunk in range(3):
            total = zr[chunk, 0].astype(f32)
            for r in range(1, zr.shape[1]):
                total = total + zr[chunk, r].astype(f32)
            totals.append(total)
        size = out.shape[1]
        for j in range(3):
            att[j] = totals[0][:, j * size : (j + 1) * size]
        out[...] = totals[0][:, 3 * size : 4 * size]
        exp[...] = totals[1]
        shr[...] = totals[2]
    hs, ls = bias_t.shape[1], bias_l.shape[1]
    ft, fl = off_t.shape[1], off_l.shape[1]
    tw, lw = vec_t.shape[2], vec_l.shape[2]
    off_t[...] = sums[0:1, 0:ft]
    off_l[...] = sums[0:1, ft : ft + fl]
    bias_t[0:1] = sums[1:2, 0:hs]
    bias_t[1:2] = sums[1:2, 2 * hs : 3 * hs]
    bias_l[0:1] = sums[1:2, 3 * hs : 3 * hs + ls]
    bias_l[1:2] = sums[1:2, 3 * hs + 2 * ls : 3 * hs + 3 * ls]
    for row in range(6):
        vec_t[row] = sums[8 + row : 9 + row, 0:tw]
        vec_l[row] = sums[8 + row : 9 + row, tw : tw + lw]
    for copy in copies:
        copy.wait()


def local(
    dp,
    text_in,
    layout_in,
    text_cot,
    layout_cot,
    lengths,
    text_attend,
    text_biases,
    text_output,
    text_expand,
    text_offset,
    text_shrink,
    text_vectors,
    layout_attend,
    layout_biases,
    layout_output,
    layout_expand,
    layout_offset,
    layout_shrink,
    layout_vectors,
):
    rows, tw = text_in.shape[1:]
    lw = layout_in.shape[2]
    width, tokens = tw + lw, 2 * rows
    hs, ls = text_output.shape[2], layout_output.shape[2]
    ft, fl = text_expand.shape[2], layout_expand.shape[2]
    zt, zl = tw // dp, lw // dp
    z_inside = dp == 4

    def shape(dims, dtype=bf16):
        return jax.ShapeDtypeStruct(dims, dtype)

    def attend_rows(attend):
        return attend[0].transpose(1, 2, 0).reshape(-1, attend.shape[1])

    hbm = pl.BlockSpec(memory_space=pltpu.HBM)
    vmem = pl.BlockSpec(memory_space=pltpu.VMEM)
    heads = hs // HEAD
    row_shapes = [shape((2, rows, tw)), shape((2, lw, rows)), shape((2, rows, tw)), shape((2, lw, rows))]
    out_shape = row_shapes + [
        shape((16, SMALL), f32),
        shape((3, tw, tw)), shape((3, lw, lw)),
        shape((3, 2, tw // 4, tw)), shape((3, 2, lw // 4, lw)), shape((3, tw // 2, tw)), shape((3, lw // 2, lw)),
        shape((2, 3, 2, tw, tw)), shape((2, 3, 2, lw, lw)),
        shape((2, 3, tw // 2, tw)), shape((2, 3, lw // 2, lw)), shape((3, tw // 2, tw)), shape((3, lw // 2, lw)),
        shape((3, tw // 4, tw)), shape((3, lw // 4, lw)),
        shape((3, 2, tw, tw)), shape((3, 2, lw, lw)),
        shape((3, tw, tw)), shape((3, lw, lw)),
        shape((2 * heads, tokens, tokens)),
    ]
    dma = pltpu.SemaphoreType.DMA
    scratch = [
        pltpu.VMEM((2, 2, 3, tw, tw), bf16),
        pltpu.VMEM((2, 2, 3, lw, lw), bf16),
        pltpu.VMEM((2, 2, 16, SMALL), bf16),
        pltpu.VMEM((2, 16, SMALL), f32),
        pltpu.VMEM((16, SMALL), bf16),
        pltpu.VMEM((16, SMALL), f32),
        pltpu.VMEM((tokens, LANES), f32),
        pltpu.VMEM((tokens, tw), bf16),
        pltpu.VMEM((lw, tokens), bf16),
        pltpu.VMEM((2, width, tokens), bf16),
        pltpu.VMEM((2, 2, 3 * hs, tokens), bf16),
        pltpu.VMEM((2, 2, 3 * ls, tokens), bf16),
        pltpu.VMEM((2 * heads, tokens, tokens), bf16),
        pltpu.VMEM((2, 2, hs, tokens), bf16),
        pltpu.VMEM((2, 2, ls, tokens), bf16),
        pltpu.VMEM((2, width, tokens), bf16),
        pltpu.VMEM((2, width, tokens), bf16),
        pltpu.VMEM((2, width, tokens), bf16),
        pltpu.VMEM((2, 2, ft + fl, tokens), bf16),
        pltpu.VMEM((2, 2, ft + fl, tokens), bf16),
        pltpu.VMEM((2, 8, tokens), f32),
        pltpu.VMEM((width, tokens), f32),
        pltpu.VMEM((width, tokens), bf16),
        pltpu.VMEM((2, width, tokens), bf16),
        pltpu.VMEM((width, tokens), bf16),
        pltpu.VMEM((width, tokens), bf16),
        pltpu.VMEM((2, ft + fl, tokens), bf16),
        pltpu.VMEM((2, 3 * hs + 3 * ls, tokens), bf16),
        pltpu.VMEM((3, SMALL, 16), f32),
        pltpu.VMEM((2, tw, tw), bf16),
        pltpu.VMEM((2, lw, lw), bf16),
        pltpu.VMEM((2, tw // 2, tw), bf16),
        pltpu.VMEM((2, lw // 2, lw), bf16),
        pltpu.VMEM((2, tw // 4, tw), bf16),
        pltpu.VMEM((2, lw // 4, lw), bf16),
        pltpu.VMEM((3, tw, tw), bf16),
        pltpu.VMEM((3, lw, lw), bf16),
        pltpu.VMEM((2, 2, 16, SMALL), f32),
        pltpu.VMEM((4, 16, SMALL), f32),
        pltpu.VMEM((16, SMALL), f32),
        pltpu.VMEM((3, 16, SMALL), f32),
        dma((2, 2, 17)), dma((17, 2)), dma((2, 17, 2)), dma((3,)), dma((4, 5)), dma((8,)), dma((8,)),
        dma((4, 3)), dma((2, 2)), dma((2,)),
        dma((2, 3, 2)), dma((2, 3, 2)), dma((2, 3, 2, 2)), dma((2, 3, 2, 2)), dma((2, 3, 2)), dma((2, 3, 2)),
        dma((3, 2, 3, 2)), dma((3, 2)), dma((3, 2)), dma((3, 3, 2)), dma((3, 2, 2)), dma((3, 2)),
        dma((2, 3)), dma((2, 3)), dma((3, 2, 2, 4)),
        dma((2, 2)), dma((4,)), dma((3,)), dma((3,)), dma((1,)),
    ]
    results = pl.pallas_call(
        functools.partial(kernel, dp, z_inside),
        out_shape=out_shape,
        in_specs=[hbm] * 12 + [vmem] * 6 + [pl.BlockSpec(memory_space=pltpu.SMEM)],
        out_specs=[hbm] * len(out_shape),
        scratch_shapes=scratch,
        compiler_params=pltpu.CompilerParams(
            collective_id=0, has_side_effects=True, vmem_limit_bytes=63 * 1024 * 1024
        ),
    )(
        text_in, layout_in.transpose(0, 2, 1), text_cot, layout_cot.transpose(0, 2, 1),
        attend_rows(text_attend), text_output[0].T, text_expand[0], text_shrink[0],
        attend_rows(layout_attend), layout_output[0].T, layout_expand[0], layout_shrink[0],
        text_biases[0], layout_biases[0], text_offset, layout_offset, text_vectors[0], layout_vectors[0], lengths,
    )
    row_results, sums = results[:4], results[4]
    if z_inside:
        parts_t, parts_l = results[7], results[8]
    else:
        parts_t = lax.psum_scatter(results[5], "dp", scatter_dimension=1, tiled=True)[:, None]
        parts_l = lax.psum_scatter(results[6], "dp", scatter_dimension=1, tiled=True)[:, None]
        sums = lax.psum(sums, "dp")
    final_shapes = row_shapes + [
        shape((3, zt, hs), f32), shape((zt, hs), f32), shape((zt, ft), f32), shape((zt, ft), f32),
        shape((3, zl, ls), f32), shape((zl, ls), f32), shape((zl, fl), f32), shape((zl, fl), f32),
        shape((2, hs), f32), shape((1, ft), f32), shape((6, 1, tw), f32),
        shape((2, ls), f32), shape((1, fl), f32), shape((6, 1, lw), f32),
    ]
    (
        text_out, lay_out, text_back, lay_back, att_t, out_t, exp_t, shr_t, att_l, out_l, exp_l, shr_l,
        bias_t, off_t, vec_t, bias_l, off_l, vec_l,
    ) = pl.pallas_call(
        finishing,
        out_shape=final_shapes,
        in_specs=[hbm] * 7,
        out_specs=[hbm] * 4 + [vmem] * 14,
        scratch_shapes=[
            pltpu.VMEM(parts_t.shape, bf16), pltpu.VMEM(parts_l.shape, bf16), pltpu.VMEM((16, SMALL), f32),
            *(pltpu.VMEM(rows.shape, bf16) for rows in row_shapes), dma((11,)),
        ],
        compiler_params=pltpu.CompilerParams(vmem_limit_bytes=62 * 1024 * 1024),
    )(parts_t, parts_l, sums, *row_results)
    return (
        text_out[None],
        lay_out.transpose(0, 2, 1)[None],
        text_back[None],
        lay_back.transpose(0, 2, 1)[None],
        att_t.transpose(1, 0, 2)[None],
        bias_t[None],
        out_t[None],
        exp_t[None],
        off_t,
        shr_t[None],
        vec_t.transpose(1, 0, 2),
        att_l.transpose(1, 0, 2)[None],
        bias_l[None],
        out_l[None],
        exp_l[None],
        off_l,
        shr_l[None],
        vec_l.transpose(1, 0, 2),
    )


def solution(mesh):
    return jax.shard_map(
        functools.partial(local, mesh.shape["dp"]),
        mesh=mesh,
        in_specs=(
            P(None, ("dp", "tensor"), None),
            P(None, ("dp", "tensor"), None),
            P(None, ("dp", "tensor"), None),
            P(None, ("dp", "tensor"), None),
            P(None, "dp"),
            P("section", None, None, "tensor"),
            P("section", None, "tensor"),
            P("section", None, "tensor"),
            P("section", None, "tensor"),
            P("section", "tensor"),
            P("section", None, "tensor"),
            P("section", None, None),
            P("section", None, None, "tensor"),
            P("section", None, "tensor"),
            P("section", None, "tensor"),
            P("section", None, "tensor"),
            P("section", "tensor"),
            P("section", None, "tensor"),
            P("section", None, None),
        ),
        out_specs=(
            P("section", None, ("dp", "tensor"), None),
            P("section", None, ("dp", "tensor"), None),
            P("section", None, ("dp", "tensor"), None),
            P("section", None, ("dp", "tensor"), None),
            P("section", "dp", None, "tensor"),
            P("section", None, "tensor"),
            P("section", "dp", "tensor"),
            P("section", "dp", "tensor"),
            P("section", "tensor"),
            P("section", "dp", "tensor"),
            P("section", None, None),
            P("section", "dp", None, "tensor"),
            P("section", None, "tensor"),
            P("section", "dp", "tensor"),
            P("section", "dp", "tensor"),
            P("section", "tensor"),
            P("section", "dp", "tensor"),
            P("section", None, None),
        ),
        check_vma=False,
    )
```

```python
import functools
import math

import jax
import jax.numpy as jnp
from jax import lax
from jax.experimental import pallas as pl
from jax.experimental.pallas import tpu as pltpu
from jax.sharding import PartitionSpec as P

HEAD = 64
LHEAD = 16
MESH = pl.DeviceIdType.MESH
bf16 = jnp.bfloat16
f32 = jnp.float32
norm_epsilon = 1e-05
masked_score = -1e30
LANES = 128
SMALL = 1024
STEPS = 12


def mm(left, right, left_axis, right_axis):
    return lax.dot_general(
        left, right, (((left_axis,), (right_axis,)), ((), ())), preferred_element_type=f32
    )


def flip(index, bit):
    return index + bit - 2 * bit * lax.rem(lax.div(index, bit), 2)


def loop(start, stop, body):
    lax.fori_loop(start, stop, lambda i, carry: (body(i), carry)[1], 0)


def at(start, size):
    return pl.ds(pl.multiple_of(start, 16), size)


def lanes_at(start, size):
    return pl.ds(pl.multiple_of(start, LANES), size)


def kernel(
    dp,
    z_inside,
    text_in, lay_in, text_cot, lay_cot, att_t, out_t, exp_t, shr_t, att_l, out_l, exp_l, shr_l,
    bias_t, bias_l, off_t, off_l, vec_t, vec_l, lengths,
    text_out, lay_out, text_back, lay_back, sm_out,
    zs_t, zs_l, zr_t, zr_l, zh_t, zh_l, gb_t, gb_l, rz_t, rz_l, rh_t, rh_l, r1_t, r1_l, r2_t, r2_l, ro_t, ro_l, p_keep,
    w_t, w_l, small, vecs, own_small, own_vec, key_bias, rows_t, rows_l, x_fm, qkv_t, qkv_l, probs,
    ctx_t, ctx_l, xh1, n1b, xh2, act, gp, stats, acc, exs, exr, tmpb, g_fm, dup, dqkv, cols,
    stg_t, stg_l, zv_t, zv_l, tv_t, tv_l, fv_t, fv_l, smsg, srec, ssum, szr,
    ag_recv, ag_own, ag_fwd, vec_sem, row_sem, ex_send, ex_recv, out_sem, stg_sem, p_sem,
    rz_send, rz_recv, s1_send, d_send, r1_recv, s2_send, s2_recv, so_send, so_recv, z_send, z_recv, zh_recv,
    zv_sem, tv_sem, fv_sem,
    sm_send, sm_recv, sz_send, sz_recv, so_sem,
):
    c = lax.axis_index("section")
    d = lax.axis_index("dp")
    t = lax.axis_index("tensor")
    t1, t2 = flip(t, 1), flip(t, 2)
    t3 = flip(t1, 2)
    xb = lax.rem(t, 2)
    zp = lax.rem(d, 2)
    tf = t1 + zp * (t2 - t1)
    td = t2 + zp * (t1 - t2)
    dz = flip(d, 1)
    tw = text_in.shape[2]
    lw = lay_in.shape[1]
    width = tw + lw
    tokens = x_fm.shape[2]
    half = tokens // 2
    quarter = tokens // 4
    hid_t, hid_l = exp_t.shape[1], exp_l.shape[1]
    hs, ls = out_t.shape[0], out_l.shape[0]
    heads = hs // HEAD
    blocks = tokens // LANES
    tq, lq = tw // 4, lw // 4
    streams = ((0, tw), (tw, lw))
    z_peers = [lax.rem(d + r, dp) for r in range(1, dp)] if z_inside else [dz]

    def on(core, task, *args):
        @pl.when(c == core)
        def _():
            task(*args)

    def remote(src, dst, send, recv, device):
        return pltpu.make_async_remote_copy(
            src_ref=src, dst_ref=dst, send_sem=send, recv_sem=recv, device_id=device, device_id_type=MESH
        )

    def local_copy(src, dst, sem):
        return pltpu.make_async_copy(src, dst, sem)

    def landed(ref, sem):
        pltpu.make_async_copy(ref, ref, sem).wait()

    def start(copies):
        for copy in copies:
            copy.start()

    def wait(copies):
        for copy in copies:
            copy.wait()

    barrier = pltpu.get_barrier_semaphore()
    peers = [(1 - c, d, t)] + [(k, d, other) for other in (t1, t2, t3) for k in range(2)] + [(c, z, t) for z in z_peers]
    for peer in peers:
        pl.semaphore_signal(barrier, inc=1, device_id=peer, device_id_type=MESH)

    own_vec[...] = jnp.zeros(own_vec.shape, f32)
    own_vec[0:1, 0:hid_t] = off_t[...].astype(f32)
    own_vec[0:1, hid_t : hid_t + hid_l] = off_l[...].astype(f32)
    own_vec[1:2, 0:hs] = bias_t[0:1].astype(f32)
    own_vec[1:2, 2 * hs : 3 * hs] = bias_t[1:2].astype(f32)
    own_vec[1:2, 3 * hs : 3 * hs + ls] = bias_l[0:1].astype(f32)
    own_vec[1:2, 3 * hs + 2 * ls : 3 * hs + 3 * ls] = bias_l[1:2].astype(f32)
    own_small[...] = own_vec[...].astype(bf16)
    own_vec[0:6, 0:tw] = vec_t[...].astype(f32)
    own_vec[0:6, tw:width] = vec_l[...].astype(f32)
    pl.semaphore_wait(barrier, len(peers))
    other = (1 - c, d, t)

    def row_copies(text, lay, text_to, lay_to, base):
        mine, theirs = xb * half, (1 - xb) * half
        part = c * quarter
        own = [
            local_copy(text.at[xb], text_to.at[at(mine, half)], row_sem.at[base, 0]),
            local_copy(lay.at[xb], lay_to.at[:, lanes_at(mine, half)], row_sem.at[base + 1, 0]),
        ]
        away = [
            remote(
                text.at[1 - xb, at(part, quarter)], text_to.at[at(mine + part, quarter)],
                row_sem.at[base, 1], row_sem.at[base, 2], (c, d, t1),
            ),
            remote(
                lay.at[1 - xb, :, lanes_at(part, quarter)], lay_to.at[:, lanes_at(mine + part, quarter)],
                row_sem.at[base + 1, 1], row_sem.at[base + 1, 2], (c, d, t1),
            ),
        ]
        text_part = text_to.at[at(theirs + part, quarter)]
        lay_part = lay_to.at[:, lanes_at(theirs + part, quarter)]
        across = [
            remote(text_part, text_part, row_sem.at[base, 3], row_sem.at[base, 4], other),
            remote(lay_part, lay_part, row_sem.at[base + 1, 3], row_sem.at[base + 1, 4], other),
        ]
        return own, away, across

    cot_t = fv_t.at[0, pl.ds(0, tokens)]
    in_rows = row_copies(text_in, lay_in, rows_t, x_fm.at[0, pl.ds(tw, lw)], 0)
    cot_rows = row_copies(text_cot, lay_cot, cot_t, g_fm.at[pl.ds(tw, lw)], 2)

    def rows_begin(copies):
        own, away, across = copies
        start(away + own)

    def rows_cross(copies):
        own, away, across = copies
        wait(away)
        start(across)

    def rows_arrive(copies):
        own, away, across = copies
        wait(own + across)

    text_sources = [att_t.at[pl.ds(j * hs, hs)] for j in range(3)] + [out_t]
    text_sources += [exp_t.at[pl.ds(j * hs, hs)] for j in range(4)] + [shr_t.at[pl.ds(j * hs, hs)] for j in range(4)]
    lay_sources = {12: att_l, 13: out_l, 14: exp_l, 15: shr_l}
    lay_places = {12: (0, 0, 3 * ls), 13: (0, 3 * ls, ls), 14: (1, 0, lw), 15: (2, 0, lw)}
    riders = {0: [12, 16], 3: [13], 4: [14], 8: [15]}

    def source(p):
        if p < STEPS:
            return text_sources[p]
        return lay_sources[p] if p < 16 else own_small

    def place(layer, slot, p):
        if p < STEPS:
            return w_t.at[layer, slot, p // 4, pl.ds((p % 4) * hs, hs)]
        if p < 16:
            which, first, size = lay_places[p]
            return w_l.at[layer, slot, which, pl.ds(first, size)]
        return small.at[layer, slot]

    def pieces(j):
        return [j] + riders.get(j, [])

    all_pieces = [p for j in range(STEPS) for p in pieces(j)]

    def own_first(p):
        return remote(
            source(p), place(c, 1 - zp, p), ag_own.at[p, 0], ag_recv.at[c, 1 - zp, p], (zp, d, tf)
        )

    def own_core(p):
        return remote(source(p), place(1, 0, p), ag_own.at[p, 1], ag_recv.at[1, 0, p], (0, d, t))

    def own_local(p):
        return local_copy(source(p), place(0, 0, p), ag_recv.at[0, 0, p])

    def forwards(layer, p):
        return [
            remote(
                place(layer, 1 - zp, p), place(layer, 1, p),
                ag_fwd.at[p, 0], ag_recv.at[layer, 1, p], (1, d, td),
            ),
            remote(
                place(layer, 1 - zp, p), place(layer, 1 - zp, p),
                ag_fwd.at[p, 1], ag_recv.at[layer, 1 - zp, p], (zp, dz, t),
            ),
        ]

    def fw(layer, *steps):
        @pl.when(c == zp)
        def _():
            for j in steps:
                for p in pieces(j):
                    landed(place(layer, 1 - zp, p), ag_recv.at[layer, 1 - zp, p])
                    if layer == 1:
                        for copy in forwards(0, p):
                            copy.wait_send()
                    start(forwards(layer, p))

    def need(layer, *steps):
        for j in steps:
            for p in pieces(j):
                landed(place(layer, zp, p), ag_recv.at[layer, zp, p])

        @pl.when(c != zp)
        def _():
            for j in steps:
                for p in pieces(j):
                    landed(place(layer, 1 - zp, p), ag_recv.at[layer, 1 - zp, p])

    vec_copies = [
        local_copy(own_vec, vecs.at[c], vec_sem.at[0]),
        remote(own_vec, vecs.at[c], vec_sem.at[1], vec_sem.at[2], other),
    ]

    early = [p for j in range(3) for p in pieces(j)]

    @pl.when(c == 0)
    def _():
        start([own_first(p) for p in early])

    rows_begin(in_rows)
    start(vec_copies)

    @pl.when(c == 0)
    def _():
        start([own_first(p) for p in all_pieces if p not in early])

    @pl.when(c == 0)
    def _():
        start([own_local(p) for p in all_pieces])

    @pl.when(c == 1)
    def _():
        start([own_core(p) for p in all_pieces])

    def start_second_layer():
        @pl.when(c == 1)
        def _():
            start([own_first(p) for p in all_pieces])

    page_len = lengths[xb, lax.div(t, 2)]
    positions = lax.broadcasted_iota(jnp.int32, key_bias.shape, 0)
    key_bias[...] = jnp.where(positions < page_len, 0.0, masked_score).astype(f32)
    smsg[...] = jnp.zeros(smsg.shape, f32)
    ones = jnp.ones((8, tokens), bf16)
    wait(vec_copies)

    def load_columns(layer):
        for k in range(2):
            cols[k] = small[layer, k].astype(f32).T
        cols[2] = vecs[layer].T

    def column(k, first, size, lane):
        return cols[k, pl.ds(first, size), lane : lane + 1]

    def exchange_copy(n):
        return remote(exs, exr.at[n % 2], ex_send.at[0], ex_recv.at[n % 2], other)

    def exchanged(n, first, size, lanes):
        return exs[pl.ds(first, size), lanes].astype(f32) + exr[n % 2, pl.ds(first, size), lanes].astype(f32)

    def project(layer, s):
        mixed = mm(w_t[layer, s, 0, 0 : 3 * hs], x_fm[layer, 0:tw], 1, 0)
        qkv_t[layer, s] = (mixed + cols[s, 0 : 3 * hs, 1:2]).astype(bf16)
        mixed = mm(w_l[layer, s, 0, 0 : 3 * ls], x_fm[layer, tw:width], 1, 0)
        qkv_l[layer, s] = (mixed + cols[s, 3 * hs : 3 * hs + 3 * ls, 1:2]).astype(bf16)

    def head_rows(layer, s, part, h):
        return (
            qkv_t[layer, s, at(part * hs + h * HEAD, HEAD)],
            qkv_l[layer, s, at(part * ls + h * LHEAD, LHEAD)],
        )

    def query(layer, s, h):
        text, lay = head_rows(layer, s, 0, h)
        return jnp.concatenate([text * HEAD**-0.5, lay * LHEAD**-0.5], axis=0).astype(bf16)

    def attend_forward(layer, i):
        s, h = lax.div(i, heads), lax.rem(i, heads)
        keys = jnp.concatenate(head_rows(layer, s, 1, h), axis=0)
        values = jnp.concatenate(head_rows(layer, s, 2, h), axis=0)
        scores = mm(keys, query(layer, s, h), 0, 0) + key_bias[:, 0:1]
        exponent = jnp.exp(scores - jnp.max(scores, axis=0, keepdims=True))
        low = (exponent * (1.0 / jnp.sum(exponent, axis=0, keepdims=True))).astype(bf16)
        probs[i] = low
        context = mm(values, low, 1, 0).astype(bf16)
        ctx_t[layer, s, at(h * HEAD, HEAD)] = context[0:HEAD]
        ctx_l[layer, s, at(h * LHEAD, LHEAD)] = context[HEAD:]

    def attention_partial(layer):
        exs[0:tw] = (
            mm(w_t[layer, 0, 0, 3 * hs : 4 * hs], ctx_t[layer, 0], 0, 0)
            + mm(w_t[layer, 1, 0, 3 * hs : 4 * hs], ctx_t[layer, 1], 0, 0)
        ).astype(bf16)
        exs[tw:width] = (
            mm(w_l[layer, 0, 0, 3 * ls : 4 * ls], ctx_l[layer, 0], 0, 0)
            + mm(w_l[layer, 1, 0, 3 * ls : 4 * ls], ctx_l[layer, 1], 0, 0)
        ).astype(bf16)

    def normalize(hidden):
        center = hidden - jnp.mean(hidden, axis=0, keepdims=True)
        scale = lax.rsqrt(jnp.mean(center * center, axis=0, keepdims=True) + norm_epsilon)
        return center * scale, scale

    def norm_forward(layer, n, which, base, hat_ref, finish):
        def block(b):
            lanes = lanes_at(b * LANES, LANES)
            for k, (first, size) in enumerate(streams):
                hidden = base(first, size, lanes) + exchanged(n, first, size, lanes)
                hat, scale = normalize(hidden + column(2, first, size, 3 * which))
                hat_ref[layer, pl.ds(first, size), lanes] = hat.astype(bf16)
                row = 2 * which + k
                stats[layer, row : row + 1, lanes] = scale
                result = hat * column(2, first, size, 3 * which + 1) + column(2, first, size, 3 * which + 2)
                finish(first, size, lanes, result)

        loop(0, blocks, block)

    def first_norm(layer, n):
        def finish(first, size, lanes, result):
            acc[pl.ds(first, size), lanes] = result
            n1b[layer, pl.ds(first, size), lanes] = result.astype(bf16)

        norm_forward(
            layer, n, 0, lambda s, z, lanes: x_fm[layer, pl.ds(s, z), lanes].astype(f32), xh1, finish
        )

    def second_norm(layer, n, dest):
        def finish(first, size, lanes, result):
            dest[pl.ds(first, size), lanes] = result.astype(bf16)

        norm_forward(layer, n, 1, lambda s, z, lanes: acc[pl.ds(s, z), lanes], xh2, finish)

    def gelu_pair(raised):
        cdf = 0.5 * (1.0 + lax.erf(raised * math.sqrt(0.5)))
        slope = cdf + raised * (jnp.exp(-0.5 * raised * raised) * (1.0 / math.sqrt(2.0 * math.pi)))
        return (raised * cdf).astype(bf16), slope.astype(bf16)

    hb = 256
    per_slot = hid_t // hb

    def expand_block(layer, i):
        s, b = lax.div(i, per_slot), lax.rem(i, per_slot)
        rows = lanes_at(b * hb, hb)
        raised = mm(w_t[layer, s, 1, :, rows], n1b[layer, 0:tw], 0, 0) + cols[s, rows, 0:1]
        act[layer, s, rows], gp[layer, s, rows] = gelu_pair(raised)

    def expand_lay(layer, s):
        raised = mm(w_l[layer, s, 1], n1b[layer, tw:width], 0, 0) + cols[s, hid_t : hid_t + hid_l, 0:1]
        act[layer, s, hid_t:], gp[layer, s, hid_t:] = gelu_pair(raised)

    def shrink_partial(layer):
        exs[0:tw] = (
            mm(w_t[layer, 0, 2], act[layer, 0, 0:hid_t], 1, 0) + mm(w_t[layer, 1, 2], act[layer, 1, 0:hid_t], 1, 0)
        ).astype(bf16)
        exs[tw:width] = (
            mm(w_l[layer, 0, 2], act[layer, 0, hid_t:], 1, 0) + mm(w_l[layer, 1, 2], act[layer, 1, hid_t:], 1, 0)
        ).astype(bf16)

    def rows_out(base, text_to, lay_to):
        mine, theirs = xb * half, (1 - xb) * half
        pairs = (
            (rows_t.at[at(mine, half)], rows_t.at[at(theirs, half)], text_to),
            (rows_l.at[:, lanes_at(mine, half)], rows_l.at[:, lanes_at(theirs, half)], lay_to),
        )
        copies = []
        for k, (own, away, dest) in enumerate(pairs):
            copies.append(local_copy(own, dest.at[xb], out_sem.at[base + k, 0]))
            copies.append(
                remote(away, dest.at[xb], out_sem.at[base + k, 1], out_sem.at[base + k, 2], (c, d, t1))
            )
        return copies

    def stage_rows(layer, value):
        @pl.when(c == layer)
        def _():
            rows_t[...] = value[0:tw].T
            rows_l[...] = value[tw:width]

    def send_rows(layer, base, dest_pair, value):
        stage_rows(layer, value)

        @pl.when(c == layer)
        def _():
            start(rows_out(base, *dest_pair))

    def finish_rows(layer, base, dest_pair):
        @pl.when(c == layer)
        def _():
            wait(rows_out(base, *dest_pair))

    out_pair, back_pair = (text_out, lay_out), (text_back, lay_back)
    fw(0, 0)
    fw(0, 1)
    fw(0, 2)
    rows_cross(in_rows)
    need(0, 0)
    load_columns(0)
    fw(0, 3)
    need(0, 1)
    rows_arrive(in_rows)
    x_fm[0, 0:tw] = rows_t[...].T
    need(0, 2)

    p_store = local_copy(probs, p_keep, p_sem.at[0])
    p_load = local_copy(p_keep, probs, p_sem.at[1])

    for layer in range(2):
        last = layer == 1
        if last:
            fw(layer, 2)
            need(layer, 1)
            fw(layer, 3)
            need(layer, 2)
        project(layer, 0)
        fw(layer, 4)
        project(layer, 1)
        if last:
            p_store.wait()
        fw(layer, 5)
        head = functools.partial(attend_forward, layer)
        loop(0, 2, head)
        fw(layer, 6)
        loop(2, 4, head)
        fw(layer, 7)
        loop(4, 6, head)
        if not last:
            p_store.start()
        need(layer, 3)
        attention_partial(layer)
        swap = exchange_copy(2 * layer)
        swap.start()
        fw(layer, 8)
        swap.wait()
        first_norm(layer, 2 * layer)
        fw(layer, 9)
        need(layer, 4, 5, 6, 7)
        expand = functools.partial(expand_block, layer)
        loop(0, per_slot, expand)
        fw(layer, 10)
        if not last:
            need(layer, 8, 9)
            start_second_layer()
        loop(per_slot, 2 * per_slot, expand)
        fw(layer, 11)
        if last:
            pl.when(zp == 0)(lambda: rows_begin(cot_rows))
            stage_rows(0, x_fm.at[1])
        loop(0, 2, functools.partial(expand_lay, layer))
        if last:
            need(layer, 8, 9, 10, 11)
            pl.when(zp == 1)(lambda: rows_begin(cot_rows))
            on(0, lambda: start(rows_out(0, *out_pair)))
        else:
            need(layer, 10)
            fw(1, 0)
            need(layer, 11)
        shrink_partial(layer)
        swap = exchange_copy(2 * layer + 1)
        swap.start()
        if not last:
            fw(1, 1)
        else:
            rows_cross(cot_rows)
        swap.wait()
        if not last:
            second_norm(0, 1, x_fm.at[1])
            need(1, 0)
            load_columns(1)
        else:
            second_norm(1, 3, dup.at[0])
            rows_arrive(cot_rows)
            g_fm[0:tw] = cot_t[...].T

    def grad_store(layer, chunk, s):
        return [
            local_copy(stg_t.at[s], gb_t.at[layer, chunk, s], stg_sem.at[s, 0]),
            local_copy(stg_l.at[s], gb_l.at[layer, chunk, s], stg_sem.at[s, 1]),
        ]

    def store_grad(layer, chunk, s, text_value, lay_value):
        stg_t[s] = text_value
        stg_l[s] = lay_value
        start(grad_store(layer, chunk, s))

    groups = (
        (gb_t, rz_t, r1_t, r2_t, ro_t, zs_t, zr_t, zv_t, tv_t, fv_t, w_t, tq),
        (gb_l, rz_l, r1_l, r2_l, ro_l, zs_l, zr_l, zv_l, tv_l, fv_l, w_l, lq),
    )
    tx = t1 + c * (t2 - t1)
    near, far = 2 * zp, 2 * (1 - zp)

    def quarters(first, count, size):
        return at(first * size, count * size)

    def by_half(layer, chunk):
        return layer == 1 and chunk == 2

    def first_sends(layer, chunk, core):
        copies = []
        for g, (gb, rz, r1, r2, ro, zs, zr, zv, tv, fv, w, size) in enumerate(groups):
            if by_half(layer, chunk):
                parts = [pl.ds(0, 4 * size) if core else quarters(far, 2, size)]
            else:
                parts = [quarters(far, 2, size), quarters(near + core, 1, size)]
            for i, rows in enumerate(parts):
                copies.append(
                    remote(
                        gb.at[layer, chunk, 1 - core, rows], r2.at[chunk, core, rows],
                        s1_send.at[layer, chunk, g, i], s2_recv.at[chunk, core, i, g],
                        (layer, d, t2 if core else t1),
                    )
                )
        return copies[::2] + copies[1::2] if len(copies) > 2 else copies

    def direct(layer, chunk, i):
        for core in range(2):
            on(core, lambda: start(first_sends(layer, chunk, core)[2 * i : 2 * i + 2]))

    def own_sends(chunk):
        return [
            remote(gb.at[1, chunk, 0], ro.at[chunk], so_send.at[chunk, g], so_recv.at[chunk, g], other)
            for g, (gb, rz, r1, r2, ro, *_) in enumerate(groups)
        ]

    def pair_sends(layer, chunk):
        return [
            remote(
                gb.at[layer, chunk, 1, quarters(far, 2, size)], rz.at[layer, chunk],
                rz_send.at[layer, chunk, g], rz_recv.at[layer, chunk, g], (1, dz, t),
            )
            for g, (gb, rz, *_, size) in enumerate(groups)
        ]

    def diagonal_sends(layer, chunk):
        copies = []
        for g, (gb, rz, r1, *_, size) in enumerate(groups):
            if by_half(layer, chunk):
                parts = [(quarters(near, 2, size), (rh_t, rh_l)[g].at[chunk], (0, d, t2))]
            else:
                come = r1.at[3 * layer + chunk]
                parts = [(quarters(near + i, 1, size), come, (1 - i, d, (t1, t2)[i])) for i in range(2)]
            for i, (rows, dest, device) in enumerate(parts):
                copies.append(
                    remote(
                        gb.at[layer, chunk, 1, rows], dest,
                        d_send.at[layer, chunk, g, i], r1_recv.at[layer, chunk, g], device,
                    )
                )
        return copies

    def grads_go(layer, chunk, *slots):
        for s in slots or (1, 0):
            wait(grad_store(layer, chunk, s))
            if s == 1:
                on(1, lambda: start(pair_sends(layer, chunk)))
            elif layer == 1:
                on(0, lambda: start(own_sends(chunk)))

    def pair_loads(layer, chunk):
        copies = []
        for g, (gb, rz, r1, r2, ro, zs, zr, zv, tv, fv, w, size) in enumerate(groups):
            copies.append(local_copy(gb.at[layer, chunk, 1, quarters(near, 2, size)], zv.at[0], zv_sem.at[g, 0]))
            copies.append(local_copy(rz.at[layer, chunk], zv.at[1], zv_sem.at[g, 1]))
        return copies

    def pair_stores(layer, chunk):
        return [
            local_copy(zv.at[0], gb.at[layer, chunk, 1, quarters(near, 2, size)], zv_sem.at[g, 2])
            for g, (gb, rz, r1, r2, ro, zs, zr, zv, tv, fv, w, size) in enumerate(groups)
        ]

    def pair_load(layer, chunk):
        @pl.when(c == 1)
        def _():
            for g, (gb, rz, *_) in enumerate(groups):
                landed(rz.at[layer, chunk], rz_recv.at[layer, chunk, g])
            start(pair_loads(layer, chunk))

    def pair_add(layer, chunk):
        @pl.when(c == 1)
        def _():
            wait(pair_loads(layer, chunk))
            for zv in (zv_t, zv_l):
                zv[0] = (zv[0].astype(f32) + zv[1].astype(f32)).astype(bf16)
            start(pair_stores(layer, chunk))

    def pair_send(layer, chunk):
        @pl.when(c == 1)
        def _():
            wait(pair_stores(layer, chunk))
            start(diagonal_sends(layer, chunk))

    def transit_parts(layer, chunk):
        parts = []
        for g, (gb, rz, r1, r2, ro, zs, zr, zv, tv, fv, w, size) in enumerate(groups):
            if by_half(layer, chunk):
                parts.append((gb.at[1, chunk, 1, quarters(near, 2, size)], (rh_t, rh_l)[g].at[chunk], zv, zv_sem))
            else:
                rows = quarters(near + 1 - c, 1, size)
                parts.append((gb.at[layer, chunk, 1 - c, rows], r1.at[3 * layer + chunk], tv, tv_sem))
        return parts

    def transit_loads(layer, chunk):
        copies = []
        for g, (mine, come, held, sem) in enumerate(transit_parts(layer, chunk)):
            copies.append(local_copy(mine, held.at[0], sem.at[g, 0]))
            copies.append(local_copy(come, held.at[1], sem.at[g, 1]))
        return copies

    def transit_stores(layer, chunk):
        return [
            local_copy(held.at[0], mine, sem.at[g, 2])
            for g, (mine, come, held, sem) in enumerate(transit_parts(layer, chunk))
        ]

    def second_sends(layer, chunk):
        copies = []
        for g, (mine, come, held, sem) in enumerate(transit_parts(layer, chunk)):
            gb, rz, r1, r2, *_, size = groups[g]
            if by_half(layer, chunk):
                dest, device, way, which = r2.at[chunk, 0, quarters(near, 2, size)], (1, d, t1), 0, 1
            else:
                dest, device = r2.at[chunk, c, quarters(near + 1 - c, 1, size)], (layer, d, tx)
                way, which = c, 2
            copies.append(
                remote(mine, dest, s2_send.at[layer, chunk, g], s2_recv.at[chunk, way, which, g], device)
            )
        return copies

    def transit_load(layer, chunk):
        for g, (mine, come, held, sem) in enumerate(transit_parts(layer, chunk)):
            landed(come, r1_recv.at[layer, chunk, g])
        start(transit_loads(layer, chunk))

    def transit_add(layer, chunk):
        wait(transit_loads(layer, chunk))
        for mine, come, held, sem in transit_parts(layer, chunk):
            held[0] = (held[0].astype(f32) + held[1].astype(f32)).astype(bf16)
        start(transit_stores(layer, chunk))

    def transit_send(layer, chunk):
        wait(transit_stores(layer, chunk))
        start(second_sends(layer, chunk))

    def final_loads(layer, chunk, stage):
        copies = []
        for g, (gb, rz, r1, r2, ro, zs, zr, zv, tv, fv, w, size) in enumerate(groups):
            rows = quarters(near if stage else far, 2, size)
            own = ro.at[chunk, rows] if layer == 1 else gb.at[0, chunk, 0, rows]
            terms = [
                (own, w.at[1, 0, chunk, rows]),
                (r2.at[chunk, 0, rows], w.at[1, 1, chunk, rows]),
                (r2.at[chunk, 1, rows], fv.at[chunk, rows]),
            ]
            if z_inside and stage == 1:
                terms.append(((zh_t, zh_l)[g].at[chunk], fv.at[chunk, quarters(far, 2, size)]))
            for i, (src, dst) in enumerate(terms):
                copies.append(local_copy(src, dst, fv_sem.at[g, i]))
        return copies

    def final_load(layer, chunk, stage):
        @pl.when(c == layer)
        def _():
            for g, (gb, rz, r1, r2, ro, zs, zr, zv, tv, fv, w, size) in enumerate(groups):

                def came(way, first, count, which):
                    landed(r2.at[chunk, way, quarters(first, count, size)], s2_recv.at[chunk, way, which, g])

                if layer == 1 and stage == 0:
                    landed(ro.at[chunk], so_recv.at[chunk, g])
                if by_half(layer, chunk) and stage == 0:
                    came(0, far, 2, 0)
                    came(1, 0, 4, 0)
                elif by_half(layer, chunk):
                    came(0, near, 2, 1)
                else:
                    for way in range(2):
                        if stage == 0:
                            came(way, far, 2, 0)
                        else:
                            came(way, near + way, 1, 1)
                            came(way, near + 1 - way, 1, 2)
                if z_inside and stage == 1:
                    landed((zh_t, zh_l)[g].at[chunk], zh_recv.at[chunk, g])
            start(final_loads(layer, chunk, stage))

    def half_send(chunk, g):
        gb, rz, r1, r2, ro, zs, zr, zv, tv, fv, w, size = groups[g]
        return remote(
            w.at[1, 0, chunk, quarters(far, 2, size)], (zh_t, zh_l)[g].at[chunk],
            z_send.at[chunk, 0, g], zh_recv.at[chunk, g], (c, dz, t),
        )

    def quarter_send(chunk, i, g, away):
        gb, rz, r1, r2, ro, zs, zr, zv, tv, fv, w, size = groups[g]
        piece, dest = w.at[1, 0, chunk, quarters(near + i, 1, size)], zr.at[chunk, lax.div(d, 2)]
        recv = z_recv.at[chunk, lax.div(d, 2), g]
        if away:
            return remote(piece, dest, z_send.at[chunk, 1 + i, g], recv, (c, near + i, t))
        return local_copy(piece, dest, recv)

    def sum_stores(chunk, stage):
        copies = []
        for g, (gb, rz, r1, r2, ro, zs, zr, zv, tv, fv, w, size) in enumerate(groups):
            rows = quarters(near if stage else far, 2, size)
            copies.append(local_copy(w.at[1, 0, chunk, rows], zs.at[chunk, rows], z_send.at[chunk, stage, g]))
        return copies

    def final_add(layer, chunk, stage):
        @pl.when(c == layer)
        def _():
            wait(final_loads(layer, chunk, stage))
            for gb, rz, r1, r2, ro, zs, zr, zv, tv, fv, w, size in groups:
                rows = quarters(near if stage else far, 2, size)
                total = w[1, 0, chunk, rows].astype(f32) + w[1, 1, chunk, rows].astype(f32)
                total = total + fv[chunk, rows].astype(f32)
                if z_inside and stage == 1:
                    total = total + fv[chunk, quarters(far, 2, size)].astype(f32)
                w[1, 0, chunk, rows] = total.astype(bf16)
            if not z_inside:
                start(sum_stores(chunk, stage))
            elif stage == 0:
                start([half_send(chunk, g) for g in range(2)])
            else:
                for i in range(2):

                    @pl.when(near + i != d)
                    def _():
                        start([quarter_send(chunk, i, g, True) for g in range(2)])

                    @pl.when(near + i == d)
                    def _():
                        start([quarter_send(chunk, i, g, False) for g in range(2)])

    def sums_done():
        for chunk in range(3):
            if not z_inside:
                wait(sum_stores(chunk, 0) + sum_stores(chunk, 1))
                continue
            for g in range(2):
                half_send(chunk, g).wait_send()
                for i in range(2):

                    @pl.when(near + i != d)
                    def _():
                        quarter_send(chunk, i, g, True).wait_send()

                for k in range(2):
                    landed(groups[g][6].at[chunk, k], z_recv.at[chunk, k, g])

    def small_sends(layer):
        zero = [remote(smsg.at[layer, 1], srec.at[0], sm_send.at[layer, 0], sm_recv.at[0], (layer, d, t1))]
        if layer == 1:
            zero.append(remote(smsg.at[1, 0], srec.at[3], sm_send.at[1, 1], sm_recv.at[3], other))
        one = [
            remote(smsg.at[layer, 0], srec.at[1], sm_send.at[layer, 0], sm_recv.at[1], (layer, d, t2)),
            remote(smsg.at[layer, 1], srec.at[2], sm_send.at[layer, 1], sm_recv.at[2], (layer, d, t3)),
        ]
        return zero, one

    def small_go(layer):
        zero, one = small_sends(layer)

        @pl.when(c == 0)
        def _():
            start(zero)

        @pl.when(c == 1)
        def _():
            start(one)

    def small_z():
        if not z_inside:
            return []
        return [
            remote(ssum, szr.at[r - 1], sz_send.at[r - 1], sz_recv.at[r - 1], (c, lax.rem(d + r, dp), t))
            for r in range(1, dp)
        ]

    def small_total(layer):
        @pl.when(c == layer)
        def _():
            for i in range(3):
                landed(srec.at[i], sm_recv.at[i])
            if layer == 1:
                landed(srec.at[3], sm_recv.at[3])
                own = srec[3]
            else:
                own = smsg[0, 0]
            ssum[...] = own + srec[0] + srec[1] + srec[2]
            start(small_z())

    def row_sums(ref):
        return mm(ones, ref[...], 1, 1)[0:1]

    def vector_sum(layer, row, value):
        for s in range(2):
            smsg[layer, s, 8 + row : 9 + row, 0:width] = value

    def norm_backward(layer, which, hat_ref, incoming):
        def block(b):
            lanes = lanes_at(b * LANES, LANES)
            for k, (first, size) in enumerate(streams):
                grad = incoming(first, size, lanes)
                hat = hat_ref[layer, pl.ds(first, size), lanes].astype(f32)
                row = 2 * which + k
                scale = stats[layer, row : row + 1, lanes]
                gained = grad * column(2, first, size, 3 * which + 1)
                mean_grad = jnp.mean(gained, axis=0, keepdims=True)
                mean_both = jnp.mean(gained * hat, axis=0, keepdims=True)
                result = scale * (gained - mean_grad - hat * mean_both)
                acc[pl.ds(first, size), lanes] = result
                tmpb[pl.ds(first, size), lanes] = result.astype(bf16)
                exs[pl.ds(first, size), lanes] = (grad * hat).astype(bf16)
                g_fm[pl.ds(first, size), lanes] = grad.astype(bf16)

        loop(0, blocks, block)

    def norm_sums(layer, which):
        vector_sum(layer, 3 * which + 1, row_sums(exs))
        vector_sum(layer, 3 * which + 2, row_sums(g_fm))
        vector_sum(layer, 3 * which, row_sums(tmpb))

    def ffn_backward(layer):
        def text_block(i):
            s, b = lax.div(i, per_slot), lax.rem(i, per_slot)
            rows = lanes_at(b * hb, hb)
            back = mm(w_t[layer, s, 2, :, rows], tmpb[0:tw], 0, 0)
            dup[s, rows] = (back * gp[layer, s, rows].astype(f32)).astype(bf16)

        loop(0, 2 * per_slot, text_block)

        def lay_block(s):
            back = mm(w_l[layer, s, 2], tmpb[tw:width], 0, 0)
            dup[s, hid_t:] = (back * gp[layer, s, hid_t:].astype(f32)).astype(bf16)

        loop(0, 2, lay_block)

    def shrink_grads(layer, s):
        store_grad(
            layer, 2, s,
            mm(tmpb[0:tw], act[layer, s, 0:hid_t], 1, 1).astype(bf16),
            mm(tmpb[tw:width], act[layer, s, hid_t:], 1, 1).astype(bf16),
        )

    def expand_grads(layer, s):
        store_grad(
            layer, 1, s,
            mm(n1b[layer, 0:tw], dup[s, 0:hid_t], 1, 1).astype(bf16),
            mm(n1b[layer, tw:width], dup[s, hid_t:], 1, 1).astype(bf16),
        )

    def expand_partial(layer):
        exs[0:tw] = (
            mm(w_t[layer, 0, 1], dup[0, 0:hid_t], 1, 0) + mm(w_t[layer, 1, 1], dup[1, 0:hid_t], 1, 0)
        ).astype(bf16)
        exs[tw:width] = (
            mm(w_l[layer, 0, 1], dup[0, hid_t:], 1, 0) + mm(w_l[layer, 1, 1], dup[1, hid_t:], 1, 0)
        ).astype(bf16)

    def context_grads(layer, s):
        dup[s, 0:hs] = mm(w_t[layer, s, 0, 3 * hs : 4 * hs], tmpb[0:tw], 1, 0).astype(bf16)
        dup[s, hs : hs + ls] = mm(w_l[layer, s, 0, 3 * ls : 4 * ls], tmpb[tw:width], 1, 0).astype(bf16)

    def attend_backward(layer, i):
        s, h = lax.div(i, heads), lax.rem(i, heads)
        queries = query(layer, s, h)
        key_text, key_lay = head_rows(layer, s, 1, h)
        keys = jnp.concatenate([key_text * HEAD**-0.5, key_lay * LHEAD**-0.5], axis=0).astype(bf16)
        values = jnp.concatenate(head_rows(layer, s, 2, h), axis=0)
        grads = jnp.concatenate([dup[s, at(h * HEAD, HEAD)], dup[s, at(hs + h * LHEAD, LHEAD)]], axis=0)
        low = probs[i]
        prob = low.astype(f32)
        dprob = mm(values, grads, 0, 0)
        inner = jnp.sum(dprob * prob, axis=0, keepdims=True)
        dscore = (prob * (dprob - inner)).astype(bf16)
        results = (mm(keys, dscore, 1, 0), mm(queries, dscore, 1, 1), mm(grads, low, 1, 1))
        for part, result in enumerate(results):
            result = result.astype(bf16)
            dqkv[s, at(part * hs + h * HEAD, HEAD)] = result[0:HEAD]
            dqkv[s, at(3 * hs + part * ls + h * LHEAD, LHEAD)] = result[HEAD:]

    def attend_grads(layer, s):
        text = jnp.concatenate(
            [mm(x_fm[layer, 0:tw], dqkv[s, 0 : 3 * hs], 1, 1), mm(tmpb[0:tw], ctx_t[layer, s], 1, 1)], axis=1
        )
        lay = jnp.concatenate(
            [mm(x_fm[layer, tw:width], dqkv[s, 3 * hs :], 1, 1), mm(tmpb[tw:width], ctx_l[layer, s], 1, 1)], axis=1
        )
        store_grad(layer, 0, s, text.astype(bf16), lay.astype(bf16))

    def attend_partial(layer):
        exs[0:tw] = (
            mm(w_t[layer, 0, 0, 0 : 3 * hs], dqkv[0, 0 : 3 * hs], 0, 0)
            + mm(w_t[layer, 1, 0, 0 : 3 * hs], dqkv[1, 0 : 3 * hs], 0, 0)
        ).astype(bf16)
        exs[tw:width] = (
            mm(w_l[layer, 0, 0, 0 : 3 * ls], dqkv[0, 3 * hs :], 0, 0)
            + mm(w_l[layer, 1, 0, 0 : 3 * ls], dqkv[1, 3 * hs :], 0, 0)
        ).astype(bf16)

    def small_sums(layer, s, row, ref, size):
        smsg[layer, s, row : row + 1, 0:size] = mm(ones, ref[s], 1, 1)[0:1]

    def first_grad(n, first, size, lanes):
        return acc[pl.ds(first, size), lanes] + exchanged(n, first, size, lanes)

    def gather_sent():
        for layer in range(2):

            @pl.when(c == layer)
            def _():
                for p in all_pieces:
                    own_first(p).wait_send()
                    if layer == 1:
                        own_core(p).wait_send()

        @pl.when(c == zp)
        def _():
            for p in all_pieces:
                for copy in forwards(1, p):
                    copy.wait_send()

    def run(*tasks):
        for task in tasks:
            task[0](*task[1:])

    Z, T, F = (pair_load, pair_add, pair_send), (transit_load, transit_add, transit_send), (final_load, final_add)
    service = {
        (1, "ffn swap"): [(direct, 1, 1, 0), (on, 0, direct, 1, 1, 1)],
        (1, "context"): [(gather_sent,), (Z[0], 1, 2)],
        (1, "heads 0"): [(Z[1], 1, 2)],
        (1, "heads 1"): [(Z[2], 1, 2), (Z[0], 1, 1), (F[0], 1, 2, 0)],
        (1, "heads 2"): [(Z[1], 1, 1)],
        (1, "attend grads"): [(Z[2], 1, 1), (F[1], 1, 2, 0)],
        (1, "swap"): [
            (on, 1, direct, 1, 1, 1), (direct, 1, 0, 0), (on, 0, direct, 1, 0, 1),
        ],
        (0, "shrink grads"): [(on, 0, direct, 0, 2, 0), (on, 0, T[0], 1, 2)],
        (0, "ffn"): [(on, 0, T[1], 1, 2)],
        (0, "expand grads"): [(on, 0, T[2], 1, 2), (on, 0, direct, 0, 2, 1), (T[0], 1, 1), (Z[0], 1, 0), (F[0], 1, 1, 0)],
        (0, "ffn swap"): [(Z[1], 1, 0), (on, 1, direct, 1, 0, 1), (T[1], 1, 1), (F[1], 1, 1, 0)],
        (0, "first norm"): [(Z[2], 1, 0), (T[2], 1, 1), (on, 1, direct, 0, 2, 0), (Z[0], 0, 2)],
        (0, "context"): [(Z[1], 0, 2)],
        (0, "heads 0"): [(Z[2], 0, 2)],
        (0, "heads 1"): [(Z[0], 0, 1), (T[0], 1, 0)],
        (0, "heads 2"): [(Z[1], 0, 1), (T[1], 1, 0), (on, 1, direct, 0, 2, 1), (on, 0, direct, 0, 1, 0)],
        (0, "attend grads"): [(Z[2], 0, 1), (T[2], 1, 0)],
        (0, "swap"): [(on, 1, direct, 0, 1, 0), (on, 0, direct, 0, 0, 0), (F[0], 1, 0, 0)],
        (0, "finished"): [(T[0], 0, 2), (F[1], 1, 0, 0), (T[1], 0, 2)],
    }

    for layer in (1, 0):
        last = layer == 0
        n = 4 + 2 * (1 - layer)

        def point(name):
            run(*service.get((layer, name), []))

        if last:
            load_columns(0)
        point("begin")
        norm_backward(layer, 1, xh2, lambda s, z, lanes: g_fm[pl.ds(s, z), lanes].astype(f32))
        point("second norm")
        for s in (1, 0):
            shrink_grads(layer, s)
        grads_go(layer, 2, 1)
        if not last:
            on(0, direct, 1, 2, 0)
        norm_sums(layer, 1)
        grads_go(layer, 2, 0)
        if not last:
            on(1, direct, 1, 2, 0)
        if not last:
            send_rows(1, 0, out_pair, dup.at[0])
        point("shrink grads")
        ffn_backward(layer)
        point("ffn")
        for s in range(2):
            expand_grads(layer, s)
        point("expand grads")
        expand_partial(layer)
        swap = exchange_copy(n)
        swap.start()
        for s in range(2):
            small_sums(layer, s, 0, dup, hid_t + hid_l)
        grads_go(layer, 1)
        point("ffn swap")
        swap.wait()
        norm_backward(layer, 0, xh1, functools.partial(first_grad, n))
        norm_sums(layer, 0)
        point("first norm")
        if last:
            p_load.wait()
        for s in range(2):
            context_grads(layer, s)
        point("context")
        head = functools.partial(attend_backward, layer)
        for i in range(3):
            loop(2 * i, 2 * i + 2, head)
            point(f"heads {i}")
        if not last:
            p_load.start()
        for s in range(2):
            attend_grads(layer, s)
        point("attend grads")
        attend_partial(layer)
        swap = exchange_copy(n + 1)
        swap.start()
        for s in range(2):
            small_sums(layer, s, 1, dqkv, 3 * hs + 3 * ls)
        small_go(layer)
        point("last grads")
        grads_go(layer, 0)
        point("swap")
        swap.wait()
        point("swapped")

        def finish(b):
            lanes = lanes_at(b * LANES, LANES)
            for first, size in streams:
                g_fm[pl.ds(first, size), lanes] = first_grad(n + 1, first, size, lanes).astype(bf16)

        loop(0, blocks, finish)
        point("finished")
        finish_rows(layer, 0, out_pair)
        stage_rows(layer, g_fm)

    def transit(layer, chunk):
        run(*((step, layer, chunk) for step in T))

    def final(layer, chunk, stage):
        run(*((step, layer, chunk, stage) for step in F))

    transit_send(0, 2)

    @pl.when(c == 0)
    def _():
        run((direct, 0, 1, 1), (final, 0, 2, 0), (transit, 0, 1), (final, 0, 1, 0), (transit, 0, 0))
        run((direct, 0, 0, 1), (small_total, 0))
        start(rows_out(2, *back_pair))
        run((final, 0, 0, 0), (final, 0, 2, 1), (final, 0, 1, 1), (final, 0, 0, 1))

    @pl.when(c == 1)
    def _():
        run(*((step, 0, 0) for step in Z), (direct, 0, 0, 0), (transit, 0, 1), (direct, 0, 1, 1))
        run((final, 1, 2, 1), (final, 1, 1, 1), (transit, 0, 0), (direct, 0, 0, 1), (final, 1, 0, 1))
        start(rows_out(2, *back_pair))
        small_total(1)

    for copy in small_z():
        copy.wait()
    if z_inside:
        for r in range(1, dp):
            ssum[...] = ssum[...] + szr[r - 1]
    sm_copy = local_copy(ssum, sm_out, so_sem.at[0])
    sm_copy.start()
    wait(rows_out(2, *back_pair))
    for layer in range(2):
        smalls = small_sends(layer)
        for core in range(2):

            @pl.when(c == core)
            def _():
                for copy in smalls[core]:
                    copy.wait_send()
                for chunk in range(3):
                    copies = first_sends(layer, chunk, core)
                    if core == 1:
                        copies += pair_sends(layer, chunk) + diagonal_sends(layer, chunk)
                    elif layer == 1:
                        copies += own_sends(chunk)
                    if core == 0 or not by_half(layer, chunk):
                        copies += second_sends(layer, chunk)
                    for copy in copies:
                        copy.wait_send()

    sums_done()
    sm_copy.wait()


def finishing(
    parts_t, parts_l, sums_in, rows_in_0, rows_in_1, rows_in_2, rows_in_3,
    rows_0, rows_1, rows_2, rows_3, att_t, out_t, exp_t, shr_t, att_l, out_l, exp_l, shr_l,
    bias_t, off_t, vec_t, bias_l, off_l, vec_l,
    zr_t, zr_l, sums, held_0, held_1, held_2, held_3, sems,
):
    pairs = ((rows_in_0, held_0), (rows_in_1, held_1), (rows_in_2, held_2), (rows_in_3, held_3))
    pairs += ((parts_t, zr_t), (parts_l, zr_l), (sums_in, sums))
    loads = [pltpu.make_async_copy(src, dst, sems.at[i]) for i, (src, dst) in enumerate(pairs)]
    for copy in loads:
        copy.start()
    pairs = ((held_0, rows_0), (held_1, rows_1), (held_2, rows_2), (held_3, rows_3))
    copies = [pltpu.make_async_copy(src, dst, sems.at[7 + i]) for i, (src, dst) in enumerate(pairs)]
    for load, copy in zip(loads[:4], copies):
        load.wait()
        copy.start()
    for load in loads[4:]:
        load.wait()
    for zr, att, out, exp, shr in ((zr_t, att_t, out_t, exp_t, shr_t), (zr_l, att_l, out_l, exp_l, shr_l)):
        totals = []
        for chunk in range(3):
            total = zr[chunk, 0].astype(f32)
            for r in range(1, zr.shape[1]):
                total = total + zr[chunk, r].astype(f32)
            totals.append(total)
        size = out.shape[1]
        for j in range(3):
            att[j] = totals[0][:, j * size : (j + 1) * size]
        out[...] = totals[0][:, 3 * size : 4 * size]
        exp[...] = totals[1]
        shr[...] = totals[2]
    hs, ls = bias_t.shape[1], bias_l.shape[1]
    ft, fl = off_t.shape[1], off_l.shape[1]
    tw, lw = vec_t.shape[2], vec_l.shape[2]
    off_t[...] = sums[0:1, 0:ft]
    off_l[...] = sums[0:1, ft : ft + fl]
    bias_t[0:1] = sums[1:2, 0:hs]
    bias_t[1:2] = sums[1:2, 2 * hs : 3 * hs]
    bias_l[0:1] = sums[1:2, 3 * hs : 3 * hs + ls]
    bias_l[1:2] = sums[1:2, 3 * hs + 2 * ls : 3 * hs + 3 * ls]
    for row in range(6):
        vec_t[row] = sums[8 + row : 9 + row, 0:tw]
        vec_l[row] = sums[8 + row : 9 + row, tw : tw + lw]
    for copy in copies:
        copy.wait()


def local(
    dp,
    text_in,
    layout_in,
    text_cot,
    layout_cot,
    lengths,
    text_attend,
    text_biases,
    text_output,
    text_expand,
    text_offset,
    text_shrink,
    text_vectors,
    layout_attend,
    layout_biases,
    layout_output,
    layout_expand,
    layout_offset,
    layout_shrink,
    layout_vectors,
):
    rows, tw = text_in.shape[1:]
    lw = layout_in.shape[2]
    width, tokens = tw + lw, 2 * rows
    hs, ls = text_output.shape[2], layout_output.shape[2]
    ft, fl = text_expand.shape[2], layout_expand.shape[2]
    zt, zl = tw // dp, lw // dp
    z_inside = dp == 4

    def shape(dims, dtype=bf16):
        return jax.ShapeDtypeStruct(dims, dtype)

    def attend_rows(attend):
        return attend[0].transpose(1, 2, 0).reshape(-1, attend.shape[1])

    hbm = pl.BlockSpec(memory_space=pltpu.HBM)
    vmem = pl.BlockSpec(memory_space=pltpu.VMEM)
    heads = hs // HEAD
    row_shapes = [shape((2, rows, tw)), shape((2, lw, rows)), shape((2, rows, tw)), shape((2, lw, rows))]
    out_shape = row_shapes + [
        shape((16, SMALL), f32),
        shape((3, tw, tw)), shape((3, lw, lw)),
        shape((3, 2, tw // 4, tw)), shape((3, 2, lw // 4, lw)), shape((3, tw // 2, tw)), shape((3, lw // 2, lw)),
        shape((2, 3, 2, tw, tw)), shape((2, 3, 2, lw, lw)),
        shape((2, 3, tw // 2, tw)), shape((2, 3, lw // 2, lw)), shape((3, tw // 2, tw)), shape((3, lw // 2, lw)),
        shape((5, tw // 4, tw)), shape((5, lw // 4, lw)),
        shape((3, 2, tw, tw)), shape((3, 2, lw, lw)),
        shape((3, tw, tw)), shape((3, lw, lw)),
        shape((2 * heads, tokens, tokens)),
    ]
    dma = pltpu.SemaphoreType.DMA
    scratch = [
        pltpu.VMEM((2, 2, 3, tw, tw), bf16),
        pltpu.VMEM((2, 2, 3, lw, lw), bf16),
        pltpu.VMEM((2, 2, 16, SMALL), bf16),
        pltpu.VMEM((2, 16, SMALL), f32),
        pltpu.VMEM((16, SMALL), bf16),
        pltpu.VMEM((16, SMALL), f32),
        pltpu.VMEM((tokens, LANES), f32),
        pltpu.VMEM((tokens, tw), bf16),
        pltpu.VMEM((lw, tokens), bf16),
        pltpu.VMEM((2, width, tokens), bf16),
        pltpu.VMEM((2, 2, 3 * hs, tokens), bf16),
        pltpu.VMEM((2, 2, 3 * ls, tokens), bf16),
        pltpu.VMEM((2 * heads, tokens, tokens), bf16),
        pltpu.VMEM((2, 2, hs, tokens), bf16),
        pltpu.VMEM((2, 2, ls, tokens), bf16),
        pltpu.VMEM((2, width, tokens), bf16),
        pltpu.VMEM((2, width, tokens), bf16),
        pltpu.VMEM((2, width, tokens), bf16),
        pltpu.VMEM((2, 2, ft + fl, tokens), bf16),
        pltpu.VMEM((2, 2, ft + fl, tokens), bf16),
        pltpu.VMEM((2, 8, tokens), f32),
        pltpu.VMEM((width, tokens), f32),
        pltpu.VMEM((width, tokens), bf16),
        pltpu.VMEM((2, width, tokens), bf16),
        pltpu.VMEM((width, tokens), bf16),
        pltpu.VMEM((width, tokens), bf16),
        pltpu.VMEM((2, ft + fl, tokens), bf16),
        pltpu.VMEM((2, 3 * hs + 3 * ls, tokens), bf16),
        pltpu.VMEM((3, SMALL, 16), f32),
        pltpu.VMEM((2, tw, tw), bf16),
        pltpu.VMEM((2, lw, lw), bf16),
        pltpu.VMEM((2, tw // 2, tw), bf16),
        pltpu.VMEM((2, lw // 2, lw), bf16),
        pltpu.VMEM((2, tw // 4, tw), bf16),
        pltpu.VMEM((2, lw // 4, lw), bf16),
        pltpu.VMEM((3, tw, tw), bf16),
        pltpu.VMEM((3, lw, lw), bf16),
        pltpu.VMEM((2, 2, 16, SMALL), f32),
        pltpu.VMEM((4, 16, SMALL), f32),
        pltpu.VMEM((16, SMALL), f32),
        pltpu.VMEM((3, 16, SMALL), f32),
        dma((2, 2, 17)), dma((17, 2)), dma((17, 2)), dma((3,)), dma((4, 5)), dma((1,)), dma((2,)),
        dma((4, 3)), dma((2, 2)), dma((2,)),
        dma((2, 3, 2)), dma((2, 3, 2)), dma((2, 3, 2, 2)), dma((2, 3, 2, 2)), dma((2, 3, 2)), dma((2, 3, 2)),
        dma((3, 2, 3, 2)), dma((3, 2)), dma((3, 2)), dma((3, 3, 2)), dma((3, 2, 2)), dma((3, 2)),
        dma((2, 3)), dma((2, 3)), dma((2, 4)),
        dma((2, 2)), dma((4,)), dma((3,)), dma((3,)), dma((1,)),
    ]
    results = pl.pallas_call(
        functools.partial(kernel, dp, z_inside),
        out_shape=out_shape,
        in_specs=[hbm] * 12 + [vmem] * 6 + [pl.BlockSpec(memory_space=pltpu.SMEM)],
        out_specs=[hbm] * len(out_shape),
        scratch_shapes=scratch,
        compiler_params=pltpu.CompilerParams(
            collective_id=0, has_side_effects=True, vmem_limit_bytes=63 * 1024 * 1024
        ),
    )(
        text_in, layout_in.transpose(0, 2, 1), text_cot, layout_cot.transpose(0, 2, 1),
        attend_rows(text_attend), text_output[0].T, text_expand[0], text_shrink[0],
        attend_rows(layout_attend), layout_output[0].T, layout_expand[0], layout_shrink[0],
        text_biases[0], layout_biases[0], text_offset, layout_offset, text_vectors[0], layout_vectors[0], lengths,
    )
    row_results, sums = results[:4], results[4]
    if z_inside:
        parts_t, parts_l = results[7], results[8]
    else:
        parts_t = lax.psum_scatter(results[5], "dp", scatter_dimension=1, tiled=True)[:, None]
        parts_l = lax.psum_scatter(results[6], "dp", scatter_dimension=1, tiled=True)[:, None]
        sums = lax.psum(sums, "dp")
    final_shapes = row_shapes + [
        shape((3, zt, hs), f32), shape((zt, hs), f32), shape((zt, ft), f32), shape((zt, ft), f32),
        shape((3, zl, ls), f32), shape((zl, ls), f32), shape((zl, fl), f32), shape((zl, fl), f32),
        shape((2, hs), f32), shape((1, ft), f32), shape((6, 1, tw), f32),
        shape((2, ls), f32), shape((1, fl), f32), shape((6, 1, lw), f32),
    ]
    (
        text_out, lay_out, text_back, lay_back, att_t, out_t, exp_t, shr_t, att_l, out_l, exp_l, shr_l,
        bias_t, off_t, vec_t, bias_l, off_l, vec_l,
    ) = pl.pallas_call(
        finishing,
        out_shape=final_shapes,
        in_specs=[hbm] * 7,
        out_specs=[hbm] * 4 + [vmem] * 14,
        scratch_shapes=[
            pltpu.VMEM(parts_t.shape, bf16), pltpu.VMEM(parts_l.shape, bf16), pltpu.VMEM((16, SMALL), f32),
            *(pltpu.VMEM(rows.shape, bf16) for rows in row_shapes), dma((11,)),
        ],
        compiler_params=pltpu.CompilerParams(vmem_limit_bytes=62 * 1024 * 1024),
    )(parts_t, parts_l, sums, *row_results)
    return (
        text_out[None],
        lay_out.transpose(0, 2, 1)[None],
        text_back[None],
        lay_back.transpose(0, 2, 1)[None],
        att_t.transpose(1, 0, 2)[None],
        bias_t[None],
        out_t[None],
        exp_t[None],
        off_t,
        shr_t[None],
        vec_t.transpose(1, 0, 2),
        att_l.transpose(1, 0, 2)[None],
        bias_l[None],
        out_l[None],
        exp_l[None],
        off_l,
        shr_l[None],
        vec_l.transpose(1, 0, 2),
    )


def solution(mesh):
    return jax.shard_map(
        functools.partial(local, mesh.shape["dp"]),
        mesh=mesh,
        in_specs=(
            P(None, ("dp", "tensor"), None),
            P(None, ("dp", "tensor"), None),
            P(None, ("dp", "tensor"), None),
            P(None, ("dp", "tensor"), None),
            P(None, "dp"),
            P("section", None, None, "tensor"),
            P("section", None, "tensor"),
            P("section", None, "tensor"),
            P("section", None, "tensor"),
            P("section", "tensor"),
            P("section", None, "tensor"),
            P("section", None, None),
            P("section", None, None, "tensor"),
            P("section", None, "tensor"),
            P("section", None, "tensor"),
            P("section", None, "tensor"),
            P("section", "tensor"),
            P("section", None, "tensor"),
            P("section", None, None),
        ),
        out_specs=(
            P("section", None, ("dp", "tensor"), None),
            P("section", None, ("dp", "tensor"), None),
            P("section", None, ("dp", "tensor"), None),
            P("section", None, ("dp", "tensor"), None),
            P("section", "dp", None, "tensor"),
            P("section", None, "tensor"),
            P("section", "dp", "tensor"),
            P("section", "dp", "tensor"),
            P("section", "tensor"),
            P("section", "dp", "tensor"),
            P("section", None, None),
            P("section", "dp", None, "tensor"),
            P("section", None, "tensor"),
            P("section", "dp", "tensor"),
            P("section", "dp", "tensor"),
            P("section", "tensor"),
            P("section", "dp", "tensor"),
            P("section", None, None),
        ),
        check_vma=False,
    )
```

```python
import functools
import math

import jax
import jax.numpy as jnp
from jax import lax
from jax.experimental import pallas as pl
from jax.experimental.pallas import tpu as pltpu
from jax.sharding import PartitionSpec as P

HEAD = 64
LHEAD = 16
MESH = pl.DeviceIdType.MESH
bf16 = jnp.bfloat16
f32 = jnp.float32
norm_epsilon = 1e-05
masked_score = -1e30
LANES = 128
SMALL = 1024
STEPS = 12


def mm(left, right, left_axis, right_axis):
    return lax.dot_general(
        left, right, (((left_axis,), (right_axis,)), ((), ())), preferred_element_type=f32
    )


def flip(index, bit):
    return index + bit - 2 * bit * lax.rem(lax.div(index, bit), 2)


def loop(start, stop, body):
    lax.fori_loop(start, stop, lambda i, carry: (body(i), carry)[1], 0)


def at(start, size):
    return pl.ds(pl.multiple_of(start, 16), size)


def lanes_at(start, size):
    return pl.ds(pl.multiple_of(start, LANES), size)


def kernel(
    dp,
    z_inside,
    text_in, lay_in, text_cot, lay_cot, att_t, out_t, exp_t, shr_t, att_l, out_l, exp_l, shr_l,
    bias_t, bias_l, off_t, off_l, vec_t, vec_l, lengths,
    text_out, lay_out, text_back, lay_back, sm_out,
    zs_t, zs_l, zr_t, zr_l, zh_t, zh_l, gb_t, gb_l, rz_t, rz_l, rh_t, rh_l, r1_t, r1_l, r2_t, r2_l, ro_t, ro_l, p_keep,
    w_t, w_l, small, vecs, own_small, own_vec, key_bias, rows_t, rows_l, x_fm, qkv_t, qkv_l, probs,
    ctx_t, ctx_l, xh1, n1b, xh2, act, gp, stats, acc, exs, exr, tmpb, g_fm, dup, dqkv, cols,
    stg_t, stg_l, zv_t, zv_l, tv_t, tv_l, fv_t, fv_l, smsg, srec, ssum, szr,
    ag_recv, ag_own, ag_fwd, vec_sem, row_sem, ex_send, ex_recv, out_sem, stg_sem, p_sem,
    rz_send, rz_recv, s1_send, d_send, r1_recv, s2_send, s2_recv, so_send, so_recv, z_send, z_recv, zh_recv,
    zv_sem, tv_sem, fv_sem,
    sm_send, sm_recv, sz_send, sz_recv, so_sem,
):
    c = lax.axis_index("section")
    d = lax.axis_index("dp")
    t = lax.axis_index("tensor")
    t1, t2 = flip(t, 1), flip(t, 2)
    t3 = flip(t1, 2)
    xb = lax.rem(t, 2)
    zp = lax.rem(d, 2)
    tf = t1 + zp * (t2 - t1)
    td = t2 + zp * (t1 - t2)
    dz = flip(d, 1)
    tw = text_in.shape[2]
    lw = lay_in.shape[1]
    width = tw + lw
    tokens = x_fm.shape[2]
    half = tokens // 2
    quarter = tokens // 4
    hid_t, hid_l = exp_t.shape[1], exp_l.shape[1]
    hs, ls = out_t.shape[0], out_l.shape[0]
    heads = hs // HEAD
    blocks = tokens // LANES
    tq, lq = tw // 4, lw // 4
    streams = ((0, tw), (tw, lw))
    z_peers = [lax.rem(d + r, dp) for r in range(1, dp)] if z_inside else [dz]

    def on(core, task, *args):
        @pl.when(c == core)
        def _():
            task(*args)

    def remote(src, dst, send, recv, device):
        return pltpu.make_async_remote_copy(
            src_ref=src, dst_ref=dst, send_sem=send, recv_sem=recv, device_id=device, device_id_type=MESH
        )

    def local_copy(src, dst, sem):
        return pltpu.make_async_copy(src, dst, sem)

    def landed(ref, sem):
        pltpu.make_async_copy(ref, ref, sem).wait()

    def start(copies):
        for copy in copies:
            copy.start()

    def wait(copies):
        for copy in copies:
            copy.wait()

    barrier = pltpu.get_barrier_semaphore()
    peers = [(1 - c, d, t)] + [(k, d, other) for other in (t1, t2, t3) for k in range(2)] + [(c, z, t) for z in z_peers]
    for peer in peers:
        pl.semaphore_signal(barrier, inc=1, device_id=peer, device_id_type=MESH)

    own_vec[...] = jnp.zeros(own_vec.shape, f32)
    own_vec[0:1, 0:hid_t] = off_t[...].astype(f32)
    own_vec[0:1, hid_t : hid_t + hid_l] = off_l[...].astype(f32)
    own_vec[1:2, 0:hs] = bias_t[0:1].astype(f32)
    own_vec[1:2, 2 * hs : 3 * hs] = bias_t[1:2].astype(f32)
    own_vec[1:2, 3 * hs : 3 * hs + ls] = bias_l[0:1].astype(f32)
    own_vec[1:2, 3 * hs + 2 * ls : 3 * hs + 3 * ls] = bias_l[1:2].astype(f32)
    own_small[...] = own_vec[...].astype(bf16)
    own_vec[0:6, 0:tw] = vec_t[...].astype(f32)
    own_vec[0:6, tw:width] = vec_l[...].astype(f32)
    pl.semaphore_wait(barrier, len(peers))
    other = (1 - c, d, t)

    def row_copies(text, lay, text_to, lay_to, base):
        mine, theirs = xb * half, (1 - xb) * half
        part = c * quarter
        own = [
            local_copy(text.at[xb], text_to.at[at(mine, half)], row_sem.at[base, 0]),
            local_copy(lay.at[xb], lay_to.at[:, lanes_at(mine, half)], row_sem.at[base + 1, 0]),
        ]
        away = [
            remote(
                text.at[1 - xb, at(part, quarter)], text_to.at[at(mine + part, quarter)],
                row_sem.at[base, 1], row_sem.at[base, 2], (c, d, t1),
            ),
            remote(
                lay.at[1 - xb, :, lanes_at(part, quarter)], lay_to.at[:, lanes_at(mine + part, quarter)],
                row_sem.at[base + 1, 1], row_sem.at[base + 1, 2], (c, d, t1),
            ),
        ]
        text_part = text_to.at[at(theirs + part, quarter)]
        lay_part = lay_to.at[:, lanes_at(theirs + part, quarter)]
        across = [
            remote(text_part, text_part, row_sem.at[base, 3], row_sem.at[base, 4], other),
            remote(lay_part, lay_part, row_sem.at[base + 1, 3], row_sem.at[base + 1, 4], other),
        ]
        return own, away, across

    cot_t = fv_t.at[0, pl.ds(0, tokens)]
    in_rows = row_copies(text_in, lay_in, rows_t, x_fm.at[0, pl.ds(tw, lw)], 0)
    cot_rows = row_copies(text_cot, lay_cot, cot_t, g_fm.at[pl.ds(tw, lw)], 2)

    def rows_begin(copies):
        own, away, across = copies
        start(away + own)

    def rows_cross(copies):
        own, away, across = copies
        wait(away)
        start(across)

    def rows_arrive(copies):
        own, away, across = copies
        wait(own + across)

    text_sources = [att_t.at[pl.ds(j * hs, hs)] for j in range(3)] + [out_t]
    text_sources += [exp_t.at[pl.ds(j * hs, hs)] for j in range(4)] + [shr_t.at[pl.ds(j * hs, hs)] for j in range(3)]
    hh = hs // 2
    text_sources.append(shr_t.at[pl.ds(3 * hs, hh)])
    last_piece = 17
    lay_sources = {12: att_l, 13: out_l, 14: exp_l, 15: shr_l}
    lay_places = {12: (0, 0, 3 * ls), 13: (0, 3 * ls, ls), 14: (1, 0, lw), 15: (2, 0, lw)}
    riders = {0: [12, 16], 3: [13], 4: [14], 8: [15]}

    def source(p):
        if p < STEPS:
            return text_sources[p]
        if p == last_piece:
            return shr_t.at[pl.ds(3 * hs + hh, hh)]
        return lay_sources[p] if p < 16 else own_small

    def place(layer, slot, p):
        if p < STEPS:
            return w_t.at[layer, slot, p // 4, pl.ds((p % 4) * hs, hh if p == STEPS - 1 else hs)]
        if p == last_piece:
            return w_t.at[layer, slot, 2, pl.ds(3 * hs + hh, hh)]
        if p < 16:
            which, first, size = lay_places[p]
            return w_l.at[layer, slot, which, pl.ds(first, size)]
        return small.at[layer, slot]

    def pieces(j):
        return [last_piece] if j == STEPS else [j] + riders.get(j, [])

    all_pieces = [p for j in range(STEPS + 1) for p in pieces(j)]

    def own_first(p):
        return remote(
            source(p), place(c, 1 - zp, p), ag_own.at[p, 0], ag_recv.at[c, 1 - zp, p], (zp, d, tf)
        )

    def own_core(p):
        return remote(source(p), place(1, 0, p), ag_own.at[p, 1], ag_recv.at[1, 0, p], (0, d, t))

    def own_local(p):
        return local_copy(source(p), place(0, 0, p), ag_recv.at[0, 0, p])

    def forwards(layer, p):
        return [
            remote(
                place(layer, 1 - zp, p), place(layer, 1, p),
                ag_fwd.at[p, 0], ag_recv.at[layer, 1, p], (1, d, td),
            ),
            remote(
                place(layer, 1 - zp, p), place(layer, 1 - zp, p),
                ag_fwd.at[p, 1], ag_recv.at[layer, 1 - zp, p], (zp, dz, t),
            ),
        ]

    def fw(layer, *steps):
        @pl.when(c == zp)
        def _():
            for j in steps:
                for p in pieces(j):
                    landed(place(layer, 1 - zp, p), ag_recv.at[layer, 1 - zp, p])
                    if layer == 1:
                        for copy in forwards(0, p):
                            copy.wait_send()
                    start(forwards(layer, p))

    def need(layer, *steps):
        for j in steps:
            for p in pieces(j):
                landed(place(layer, zp, p), ag_recv.at[layer, zp, p])

        @pl.when(c != zp)
        def _():
            for j in steps:
                for p in pieces(j):
                    landed(place(layer, 1 - zp, p), ag_recv.at[layer, 1 - zp, p])

    vec_copies = [
        local_copy(own_vec, vecs.at[c], vec_sem.at[0]),
        remote(own_vec, vecs.at[c], vec_sem.at[1], vec_sem.at[2], other),
    ]

    early = [p for j in range(3) for p in pieces(j)]

    @pl.when(c == 0)
    def _():
        start([own_first(p) for p in early])

    rows_begin(in_rows)
    start(vec_copies)
    pl.when(zp == 1)(lambda: rows_begin(cot_rows))

    @pl.when(c == 0)
    def _():
        start([own_first(p) for p in all_pieces if p not in early])

    @pl.when(c == 0)
    def _():
        start([own_local(p) for p in all_pieces])

    @pl.when(c == 1)
    def _():
        start([own_core(p) for p in all_pieces])

    def start_second_layer():
        @pl.when(c == 1)
        def _():
            start([own_first(p) for p in all_pieces])

    page_len = lengths[xb, lax.div(t, 2)]
    positions = lax.broadcasted_iota(jnp.int32, key_bias.shape, 0)
    key_bias[...] = jnp.where(positions < page_len, 0.0, masked_score).astype(f32)
    smsg[...] = jnp.zeros(smsg.shape, f32)
    ones = jnp.ones((8, tokens), bf16)
    wait(vec_copies)

    def load_columns(layer):
        for k in range(2):
            cols[k] = small[layer, k].astype(f32).T
        cols[2] = vecs[layer].T

    def column(k, first, size, lane):
        return cols[k, pl.ds(first, size), lane : lane + 1]

    def exchange_copy(n):
        return remote(exs, exr.at[n % 2], ex_send.at[0], ex_recv.at[n % 2], other)

    def exchanged(n, first, size, lanes):
        return exs[pl.ds(first, size), lanes].astype(f32) + exr[n % 2, pl.ds(first, size), lanes].astype(f32)

    def project(layer, s):
        mixed = mm(w_t[layer, s, 0, 0 : 3 * hs], x_fm[layer, 0:tw], 1, 0)
        qkv_t[layer, s] = (mixed + cols[s, 0 : 3 * hs, 1:2]).astype(bf16)
        mixed = mm(w_l[layer, s, 0, 0 : 3 * ls], x_fm[layer, tw:width], 1, 0)
        qkv_l[layer, s] = (mixed + cols[s, 3 * hs : 3 * hs + 3 * ls, 1:2]).astype(bf16)

    def head_rows(layer, s, part, h):
        return (
            qkv_t[layer, s, at(part * hs + h * HEAD, HEAD)],
            qkv_l[layer, s, at(part * ls + h * LHEAD, LHEAD)],
        )

    def query(layer, s, h):
        text, lay = head_rows(layer, s, 0, h)
        return jnp.concatenate([text * HEAD**-0.5, lay * LHEAD**-0.5], axis=0).astype(bf16)

    def attend_forward(layer, i):
        s, h = lax.div(i, heads), lax.rem(i, heads)
        keys = jnp.concatenate(head_rows(layer, s, 1, h), axis=0)
        values = jnp.concatenate(head_rows(layer, s, 2, h), axis=0)
        scores = mm(keys, query(layer, s, h), 0, 0) + key_bias[:, 0:1]
        exponent = jnp.exp(scores - jnp.max(scores, axis=0, keepdims=True))
        low = (exponent * (1.0 / jnp.sum(exponent, axis=0, keepdims=True))).astype(bf16)
        probs[i] = low
        context = mm(values, low, 1, 0).astype(bf16)
        ctx_t[layer, s, at(h * HEAD, HEAD)] = context[0:HEAD]
        ctx_l[layer, s, at(h * LHEAD, LHEAD)] = context[HEAD:]

    def attention_partial(layer):
        exs[0:tw] = (
            mm(w_t[layer, 0, 0, 3 * hs : 4 * hs], ctx_t[layer, 0], 0, 0)
            + mm(w_t[layer, 1, 0, 3 * hs : 4 * hs], ctx_t[layer, 1], 0, 0)
        ).astype(bf16)
        exs[tw:width] = (
            mm(w_l[layer, 0, 0, 3 * ls : 4 * ls], ctx_l[layer, 0], 0, 0)
            + mm(w_l[layer, 1, 0, 3 * ls : 4 * ls], ctx_l[layer, 1], 0, 0)
        ).astype(bf16)

    def normalize(hidden):
        center = hidden - jnp.mean(hidden, axis=0, keepdims=True)
        scale = lax.rsqrt(jnp.mean(center * center, axis=0, keepdims=True) + norm_epsilon)
        return center * scale, scale

    def norm_forward(layer, n, which, base, hat_ref, finish):
        def block(b):
            lanes = lanes_at(b * LANES, LANES)
            for k, (first, size) in enumerate(streams):
                hidden = base(first, size, lanes) + exchanged(n, first, size, lanes)
                hat, scale = normalize(hidden + column(2, first, size, 3 * which))
                hat_ref[layer, pl.ds(first, size), lanes] = hat.astype(bf16)
                row = 2 * which + k
                stats[layer, row : row + 1, lanes] = scale
                result = hat * column(2, first, size, 3 * which + 1) + column(2, first, size, 3 * which + 2)
                finish(first, size, lanes, result)

        loop(0, blocks, block)

    def first_norm(layer, n):
        def finish(first, size, lanes, result):
            acc[pl.ds(first, size), lanes] = result
            n1b[layer, pl.ds(first, size), lanes] = result.astype(bf16)

        norm_forward(
            layer, n, 0, lambda s, z, lanes: x_fm[layer, pl.ds(s, z), lanes].astype(f32), xh1, finish
        )

    def second_norm(layer, n, dest):
        def finish(first, size, lanes, result):
            dest[pl.ds(first, size), lanes] = result.astype(bf16)

        norm_forward(layer, n, 1, lambda s, z, lanes: acc[pl.ds(s, z), lanes], xh2, finish)

    def gelu_pair(raised):
        cdf = 0.5 * (1.0 + lax.erf(raised * math.sqrt(0.5)))
        slope = cdf + raised * (jnp.exp(-0.5 * raised * raised) * (1.0 / math.sqrt(2.0 * math.pi)))
        return (raised * cdf).astype(bf16), slope.astype(bf16)

    hb = 256
    per_slot = hid_t // hb

    def expand_block(layer, i):
        s, b = lax.div(i, per_slot), lax.rem(i, per_slot)
        rows = lanes_at(b * hb, hb)
        raised = mm(w_t[layer, s, 1, :, rows], n1b[layer, 0:tw], 0, 0) + cols[s, rows, 0:1]
        act[layer, s, rows], gp[layer, s, rows] = gelu_pair(raised)

    def expand_lay(layer, s):
        raised = mm(w_l[layer, s, 1], n1b[layer, tw:width], 0, 0) + cols[s, hid_t : hid_t + hid_l, 0:1]
        act[layer, s, hid_t:], gp[layer, s, hid_t:] = gelu_pair(raised)

    def shrink_partial(layer):
        exs[0:tw] = (
            mm(w_t[layer, 0, 2], act[layer, 0, 0:hid_t], 1, 0) + mm(w_t[layer, 1, 2], act[layer, 1, 0:hid_t], 1, 0)
        ).astype(bf16)
        exs[tw:width] = (
            mm(w_l[layer, 0, 2], act[layer, 0, hid_t:], 1, 0) + mm(w_l[layer, 1, 2], act[layer, 1, hid_t:], 1, 0)
        ).astype(bf16)

    def rows_out(base, text_to, lay_to):
        mine, theirs = xb * half, (1 - xb) * half
        pairs = (
            (rows_t.at[at(mine, half)], rows_t.at[at(theirs, half)], text_to),
            (rows_l.at[:, lanes_at(mine, half)], rows_l.at[:, lanes_at(theirs, half)], lay_to),
        )
        copies = []
        for k, (own, away, dest) in enumerate(pairs):
            copies.append(local_copy(own, dest.at[xb], out_sem.at[base + k, 0]))
            copies.append(
                remote(away, dest.at[xb], out_sem.at[base + k, 1], out_sem.at[base + k, 2], (c, d, t1))
            )
        return copies

    def stage_rows(layer, value):
        @pl.when(c == layer)
        def _():
            rows_t[...] = value[0:tw].T
            rows_l[...] = value[tw:width]

    def send_rows(layer, base, dest_pair, value):
        stage_rows(layer, value)

        @pl.when(c == layer)
        def _():
            start(rows_out(base, *dest_pair))

    def finish_rows(layer, base, dest_pair):
        @pl.when(c == layer)
        def _():
            wait(rows_out(base, *dest_pair))

    out_pair, back_pair = (text_out, lay_out), (text_back, lay_back)
    fw(0, 0)
    fw(0, 1)
    fw(0, 2)
    rows_cross(in_rows)
    need(0, 0)
    load_columns(0)
    fw(0, 3)
    need(0, 1)
    rows_arrive(in_rows)
    x_fm[0, 0:tw] = rows_t[...].T
    need(0, 2)

    p_store = local_copy(probs, p_keep, p_sem.at[0])
    p_load = local_copy(p_keep, probs, p_sem.at[1])

    for layer in range(2):
        last = layer == 1
        if last:
            fw(layer, 2)
            need(layer, 1)
            fw(layer, 3)
            need(layer, 2)
        project(layer, 0)
        fw(layer, 4)
        project(layer, 1)
        if last:
            p_store.wait()
        fw(layer, 5)
        head = functools.partial(attend_forward, layer)
        loop(0, 2, head)
        fw(layer, 6)
        loop(2, 4, head)
        fw(layer, 7)
        loop(4, 6, head)
        if not last:
            p_store.start()
        need(layer, 3)
        attention_partial(layer)
        swap = exchange_copy(2 * layer)
        swap.start()
        fw(layer, 8)
        swap.wait()
        first_norm(layer, 2 * layer)
        fw(layer, 9)
        need(layer, 4, 5, 6, 7)
        expand = functools.partial(expand_block, layer)
        loop(0, per_slot, expand)
        fw(layer, 10)
        if not last:
            need(layer, 8, 9)
            start_second_layer()
        loop(per_slot, 2 * per_slot, expand)
        fw(layer, 11)
        fw(layer, 12)
        if last:
            pl.when(zp == 0)(lambda: rows_begin(cot_rows))
            stage_rows(0, x_fm.at[1])
        loop(0, 2, functools.partial(expand_lay, layer))
        if last:
            need(layer, 8, 9, 10, 11, 12)
            on(0, lambda: start(rows_out(0, *out_pair)))
        else:
            need(layer, 10)
            fw(1, 0)
            need(layer, 11, 12)
        shrink_partial(layer)
        swap = exchange_copy(2 * layer + 1)
        swap.start()
        if not last:
            fw(1, 1)
        else:
            rows_cross(cot_rows)
        swap.wait()
        if not last:
            second_norm(0, 1, x_fm.at[1])
            need(1, 0)
            load_columns(1)
        else:
            second_norm(1, 3, dup.at[0])
            rows_arrive(cot_rows)
            g_fm[0:tw] = cot_t[...].T

    def grad_store(layer, chunk, s):
        return [
            local_copy(stg_t.at[s], gb_t.at[layer, chunk, s], stg_sem.at[s, 0]),
            local_copy(stg_l.at[s], gb_l.at[layer, chunk, s], stg_sem.at[s, 1]),
        ]

    def store_grad(layer, chunk, s, text_value, lay_value):
        stg_t[s] = text_value
        stg_l[s] = lay_value
        start(grad_store(layer, chunk, s))

    groups = (
        (gb_t, rz_t, r1_t, r2_t, ro_t, zs_t, zr_t, zv_t, tv_t, fv_t, w_t, tq),
        (gb_l, rz_l, r1_l, r2_l, ro_l, zs_l, zr_l, zv_l, tv_l, fv_l, w_l, lq),
    )
    tx = t1 + c * (t2 - t1)
    near, far = 2 * zp, 2 * (1 - zp)

    def quarters(first, count, size):
        return at(first * size, count * size)

    def by_half(layer, chunk):
        return layer == 1 and chunk == 2

    def first_sends(layer, chunk, core):
        copies = []
        for g, (gb, rz, r1, r2, ro, zs, zr, zv, tv, fv, w, size) in enumerate(groups):
            if by_half(layer, chunk):
                parts = [pl.ds(0, 4 * size) if core else quarters(far, 2, size)]
            else:
                parts = [quarters(far, 2, size), quarters(near + core, 1, size)]
            for i, rows in enumerate(parts):
                copies.append(
                    remote(
                        gb.at[layer, chunk, 1 - core, rows], r2.at[chunk, core, rows],
                        s1_send.at[layer, chunk, g, i], s2_recv.at[chunk, core, i, g],
                        (layer, d, t2 if core else t1),
                    )
                )
        return copies[::2] + copies[1::2] if len(copies) > 2 else copies

    def direct(layer, chunk, i):
        for core in range(2):
            on(core, lambda: start(first_sends(layer, chunk, core)[2 * i : 2 * i + 2]))

    def own_sends(chunk):
        return [
            remote(gb.at[1, chunk, 0], ro.at[chunk], so_send.at[chunk, g], so_recv.at[chunk, g], other)
            for g, (gb, rz, r1, r2, ro, *_) in enumerate(groups)
        ]

    def pair_sends(layer, chunk):
        return [
            remote(
                gb.at[layer, chunk, 1, quarters(far, 2, size)], rz.at[layer, chunk],
                rz_send.at[layer, chunk, g], rz_recv.at[layer, chunk, g], (1, dz, t),
            )
            for g, (gb, rz, *_, size) in enumerate(groups)
        ]

    def diagonal_sends(layer, chunk):
        copies = []
        for g, (gb, rz, r1, *_, size) in enumerate(groups):
            if by_half(layer, chunk):
                parts = [(quarters(near, 2, size), (rh_t, rh_l)[g].at[chunk], (0, d, t2))]
            else:
                come = r1.at[3 * layer + chunk]
                parts = [(quarters(near + i, 1, size), come, (1 - i, d, (t1, t2)[i])) for i in range(2)]
            for i, (rows, dest, device) in enumerate(parts):
                copies.append(
                    remote(
                        gb.at[layer, chunk, 1, rows], dest,
                        d_send.at[layer, chunk, g, i], r1_recv.at[layer, chunk, g], device,
                    )
                )
        return copies

    def grads_go(layer, chunk, *slots):
        for s in slots or (1, 0):
            wait(grad_store(layer, chunk, s))
            if s == 1:
                on(1, lambda: start(pair_sends(layer, chunk)))
            elif layer == 1:
                on(0, lambda: start(own_sends(chunk)))

    def pair_loads(layer, chunk):
        copies = []
        for g, (gb, rz, r1, r2, ro, zs, zr, zv, tv, fv, w, size) in enumerate(groups):
            copies.append(local_copy(gb.at[layer, chunk, 1, quarters(near, 2, size)], zv.at[0], zv_sem.at[g, 0]))
            copies.append(local_copy(rz.at[layer, chunk], zv.at[1], zv_sem.at[g, 1]))
        return copies

    def pair_stores(layer, chunk):
        return [
            local_copy(zv.at[0], gb.at[layer, chunk, 1, quarters(near, 2, size)], zv_sem.at[g, 2])
            for g, (gb, rz, r1, r2, ro, zs, zr, zv, tv, fv, w, size) in enumerate(groups)
        ]

    def pair_load(layer, chunk):
        @pl.when(c == 1)
        def _():
            for g, (gb, rz, *_) in enumerate(groups):
                landed(rz.at[layer, chunk], rz_recv.at[layer, chunk, g])
            start(pair_loads(layer, chunk))

    def pair_add(layer, chunk):
        @pl.when(c == 1)
        def _():
            wait(pair_loads(layer, chunk))
            for zv in (zv_t, zv_l):
                zv[0] = (zv[0].astype(f32) + zv[1].astype(f32)).astype(bf16)
            start(pair_stores(layer, chunk))

    def pair_send(layer, chunk):
        @pl.when(c == 1)
        def _():
            wait(pair_stores(layer, chunk))
            start(diagonal_sends(layer, chunk))

    def transit_parts(layer, chunk):
        parts = []
        for g, (gb, rz, r1, r2, ro, zs, zr, zv, tv, fv, w, size) in enumerate(groups):
            if by_half(layer, chunk):
                parts.append((gb.at[1, chunk, 1, quarters(near, 2, size)], (rh_t, rh_l)[g].at[chunk], zv, zv_sem))
            else:
                rows = quarters(near + 1 - c, 1, size)
                parts.append((gb.at[layer, chunk, 1 - c, rows], r1.at[3 * layer + chunk], tv, tv_sem))
        return parts

    def transit_loads(layer, chunk):
        copies = []
        for g, (mine, come, held, sem) in enumerate(transit_parts(layer, chunk)):
            copies.append(local_copy(mine, held.at[0], sem.at[g, 0]))
            copies.append(local_copy(come, held.at[1], sem.at[g, 1]))
        return copies

    def transit_stores(layer, chunk):
        return [
            local_copy(held.at[0], mine, sem.at[g, 2])
            for g, (mine, come, held, sem) in enumerate(transit_parts(layer, chunk))
        ]

    def second_sends(layer, chunk):
        copies = []
        for g, (mine, come, held, sem) in enumerate(transit_parts(layer, chunk)):
            gb, rz, r1, r2, *_, size = groups[g]
            if by_half(layer, chunk):
                dest, device, way, which = r2.at[chunk, 0, quarters(near, 2, size)], (1, d, t1), 0, 1
            else:
                dest, device = r2.at[chunk, c, quarters(near + 1 - c, 1, size)], (layer, d, tx)
                way, which = c, 2
            copies.append(
                remote(mine, dest, s2_send.at[layer, chunk, g], s2_recv.at[chunk, way, which, g], device)
            )
        return copies

    def transit_load(layer, chunk):
        for g, (mine, come, held, sem) in enumerate(transit_parts(layer, chunk)):
            landed(come, r1_recv.at[layer, chunk, g])
        start(transit_loads(layer, chunk))

    def transit_add(layer, chunk):
        wait(transit_loads(layer, chunk))
        for mine, come, held, sem in transit_parts(layer, chunk):
            held[0] = (held[0].astype(f32) + held[1].astype(f32)).astype(bf16)
        start(transit_stores(layer, chunk))

    def transit_send(layer, chunk):
        wait(transit_stores(layer, chunk))
        start(second_sends(layer, chunk))

    def final_loads(layer, chunk, stage):
        copies = []
        for g, (gb, rz, r1, r2, ro, zs, zr, zv, tv, fv, w, size) in enumerate(groups):
            rows = quarters(near if stage else far, 2, size)
            own = ro.at[chunk, rows] if layer == 1 else gb.at[0, chunk, 0, rows]
            terms = [
                (own, w.at[1, 0, chunk, rows]),
                (r2.at[chunk, 0, rows], w.at[1, 1, chunk, rows]),
                (r2.at[chunk, 1, rows], fv.at[chunk, rows]),
            ]
            if z_inside and stage == 1:
                terms.append(((zh_t, zh_l)[g].at[chunk], fv.at[chunk, quarters(far, 2, size)]))
            for i, (src, dst) in enumerate(terms):
                copies.append(local_copy(src, dst, fv_sem.at[g, i]))
        return copies

    def final_load(layer, chunk, stage):
        @pl.when(c == layer)
        def _():
            for g, (gb, rz, r1, r2, ro, zs, zr, zv, tv, fv, w, size) in enumerate(groups):

                def came(way, first, count, which):
                    landed(r2.at[chunk, way, quarters(first, count, size)], s2_recv.at[chunk, way, which, g])

                if layer == 1 and stage == 0:
                    landed(ro.at[chunk], so_recv.at[chunk, g])
                if by_half(layer, chunk) and stage == 0:
                    came(0, far, 2, 0)
                    came(1, 0, 4, 0)
                elif by_half(layer, chunk):
                    came(0, near, 2, 1)
                else:
                    for way in range(2):
                        if stage == 0:
                            came(way, far, 2, 0)
                        else:
                            came(way, near + way, 1, 1)
                            came(way, near + 1 - way, 1, 2)
                if z_inside and stage == 1:
                    landed((zh_t, zh_l)[g].at[chunk], zh_recv.at[chunk, g])
            start(final_loads(layer, chunk, stage))

    def half_send(chunk, g):
        gb, rz, r1, r2, ro, zs, zr, zv, tv, fv, w, size = groups[g]
        return remote(
            w.at[1, 0, chunk, quarters(far, 2, size)], (zh_t, zh_l)[g].at[chunk],
            z_send.at[chunk, 0, g], zh_recv.at[chunk, g], (c, dz, t),
        )

    def quarter_send(chunk, i, g, away):
        gb, rz, r1, r2, ro, zs, zr, zv, tv, fv, w, size = groups[g]
        piece, dest = w.at[1, 0, chunk, quarters(near + i, 1, size)], zr.at[chunk, lax.div(d, 2)]
        recv = z_recv.at[chunk, lax.div(d, 2), g]
        if away:
            return remote(piece, dest, z_send.at[chunk, 1 + i, g], recv, (c, near + i, t))
        return local_copy(piece, dest, recv)

    def sum_stores(chunk, stage):
        copies = []
        for g, (gb, rz, r1, r2, ro, zs, zr, zv, tv, fv, w, size) in enumerate(groups):
            rows = quarters(near if stage else far, 2, size)
            copies.append(local_copy(w.at[1, 0, chunk, rows], zs.at[chunk, rows], z_send.at[chunk, stage, g]))
        return copies

    def final_add(layer, chunk, stage):
        @pl.when(c == layer)
        def _():
            wait(final_loads(layer, chunk, stage))
            for gb, rz, r1, r2, ro, zs, zr, zv, tv, fv, w, size in groups:
                rows = quarters(near if stage else far, 2, size)
                total = w[1, 0, chunk, rows].astype(f32) + w[1, 1, chunk, rows].astype(f32)
                total = total + fv[chunk, rows].astype(f32)
                if z_inside and stage == 1:
                    total = total + fv[chunk, quarters(far, 2, size)].astype(f32)
                w[1, 0, chunk, rows] = total.astype(bf16)
            if not z_inside:
                start(sum_stores(chunk, stage))
            elif stage == 0:
                start([half_send(chunk, g) for g in range(2)])
            else:
                for i in range(2):

                    @pl.when(near + i != d)
                    def _():
                        start([quarter_send(chunk, i, g, True) for g in range(2)])

                    @pl.when(near + i == d)
                    def _():
                        start([quarter_send(chunk, i, g, False) for g in range(2)])

    def sums_done():
        for chunk in range(3):
            if not z_inside:
                wait(sum_stores(chunk, 0) + sum_stores(chunk, 1))
                continue
            for g in range(2):
                half_send(chunk, g).wait_send()
                for i in range(2):

                    @pl.when(near + i != d)
                    def _():
                        quarter_send(chunk, i, g, True).wait_send()

                for k in range(2):
                    landed(groups[g][6].at[chunk, k], z_recv.at[chunk, k, g])

    def small_sends(layer):
        zero = [remote(smsg.at[layer, 1], srec.at[0], sm_send.at[layer, 0], sm_recv.at[0], (layer, d, t1))]
        if layer == 1:
            zero.append(remote(smsg.at[1, 0], srec.at[3], sm_send.at[1, 1], sm_recv.at[3], other))
        one = [
            remote(smsg.at[layer, 0], srec.at[1], sm_send.at[layer, 0], sm_recv.at[1], (layer, d, t2)),
            remote(smsg.at[layer, 1], srec.at[2], sm_send.at[layer, 1], sm_recv.at[2], (layer, d, t3)),
        ]
        return zero, one

    def small_go(layer):
        zero, one = small_sends(layer)

        @pl.when(c == 0)
        def _():
            start(zero)

        @pl.when(c == 1)
        def _():
            start(one)

    def small_z():
        if not z_inside:
            return []
        return [
            remote(ssum, szr.at[r - 1], sz_send.at[r - 1], sz_recv.at[r - 1], (c, lax.rem(d + r, dp), t))
            for r in range(1, dp)
        ]

    def small_total(layer):
        @pl.when(c == layer)
        def _():
            for i in range(3):
                landed(srec.at[i], sm_recv.at[i])
            if layer == 1:
                landed(srec.at[3], sm_recv.at[3])
                own = srec[3]
            else:
                own = smsg[0, 0]
            ssum[...] = own + srec[0] + srec[1] + srec[2]
            start(small_z())

    def row_sums(ref):
        return mm(ones, ref[...], 1, 1)[0:1]

    def vector_sum(layer, row, value):
        for s in range(2):
            smsg[layer, s, 8 + row : 9 + row, 0:width] = value

    def norm_backward(layer, which, hat_ref, incoming):
        def block(b):
            lanes = lanes_at(b * LANES, LANES)
            for k, (first, size) in enumerate(streams):
                grad = incoming(first, size, lanes)
                hat = hat_ref[layer, pl.ds(first, size), lanes].astype(f32)
                row = 2 * which + k
                scale = stats[layer, row : row + 1, lanes]
                gained = grad * column(2, first, size, 3 * which + 1)
                mean_grad = jnp.mean(gained, axis=0, keepdims=True)
                mean_both = jnp.mean(gained * hat, axis=0, keepdims=True)
                result = scale * (gained - mean_grad - hat * mean_both)
                acc[pl.ds(first, size), lanes] = result
                tmpb[pl.ds(first, size), lanes] = result.astype(bf16)
                exs[pl.ds(first, size), lanes] = (grad * hat).astype(bf16)
                g_fm[pl.ds(first, size), lanes] = grad.astype(bf16)

        loop(0, blocks, block)

    def norm_sums(layer, which):
        vector_sum(layer, 3 * which + 1, row_sums(exs))
        vector_sum(layer, 3 * which + 2, row_sums(g_fm))
        vector_sum(layer, 3 * which, row_sums(tmpb))

    def ffn_backward(layer):
        def text_block(i):
            s, b = lax.div(i, per_slot), lax.rem(i, per_slot)
            rows = lanes_at(b * hb, hb)
            back = mm(w_t[layer, s, 2, :, rows], tmpb[0:tw], 0, 0)
            dup[s, rows] = (back * gp[layer, s, rows].astype(f32)).astype(bf16)

        loop(0, 2 * per_slot, text_block)

        def lay_block(s):
            back = mm(w_l[layer, s, 2], tmpb[tw:width], 0, 0)
            dup[s, hid_t:] = (back * gp[layer, s, hid_t:].astype(f32)).astype(bf16)

        loop(0, 2, lay_block)

    def shrink_grads(layer, s):
        store_grad(
            layer, 2, s,
            mm(tmpb[0:tw], act[layer, s, 0:hid_t], 1, 1).astype(bf16),
            mm(tmpb[tw:width], act[layer, s, hid_t:], 1, 1).astype(bf16),
        )

    def expand_grads(layer, s):
        store_grad(
            layer, 1, s,
            mm(n1b[layer, 0:tw], dup[s, 0:hid_t], 1, 1).astype(bf16),
            mm(n1b[layer, tw:width], dup[s, hid_t:], 1, 1).astype(bf16),
        )

    def expand_partial(layer):
        exs[0:tw] = (
            mm(w_t[layer, 0, 1], dup[0, 0:hid_t], 1, 0) + mm(w_t[layer, 1, 1], dup[1, 0:hid_t], 1, 0)
        ).astype(bf16)
        exs[tw:width] = (
            mm(w_l[layer, 0, 1], dup[0, hid_t:], 1, 0) + mm(w_l[layer, 1, 1], dup[1, hid_t:], 1, 0)
        ).astype(bf16)

    def context_grads(layer, s):
        dup[s, 0:hs] = mm(w_t[layer, s, 0, 3 * hs : 4 * hs], tmpb[0:tw], 1, 0).astype(bf16)
        dup[s, hs : hs + ls] = mm(w_l[layer, s, 0, 3 * ls : 4 * ls], tmpb[tw:width], 1, 0).astype(bf16)

    def attend_backward(layer, i):
        s, h = lax.div(i, heads), lax.rem(i, heads)
        queries = query(layer, s, h)
        key_text, key_lay = head_rows(layer, s, 1, h)
        keys = jnp.concatenate([key_text * HEAD**-0.5, key_lay * LHEAD**-0.5], axis=0).astype(bf16)
        values = jnp.concatenate(head_rows(layer, s, 2, h), axis=0)
        grads = jnp.concatenate([dup[s, at(h * HEAD, HEAD)], dup[s, at(hs + h * LHEAD, LHEAD)]], axis=0)
        low = probs[i]
        prob = low.astype(f32)
        dprob = mm(values, grads, 0, 0)
        inner = jnp.sum(dprob * prob, axis=0, keepdims=True)
        dscore = (prob * (dprob - inner)).astype(bf16)
        results = (mm(keys, dscore, 1, 0), mm(queries, dscore, 1, 1), mm(grads, low, 1, 1))
        for part, result in enumerate(results):
            result = result.astype(bf16)
            dqkv[s, at(part * hs + h * HEAD, HEAD)] = result[0:HEAD]
            dqkv[s, at(3 * hs + part * ls + h * LHEAD, LHEAD)] = result[HEAD:]

    def attend_grads(layer, s):
        text = jnp.concatenate(
            [mm(x_fm[layer, 0:tw], dqkv[s, 0 : 3 * hs], 1, 1), mm(tmpb[0:tw], ctx_t[layer, s], 1, 1)], axis=1
        )
        lay = jnp.concatenate(
            [mm(x_fm[layer, tw:width], dqkv[s, 3 * hs :], 1, 1), mm(tmpb[tw:width], ctx_l[layer, s], 1, 1)], axis=1
        )
        store_grad(layer, 0, s, text.astype(bf16), lay.astype(bf16))

    def attend_partial(layer):
        exs[0:tw] = (
            mm(w_t[layer, 0, 0, 0 : 3 * hs], dqkv[0, 0 : 3 * hs], 0, 0)
            + mm(w_t[layer, 1, 0, 0 : 3 * hs], dqkv[1, 0 : 3 * hs], 0, 0)
        ).astype(bf16)
        exs[tw:width] = (
            mm(w_l[layer, 0, 0, 0 : 3 * ls], dqkv[0, 3 * hs :], 0, 0)
            + mm(w_l[layer, 1, 0, 0 : 3 * ls], dqkv[1, 3 * hs :], 0, 0)
        ).astype(bf16)

    def small_sums(layer, s, row, ref, size):
        smsg[layer, s, row : row + 1, 0:size] = mm(ones, ref[s], 1, 1)[0:1]

    def first_grad(n, first, size, lanes):
        return acc[pl.ds(first, size), lanes] + exchanged(n, first, size, lanes)

    def gather_sent():
        for layer in range(2):

            @pl.when(c == layer)
            def _():
                for p in all_pieces:
                    own_first(p).wait_send()
                    if layer == 1:
                        own_core(p).wait_send()

        @pl.when(c == zp)
        def _():
            for p in all_pieces:
                for copy in forwards(1, p):
                    copy.wait_send()

    def run(*tasks):
        for task in tasks:
            task[0](*task[1:])

    Z, T, F = (pair_load, pair_add, pair_send), (transit_load, transit_add, transit_send), (final_load, final_add)
    service = {
        (1, "ffn swap"): [(direct, 1, 1, 0), (on, 0, direct, 1, 1, 1)],
        (1, "context"): [(gather_sent,), (Z[0], 1, 2)],
        (1, "heads 0"): [(Z[1], 1, 2)],
        (1, "heads 1"): [(Z[2], 1, 2), (Z[0], 1, 1), (F[0], 1, 2, 0)],
        (1, "heads 2"): [(Z[1], 1, 1)],
        (1, "attend grads"): [(Z[2], 1, 1), (F[1], 1, 2, 0)],
        (1, "swap"): [
            (on, 1, direct, 1, 1, 1), (direct, 1, 0, 0), (on, 0, direct, 1, 0, 1),
        ],
        (0, "shrink grads"): [(on, 0, direct, 0, 2, 0), (on, 0, T[0], 1, 2)],
        (0, "ffn"): [(on, 0, T[1], 1, 2)],
        (0, "expand grads"): [(on, 0, T[2], 1, 2), (on, 0, direct, 0, 2, 1), (T[0], 1, 1), (Z[0], 1, 0), (F[0], 1, 1, 0)],
        (0, "ffn swap"): [(Z[1], 1, 0), (on, 1, direct, 1, 0, 1), (T[1], 1, 1), (F[1], 1, 1, 0)],
        (0, "first norm"): [(Z[2], 1, 0), (T[2], 1, 1), (on, 1, direct, 0, 2, 0), (Z[0], 0, 2)],
        (0, "context"): [(Z[1], 0, 2)],
        (0, "heads 0"): [(Z[2], 0, 2)],
        (0, "heads 1"): [(Z[0], 0, 1), (T[0], 1, 0)],
        (0, "heads 2"): [(Z[1], 0, 1), (T[1], 1, 0), (on, 1, direct, 0, 2, 1), (on, 0, direct, 0, 1, 0)],
        (0, "attend grads"): [(Z[2], 0, 1), (T[2], 1, 0)],
        (0, "swap"): [(on, 1, direct, 0, 1, 0), (on, 0, direct, 0, 0, 0), (F[0], 1, 0, 0)],
        (0, "finished"): [(T[0], 0, 2), (F[1], 1, 0, 0), (T[1], 0, 2)],
    }

    for layer in (1, 0):
        last = layer == 0
        n = 4 + 2 * (1 - layer)

        def point(name):
            run(*service.get((layer, name), []))

        if last:
            load_columns(0)
        point("begin")
        norm_backward(layer, 1, xh2, lambda s, z, lanes: g_fm[pl.ds(s, z), lanes].astype(f32))
        point("second norm")
        for s in (1, 0):
            shrink_grads(layer, s)
        grads_go(layer, 2, 1)
        if not last:
            on(0, direct, 1, 2, 0)
        norm_sums(layer, 1)
        grads_go(layer, 2, 0)
        if not last:
            on(1, direct, 1, 2, 0)
        if not last:
            send_rows(1, 0, out_pair, dup.at[0])
        point("shrink grads")
        ffn_backward(layer)
        point("ffn")
        for s in range(2):
            expand_grads(layer, s)
        point("expand grads")
        expand_partial(layer)
        swap = exchange_copy(n)
        swap.start()
        for s in range(2):
            small_sums(layer, s, 0, dup, hid_t + hid_l)
        grads_go(layer, 1)
        point("ffn swap")
        swap.wait()
        norm_backward(layer, 0, xh1, functools.partial(first_grad, n))
        norm_sums(layer, 0)
        point("first norm")
        if last:
            p_load.wait()
        for s in range(2):
            context_grads(layer, s)
        point("context")
        head = functools.partial(attend_backward, layer)
        for i in range(3):
            loop(2 * i, 2 * i + 2, head)
            point(f"heads {i}")
        if not last:
            p_load.start()
        for s in range(2):
            attend_grads(layer, s)
        point("attend grads")
        attend_partial(layer)
        swap = exchange_copy(n + 1)
        swap.start()
        for s in range(2):
            small_sums(layer, s, 1, dqkv, 3 * hs + 3 * ls)
        small_go(layer)
        point("last grads")
        grads_go(layer, 0)
        point("swap")
        swap.wait()
        point("swapped")

        def finish(b):
            lanes = lanes_at(b * LANES, LANES)
            for first, size in streams:
                g_fm[pl.ds(first, size), lanes] = first_grad(n + 1, first, size, lanes).astype(bf16)

        loop(0, blocks, finish)
        point("finished")
        finish_rows(layer, 0, out_pair)
        stage_rows(layer, g_fm)

    def transit(layer, chunk):
        run(*((step, layer, chunk) for step in T))

    def final(layer, chunk, stage):
        run(*((step, layer, chunk, stage) for step in F))

    transit_send(0, 2)

    @pl.when(c == 0)
    def _():
        run((direct, 0, 1, 1), (final, 0, 2, 0), (transit, 0, 1), (final, 0, 1, 0), (transit, 0, 0))
        run((direct, 0, 0, 1), (small_total, 0))
        start(rows_out(2, *back_pair))
        run((final, 0, 0, 0), (final, 0, 2, 1), (final, 0, 1, 1), (final, 0, 0, 1))

    @pl.when(c == 1)
    def _():
        run(*((step, 0, 0) for step in Z), (direct, 0, 0, 0), (transit, 0, 1), (direct, 0, 1, 1))
        run((final, 1, 2, 1), (final, 1, 1, 1), (transit, 0, 0), (direct, 0, 0, 1), (final, 1, 0, 1))
        start(rows_out(2, *back_pair))
        small_total(1)

    for copy in small_z():
        copy.wait()
    if z_inside:
        for r in range(1, dp):
            ssum[...] = ssum[...] + szr[r - 1]
    sm_copy = local_copy(ssum, sm_out, so_sem.at[0])
    sm_copy.start()
    wait(rows_out(2, *back_pair))
    for layer in range(2):
        smalls = small_sends(layer)
        for core in range(2):

            @pl.when(c == core)
            def _():
                for copy in smalls[core]:
                    copy.wait_send()
                for chunk in range(3):
                    copies = first_sends(layer, chunk, core)
                    if core == 1:
                        copies += pair_sends(layer, chunk) + diagonal_sends(layer, chunk)
                    elif layer == 1:
                        copies += own_sends(chunk)
                    if core == 0 or not by_half(layer, chunk):
                        copies += second_sends(layer, chunk)
                    for copy in copies:
                        copy.wait_send()

    sums_done()
    sm_copy.wait()


def finishing(
    parts_t, parts_l, sums_in, rows_in_0, rows_in_1, rows_in_2, rows_in_3,
    rows_0, rows_1, rows_2, rows_3, att_t, out_t, exp_t, shr_t, att_l, out_l, exp_l, shr_l,
    bias_t, off_t, vec_t, bias_l, off_l, vec_l,
    zr_t, zr_l, sums, held_0, held_1, held_2, held_3, sems,
):
    pairs = ((rows_in_0, held_0), (rows_in_1, held_1), (rows_in_2, held_2), (rows_in_3, held_3))
    pairs += ((parts_t, zr_t), (parts_l, zr_l), (sums_in, sums))
    loads = [pltpu.make_async_copy(src, dst, sems.at[i]) for i, (src, dst) in enumerate(pairs)]
    for copy in loads:
        copy.start()
    pairs = ((held_0, rows_0), (held_1, rows_1), (held_2, rows_2), (held_3, rows_3))
    copies = [pltpu.make_async_copy(src, dst, sems.at[7 + i]) for i, (src, dst) in enumerate(pairs)]
    for load, copy in zip(loads[:4], copies):
        load.wait()
        copy.start()
    for load in loads[4:]:
        load.wait()
    for zr, att, out, exp, shr in ((zr_t, att_t, out_t, exp_t, shr_t), (zr_l, att_l, out_l, exp_l, shr_l)):
        totals = []
        for chunk in range(3):
            total = zr[chunk, 0].astype(f32)
            for r in range(1, zr.shape[1]):
                total = total + zr[chunk, r].astype(f32)
            totals.append(total)
        size = out.shape[1]
        for j in range(3):
            att[j] = totals[0][:, j * size : (j + 1) * size]
        out[...] = totals[0][:, 3 * size : 4 * size]
        exp[...] = totals[1]
        shr[...] = totals[2]
    hs, ls = bias_t.shape[1], bias_l.shape[1]
    ft, fl = off_t.shape[1], off_l.shape[1]
    tw, lw = vec_t.shape[2], vec_l.shape[2]
    off_t[...] = sums[0:1, 0:ft]
    off_l[...] = sums[0:1, ft : ft + fl]
    bias_t[0:1] = sums[1:2, 0:hs]
    bias_t[1:2] = sums[1:2, 2 * hs : 3 * hs]
    bias_l[0:1] = sums[1:2, 3 * hs : 3 * hs + ls]
    bias_l[1:2] = sums[1:2, 3 * hs + 2 * ls : 3 * hs + 3 * ls]
    for row in range(6):
        vec_t[row] = sums[8 + row : 9 + row, 0:tw]
        vec_l[row] = sums[8 + row : 9 + row, tw : tw + lw]
    for copy in copies:
        copy.wait()


def local(
    dp,
    text_in,
    layout_in,
    text_cot,
    layout_cot,
    lengths,
    text_attend,
    text_biases,
    text_output,
    text_expand,
    text_offset,
    text_shrink,
    text_vectors,
    layout_attend,
    layout_biases,
    layout_output,
    layout_expand,
    layout_offset,
    layout_shrink,
    layout_vectors,
):
    rows, tw = text_in.shape[1:]
    lw = layout_in.shape[2]
    width, tokens = tw + lw, 2 * rows
    hs, ls = text_output.shape[2], layout_output.shape[2]
    ft, fl = text_expand.shape[2], layout_expand.shape[2]
    zt, zl = tw // dp, lw // dp
    z_inside = dp == 4

    def shape(dims, dtype=bf16):
        return jax.ShapeDtypeStruct(dims, dtype)

    def attend_rows(attend):
        return attend[0].transpose(1, 2, 0).reshape(-1, attend.shape[1])

    hbm = pl.BlockSpec(memory_space=pltpu.HBM)
    vmem = pl.BlockSpec(memory_space=pltpu.VMEM)
    heads = hs // HEAD
    row_shapes = [shape((2, rows, tw)), shape((2, lw, rows)), shape((2, rows, tw)), shape((2, lw, rows))]
    out_shape = row_shapes + [
        shape((16, SMALL), f32),
        shape((3, tw, tw)), shape((3, lw, lw)),
        shape((3, 2, tw // 4, tw)), shape((3, 2, lw // 4, lw)), shape((3, tw // 2, tw)), shape((3, lw // 2, lw)),
        shape((2, 3, 2, tw, tw)), shape((2, 3, 2, lw, lw)),
        shape((2, 3, tw // 2, tw)), shape((2, 3, lw // 2, lw)), shape((3, tw // 2, tw)), shape((3, lw // 2, lw)),
        shape((5, tw // 4, tw)), shape((5, lw // 4, lw)),
        shape((3, 2, tw, tw)), shape((3, 2, lw, lw)),
        shape((3, tw, tw)), shape((3, lw, lw)),
        shape((2 * heads, tokens, tokens)),
    ]
    dma = pltpu.SemaphoreType.DMA
    scratch = [
        pltpu.VMEM((2, 2, 3, tw, tw), bf16),
        pltpu.VMEM((2, 2, 3, lw, lw), bf16),
        pltpu.VMEM((2, 2, 16, SMALL), bf16),
        pltpu.VMEM((2, 16, SMALL), f32),
        pltpu.VMEM((16, SMALL), bf16),
        pltpu.VMEM((16, SMALL), f32),
        pltpu.VMEM((tokens, LANES), f32),
        pltpu.VMEM((tokens, tw), bf16),
        pltpu.VMEM((lw, tokens), bf16),
        pltpu.VMEM((2, width, tokens), bf16),
        pltpu.VMEM((2, 2, 3 * hs, tokens), bf16),
        pltpu.VMEM((2, 2, 3 * ls, tokens), bf16),
        pltpu.VMEM((2 * heads, tokens, tokens), bf16),
        pltpu.VMEM((2, 2, hs, tokens), bf16),
        pltpu.VMEM((2, 2, ls, tokens), bf16),
        pltpu.VMEM((2, width, tokens), bf16),
        pltpu.VMEM((2, width, tokens), bf16),
        pltpu.VMEM((2, width, tokens), bf16),
        pltpu.VMEM((2, 2, ft + fl, tokens), bf16),
        pltpu.VMEM((2, 2, ft + fl, tokens), bf16),
        pltpu.VMEM((2, 8, tokens), f32),
        pltpu.VMEM((width, tokens), f32),
        pltpu.VMEM((width, tokens), bf16),
        pltpu.VMEM((2, width, tokens), bf16),
        pltpu.VMEM((width, tokens), bf16),
        pltpu.VMEM((width, tokens), bf16),
        pltpu.VMEM((2, ft + fl, tokens), bf16),
        pltpu.VMEM((2, 3 * hs + 3 * ls, tokens), bf16),
        pltpu.VMEM((3, SMALL, 16), f32),
        pltpu.VMEM((2, tw, tw), bf16),
        pltpu.VMEM((2, lw, lw), bf16),
        pltpu.VMEM((2, tw // 2, tw), bf16),
        pltpu.VMEM((2, lw // 2, lw), bf16),
        pltpu.VMEM((2, tw // 4, tw), bf16),
        pltpu.VMEM((2, lw // 4, lw), bf16),
        pltpu.VMEM((3, tw, tw), bf16),
        pltpu.VMEM((3, lw, lw), bf16),
        pltpu.VMEM((2, 2, 16, SMALL), f32),
        pltpu.VMEM((4, 16, SMALL), f32),
        pltpu.VMEM((16, SMALL), f32),
        pltpu.VMEM((3, 16, SMALL), f32),
        dma((2, 2, 18)), dma((18, 2)), dma((18, 2)), dma((3,)), dma((4, 5)), dma((1,)), dma((2,)),
        dma((4, 3)), dma((2, 2)), dma((2,)),
        dma((2, 3, 2)), dma((2, 3, 2)), dma((2, 3, 2, 2)), dma((2, 3, 2, 2)), dma((2, 3, 2)), dma((2, 3, 2)),
        dma((3, 2, 3, 2)), dma((3, 2)), dma((3, 2)), dma((3, 3, 2)), dma((3, 2, 2)), dma((3, 2)),
        dma((2, 3)), dma((2, 3)), dma((2, 4)),
        dma((2, 2)), dma((4,)), dma((3,)), dma((3,)), dma((1,)),
    ]
    results = pl.pallas_call(
        functools.partial(kernel, dp, z_inside),
        out_shape=out_shape,
        in_specs=[hbm] * 12 + [vmem] * 6 + [pl.BlockSpec(memory_space=pltpu.SMEM)],
        out_specs=[hbm] * len(out_shape),
        scratch_shapes=scratch,
        compiler_params=pltpu.CompilerParams(
            collective_id=0, has_side_effects=True, vmem_limit_bytes=63 * 1024 * 1024
        ),
    )(
        text_in, layout_in.transpose(0, 2, 1), text_cot, layout_cot.transpose(0, 2, 1),
        attend_rows(text_attend), text_output[0].T, text_expand[0], text_shrink[0],
        attend_rows(layout_attend), layout_output[0].T, layout_expand[0], layout_shrink[0],
        text_biases[0], layout_biases[0], text_offset, layout_offset, text_vectors[0], layout_vectors[0], lengths,
    )
    row_results, sums = results[:4], results[4]
    if z_inside:
        parts_t, parts_l = results[7], results[8]
    else:
        parts_t = lax.psum_scatter(results[5], "dp", scatter_dimension=1, tiled=True)[:, None]
        parts_l = lax.psum_scatter(results[6], "dp", scatter_dimension=1, tiled=True)[:, None]
        sums = lax.psum(sums, "dp")
    final_shapes = row_shapes + [
        shape((3, zt, hs), f32), shape((zt, hs), f32), shape((zt, ft), f32), shape((zt, ft), f32),
        shape((3, zl, ls), f32), shape((zl, ls), f32), shape((zl, fl), f32), shape((zl, fl), f32),
        shape((2, hs), f32), shape((1, ft), f32), shape((6, 1, tw), f32),
        shape((2, ls), f32), shape((1, fl), f32), shape((6, 1, lw), f32),
    ]
    (
        text_out, lay_out, text_back, lay_back, att_t, out_t, exp_t, shr_t, att_l, out_l, exp_l, shr_l,
        bias_t, off_t, vec_t, bias_l, off_l, vec_l,
    ) = pl.pallas_call(
        finishing,
        out_shape=final_shapes,
        in_specs=[hbm] * 7,
        out_specs=[hbm] * 4 + [vmem] * 14,
        scratch_shapes=[
            pltpu.VMEM(parts_t.shape, bf16), pltpu.VMEM(parts_l.shape, bf16), pltpu.VMEM((16, SMALL), f32),
            *(pltpu.VMEM(rows.shape, bf16) for rows in row_shapes), dma((11,)),
        ],
        compiler_params=pltpu.CompilerParams(vmem_limit_bytes=62 * 1024 * 1024),
    )(parts_t, parts_l, sums, *row_results)
    return (
        text_out[None],
        lay_out.transpose(0, 2, 1)[None],
        text_back[None],
        lay_back.transpose(0, 2, 1)[None],
        att_t.transpose(1, 0, 2)[None],
        bias_t[None],
        out_t[None],
        exp_t[None],
        off_t,
        shr_t[None],
        vec_t.transpose(1, 0, 2),
        att_l.transpose(1, 0, 2)[None],
        bias_l[None],
        out_l[None],
        exp_l[None],
        off_l,
        shr_l[None],
        vec_l.transpose(1, 0, 2),
    )


def solution(mesh):
    return jax.shard_map(
        functools.partial(local, mesh.shape["dp"]),
        mesh=mesh,
        in_specs=(
            P(None, ("dp", "tensor"), None),
            P(None, ("dp", "tensor"), None),
            P(None, ("dp", "tensor"), None),
            P(None, ("dp", "tensor"), None),
            P(None, "dp"),
            P("section", None, None, "tensor"),
            P("section", None, "tensor"),
            P("section", None, "tensor"),
            P("section", None, "tensor"),
            P("section", "tensor"),
            P("section", None, "tensor"),
            P("section", None, None),
            P("section", None, None, "tensor"),
            P("section", None, "tensor"),
            P("section", None, "tensor"),
            P("section", None, "tensor"),
            P("section", "tensor"),
            P("section", None, "tensor"),
            P("section", None, None),
        ),
        out_specs=(
            P("section", None, ("dp", "tensor"), None),
            P("section", None, ("dp", "tensor"), None),
            P("section", None, ("dp", "tensor"), None),
            P("section", None, ("dp", "tensor"), None),
            P("section", "dp", None, "tensor"),
            P("section", None, "tensor"),
            P("section", "dp", "tensor"),
            P("section", "dp", "tensor"),
            P("section", "tensor"),
            P("section", "dp", "tensor"),
            P("section", None, None),
            P("section", "dp", None, "tensor"),
            P("section", None, "tensor"),
            P("section", "dp", "tensor"),
            P("section", "dp", "tensor"),
            P("section", "tensor"),
            P("section", "dp", "tensor"),
            P("section", None, None),
        ),
        check_vma=False,
    )
```
